32 devices in a mesh: dp: 4 (over z), mp: 8 (over y, x, core).
Axes of the slice: x: 2, y: 2, z: 4, core: 2. Of those that a mesh axis runs over, the one named last changes fastest.
Arguments:
- src_ids: int32 [32, 768], P('dp'), may hold values from 0 to 32127
- targets: int32 [32, 256], P('dp'), may hold values from 0 to 32127
- loss_pos: int32 [32, 128], P('dp'), may hold values from 0 to 255, as said below
- loss_mask: int32 [32, 128], P('dp'), may hold values from 0 to 1
- routes_src: int32 [32, 768], replicated, may hold values from 0 to 3, as said below
- routes_tgt: int32 [32, 256], replicated, may hold values from 0 to 3, as said below
- dense_w: float32 [12, 589824], P(None, 'mp'), may hold values from -1.1547005 to 1.1547005
- dense_m: float32 [12, 589824], P(None, 'mp'), may hold values from -0.0017089844 to 0.0017089844
- expert_w: float32 [2, 2, 4, 768, 3072], P(None, None, 'dp', None, 'mp'), may hold values from -0.6350853 to 0.6350853
- expert_m: float32 [2, 2, 4, 768, 3072], P(None, None, 'dp', None, 'mp'), may hold values from -0.0017089844 to 0.0017089844
- table_w: float32 [32128, 768], P('mp'), may hold values from -12 to 12
- table_m: float32 [32128, 768], P(('mp', 'dp')), may hold values from -0.00018310547 to 0.00018310547
- table_v: float32 [32128, 768], P(('mp', 'dp')), may hold values from 7.1941486e-10 to 2.8776594e-09
- gains_w: float32 [7, 768], replicated, may hold values from 0.25 to 2.25
- gains_m: float32 [7, 768], P(None, 'mp'), may hold values from -0.0009765625 to 0.0009765625
- gains_v: float32 [7, 768], P(None, 'mp'), may hold values from 1.7985371e-08 to 7.1941486e-08
- router_w: float32 [2, 768, 4], replicated, may hold values from -0.375 to 0.375
- router_m: float32 [2, 768, 4], P(None, 'mp'), may hold values from -0.0009765625 to 0.0009765625
- router_v: float32 [2, 768, 4], P(None, 'mp'), may hold values from 1.7985371e-08 to 7.1941486e-08
- bias_w: float32 [2, 32, 12], replicated, may hold values from -4 to 4
- bias_m: float32 [2, 32, 12], P(None, 'mp'), may hold values from -0.0009765625 to 0.0009765625
- bias_v: float32 [2, 32, 12], P(None, 'mp'), may hold values from 1.7985371e-08 to 7.1941486e-08
Outputs:
- loss: float32 [2], replicated
- grad_norm: float32 [], replicated
- dense_new: float32 [12, 589824], P(None, 'mp')
- dense_moment: float32 [12, 589824], P(None, 'mp')
- dense_low: bfloat16 [12, 589824], P(None, 'mp')
- expert_new: float32 [2, 2, 4, 768, 3072], P(None, None, 'dp', None, 'mp')
- expert_moment: float32 [2, 2, 4, 768, 3072], P(None, None, 'dp', None, 'mp')
- expert_low: bfloat16 [2, 2, 4, 768, 3072], P(None, None, 'dp', None, 'mp')
- table_new: float32 [32128, 768], P(('mp', 'dp'))
- table_clipped: float32 [32128, 768], P(('mp', 'dp'))
- table_second: float32 [32128, 768], P(('mp', 'dp'))
- gains_new: float32 [7, 768], P(None, 'mp')
- gains_first: float32 [7, 768], P(None, 'mp')
- gains_second: float32 [7, 768], P(None, 'mp')
- router_new: float32 [2, 768, 4], P(None, 'mp')
- router_first: float32 [2, 768, 4], P(None, 'mp')
- router_second: float32 [2, 768, 4], P(None, 'mp')
- bias_new: float32 [2, 32, 12], P(None, 'mp')
- bias_first: float32 [2, 32, 12], P(None, 'mp')
- bias_second: float32 [2, 32, 12], P(None, 'mp')
The draws below stay inside these ranges and needn't reach their ends.
Inputs may be any that keep to these rules, and one draw needn't show every extreme that they name: `routes_src`: in each device's block of 768 rows no expert is named by more than 240 rows, and some expert by exactly 240. `routes_tgt`: in each device's block of 256 rows no expert is named by more than 80 rows, and some expert by exactly 80. `loss_pos`: the 128 positions of a sequence are distinct.
All inputs are finite; a program needn't handle non-finite values.
Results may differ from the reference program's by a relative error of at most 0.025.
Values may be sent and summed in bfloat16 or wider, within the bound.
A program may use at most 512 MiB of HBM per device.

```python
import math
import jax
import jax.numpy as jnp
import numpy as np
from jax import lax

D = 768
HEADS = 12
HD = 64
FF = 3072
VOCAB = 32128
BUCKETS = 32
SRC = 768
TGT = 256
NPOS = 128
SEQ_DEV = 1
NS_ITERS = 5
STEP = 10
EXPERTS = 4
SEQS = 32
CAP_ENC = 240
CAP_DEC = 80
PARAMS = 69500928
N_DP = 4
N_MP = 8
DEVICES = 32


def route_blocks(key, length, capacity):
    rows = SEQ_DEV * length
    nblock = SEQS // SEQ_DEV
    owner = (jnp.arange(EXPERTS * capacity, dtype=jnp.int32) // capacity).astype(jnp.int32)

    def one(block_key):
        first, second, third = jax.random.split(block_key, 3)
        full = jax.random.randint(first, (), 0, EXPERTS)
        mixed = jax.random.permutation(second, owner)
        ranked = mixed[jnp.argsort((mixed != full).astype(jnp.int32), stable=True)]
        return jax.random.permutation(third, ranked[:rows])
    return jax.vmap(one)(jax.random.split(key, nblock)).reshape(SEQS, length).astype(jnp.int32)


def draw_routes_src(key, part):
    key = jax.random.fold_in(key, 17)
    return route_blocks(key, SRC, CAP_ENC)


def draw_routes_tgt(key, part):
    key = jax.random.fold_in(key, 18)
    return route_blocks(key, TGT, CAP_DEC)


def draw_loss_pos(key, part):
    key = jax.random.fold_in(key, 11)
    scores = jax.random.randint(key, (SEQS, TGT), 0, 1 << 20) * TGT + jnp.arange(TGT, dtype=jnp.int32)[None, :]
    order = jnp.argsort(scores, axis=1, stable=True)
    return order[:, :NPOS].astype(jnp.int32)


def draw_loss_mask(key, part):
    key = jax.random.fold_in(key, 12)
    sequence = jnp.arange(SEQS, dtype=jnp.int32)
    row_part = sequence // (N_MP * SEQ_DEV)
    column_part = sequence // SEQ_DEV % N_MP
    level = 200 + 350 * row_part // max(N_DP - 1, 1) + 350 * column_part // max(N_MP - 1, 1)
    draws = jax.random.randint(key, (SEQS, NPOS), 0, 1000)
    return (draws < level[:, None]).astype(jnp.int32)


def draw_table_w(key, part):
    key = jax.random.fold_in(key, 13)
    rows = jnp.arange(VOCAB, dtype=jnp.float32)[:, None] / (VOCAB - 1)
    return (1.0 + 2.0 * rows) * jax.random.truncated_normal(key, -4.0, 4.0, (VOCAB, D), jnp.float32)


def draw_dense_w(key, part):
    key = jax.random.fold_in(key, 14)
    scale = jnp.where(jnp.arange(12) % 4 == 3, 8.0, 1.0).astype(jnp.float32)[:, None] * D ** (-0.5)
    return scale * jax.random.truncated_normal(key, -4.0, 4.0, (12, D * D), jnp.float32)


def draw_expert_w(key, part):
    key = jax.random.fold_in(key, 15)
    scale = jnp.array([D ** (-0.5), 1.7 * EXPERTS * FF ** (-0.5)], jnp.float32)[None, :, None, None, None]
    shape = (2, 2, EXPERTS, D, FF)
    return scale * jax.random.truncated_normal(key, -4.0, 4.0, shape, jnp.float32)


def draw_gains_w(key, part):
    key = jax.random.fold_in(key, 16)
    slope = 0.5 + jnp.arange(D, dtype=jnp.float32) / (D - 1)
    noise = 1.0 + 0.1 * jax.random.truncated_normal(key, -4.0, 4.0, (7, D), jnp.float32)
    return slope[None, :] * noise


def place_ends(drawn, stream_key, low, largest):
    longest = drawn.shape.index(max(drawn.shape))
    spots = []
    for shift in (0, 1):
        where = [jax.random.randint(jax.random.fold_in(stream_key, axis), (), 0, length) for axis, length in enumerate(drawn.shape)]
        where[longest] = (where[longest] + shift) % drawn.shape[longest]
        spots.append(tuple(where))
    return drawn.at[spots[0]].set(low).at[spots[1]].set(largest)


def block_levels(stream_key, dims, pieces, smallest, top_value):
    factor_of = 1.0
    for position, blocks in pieces:
        steps = jax.random.uniform(jax.random.fold_in(jax.random.fold_in(stream_key, 6), position), (blocks,), jnp.float32, smallest / len(pieces), top_value / len(pieces))
        factor_of = factor_of * jnp.repeat(jnp.exp(steps), dims[position] // blocks).reshape((-1,) + (1,) * (len(dims) - 1 - position))
    return factor_of


def rank_bounds(number_of, lean):
    weights = [(1 << 20) // math.isqrt(grade ** lean) + 1 for grade in range(1, number_of + 1)]
    deviation = 1 + sum(weights) // (1 << 30)
    return np.cumsum(np.array([max(1, weight // deviation) for weight in weights]))


def ranked_ids(rng, shape, number_of, lean):
    table = rank_bounds(number_of, lean)
    ticket = jax.random.randint(jax.random.fold_in(rng, 1), shape, 0, int(table[number_of - 1]))
    rank = jnp.searchsorted(jnp.asarray(table, jnp.int32), ticket, side="right")
    return jax.random.permutation(jax.random.fold_in(rng, 2), number_of)[rank].astype(jnp.int32)


def normal_values(key, extent, deviation, reach, cuts=(), held_as=jnp.bfloat16):
    level = block_levels(key, extent, cuts, -0.22, 0.18) if cuts else 1.0
    values = jax.random.normal(key, extent, jnp.float32) * deviation * level
    return jnp.minimum(jnp.maximum(values, -reach), reach).astype(held_as)


def setup_inputs(seed: int = 0) -> dict:
    key_list = jax.random.split(jax.random.key(seed), 23)
    src_ids = place_ends(ranked_ids(key_list[0], (SEQS, SRC), VOCAB, 2), jax.random.fold_in(key_list[0], 3), 0, VOCAB - 1).astype(jnp.int32)
    targets = place_ends(ranked_ids(key_list[1], (SEQS, TGT), VOCAB, 2), jax.random.fold_in(key_list[1], 3), 0, VOCAB - 1).astype(jnp.int32)
    loss_pos = draw_loss_pos(jax.random.fold_in(key_list[22], 71), 0)
    loss_mask = draw_loss_mask(jax.random.fold_in(key_list[22], 71), 0)
    routes_src = draw_routes_src(jax.random.fold_in(key_list[22], 71), 0)
    routes_tgt = draw_routes_tgt(jax.random.fold_in(key_list[22], 71), 0)
    dense_w = draw_dense_w(jax.random.fold_in(key_list[22], 71), 0)
    dense_m = normal_values(key_list[7], (12, D * D), (PARAMS ** -0.5), 0.0017089844, ((1, 8),), jnp.float32)
    expert_w = draw_expert_w(jax.random.fold_in(key_list[22], 71), 0)
    expert_m = normal_values(key_list[9], (2, 2, EXPERTS, D, FF), (PARAMS ** -0.5), 0.0017089844, ((2, 4), (4, 8)), jnp.float32)
    table_w = draw_table_w(jax.random.fold_in(key_list[22], 71), 0)
    table_m = normal_values(key_list[11], (VOCAB, D), (0.11 * PARAMS ** -0.5), 0.00018310547, ((0, 32),), jnp.float32)
    table_v = jnp.clip(jnp.exp(math.log(2.877659444067149e-09) - 1.3862944 * jax.random.uniform(key_list[12], (VOCAB, D), jnp.float32) ** block_levels(key_list[12], (VOCAB, D), ((0, 32),), -0.2, 0.2)), 7.194148610167872e-10, 2.877659444067149e-09)
    gains_w = draw_gains_w(jax.random.fold_in(key_list[22], 71), 0)
    gains_m = normal_values(key_list[14], (7, D), (0.55 * PARAMS ** -0.5), 0.0009765625, ((1, 8),), jnp.float32)
    gains_v = jnp.clip(jnp.exp(math.log(7.194148565758951e-08) - 1.3862944 * jax.random.uniform(key_list[15], (7, D), jnp.float32) ** block_levels(key_list[15], (7, D), ((1, 8),), -0.2, 0.2)), 1.7985371414397378e-08, 7.194148565758951e-08)
    router_w = normal_values(key_list[16], (2, D, EXPERTS), (0.7 * D ** -0.5), 0.375, (), jnp.float32)
    router_m = normal_values(key_list[17], (2, D, EXPERTS), (0.55 * PARAMS ** -0.5), 0.0009765625, ((1, 8),), jnp.float32)
    router_v = jnp.clip(jnp.exp(math.log(7.194148565758951e-08) - 1.3862944 * jax.random.uniform(key_list[18], (2, D, EXPERTS), jnp.float32) ** block_levels(key_list[18], (2, D, EXPERTS), ((1, 8),), -0.2, 0.2)), 1.7985371414397378e-08, 7.194148565758951e-08)
    bias_w = normal_values(key_list[19], (2, BUCKETS, HEADS), 0.8, 4.0, (), jnp.float32)
    bias_m = normal_values(key_list[20], (2, BUCKETS, HEADS), (0.55 * PARAMS ** -0.5), 0.0009765625, ((1, 8),), jnp.float32)
    bias_v = jnp.clip(jnp.exp(math.log(7.194148565758951e-08) - 1.3862944 * jax.random.uniform(key_list[21], (2, BUCKETS, HEADS), jnp.float32) ** block_levels(key_list[21], (2, BUCKETS, HEADS), ((1, 8),), -0.2, 0.2)), 1.7985371414397378e-08, 7.194148565758951e-08)
    return {"src_ids": src_ids, "targets": targets, "loss_pos": loss_pos, "loss_mask": loss_mask, "routes_src": routes_src, "routes_tgt": routes_tgt, "dense_w": dense_w, "dense_m": dense_m, "expert_w": expert_w, "expert_m": expert_m, "table_w": table_w, "table_m": table_m, "table_v": table_v, "gains_w": gains_w, "gains_m": gains_m, "gains_v": gains_v, "router_w": router_w, "router_m": router_m, "router_v": router_v, "bias_w": bias_w, "bias_m": bias_m, "bias_v": bias_v}


@jax.custom_vjp
def low(v):
    return lax.optimization_barrier(v.astype(jnp.bfloat16)).astype(jnp.float32)

@jax.custom_vjp
def low_back(v):
    return v

def low_keep(v):
    return (low(v), None)

def low_pass(kept, grad):
    return (grad,)

def back_keep(v):
    return (v, None)

def back_low(kept, grad):
    return (low(grad),)
low.defvjp(low_keep, low_pass)
low_back.defvjp(back_keep, back_low)
highest = lax.Precision.HIGHEST
eps_norm = 1e-06
eps_gram = 1e-07
eps_adam = 1e-08
neg_fill = -1000000000.0
coef_a = 3.4445
coef_b = -4.775
coef_c = 2.0315
beta_one = 0.9
beta_two = 0.95
rate_matrix = 0.2
decay_matrix = 0.01
aux_weight = 0.01
enc_edges = (12, 16, 23, 32, 46, 64, 91)
dec_edges = (19, 21, 24, 27, 31, 35, 40, 46, 52, 59, 67, 77, 87, 99, 113)

def matmul(left, right):
    return jnp.dot(left, right, precision=highest, preferred_element_type=jnp.float32)

def normalize(rows, gain):
    return rows * lax.rsqrt(lax.optimization_barrier(jnp.mean(rows * rows, axis=-1, keepdims=True)) + eps_norm) * gain

def bucket_table(len_q, len_k, causal):
    relative = lax.broadcasted_iota(jnp.int32, (len_q, len_k), 1) - lax.broadcasted_iota(jnp.int32, (len_q, len_k), 0)
    if causal:
        distance = jnp.maximum(-relative, 0)
        far = 16 + sum(((distance >= edge).astype(jnp.int32) for edge in dec_edges))
        return jnp.where(distance < 16, distance, far).astype(jnp.int32)
    distance = jnp.abs(relative)
    far = 8 + sum(((distance >= edge).astype(jnp.int32) for edge in enc_edges))
    return (jnp.where(distance < 8, distance, far) + 16 * (relative > 0).astype(jnp.int32)).astype(jnp.int32)

def project(rows, weight):
    return low_back(low(matmul(rows, weight)))

def attention(resid, normed, context, weights, table, causal, nseq):
    queries = project(normed, weights[0]).reshape(nseq, -1, HEADS, HD)
    keys = project(context, weights[1]).reshape(nseq, -1, HEADS, HD)
    values = project(context, weights[2]).reshape(nseq, -1, HEADS, HD)
    len_q, len_k = (queries.shape[1], keys.shape[1])
    if table is None:
        bias = jnp.zeros((HEADS, len_q, len_k), jnp.float32)
    else:
        bias = jnp.transpose(table[bucket_table(len_q, len_k, causal)], (2, 0, 1))
    allowed = lax.broadcasted_iota(jnp.int32, (len_q, len_k), 1) <= lax.broadcasted_iota(jnp.int32, (len_q, len_k), 0)

    def block(parts):
        scores = jnp.einsum('sqhd,skhd->shqk', parts[0], parts[1], precision=highest) * HD ** (-0.5) + bias
        scores = low_back(scores)
        if causal:
            scores = jnp.where(allowed, scores, neg_fill)
        probs = jax.nn.softmax(scores, axis=-1)
        return jnp.einsum('shqk,skhd->sqhd', low(probs), parts[2], precision=highest)
    group = 4
    mixed = lax.map(jax.checkpoint(block), (queries.reshape(nseq // group, group, len_q, HEADS, HD), keys.reshape(nseq // group, group, len_k, HEADS, HD), values.reshape(nseq // group, group, len_k, HEADS, HD)))
    mixed = low_back(low(mixed.reshape(-1, D)))
    return resid + low_back(matmul(mixed, weights[3]))

def experts_layer(resid, gain, router, w_in, w_out, routes, cap, nblock):
    normed = low(normalize(resid, gain))
    probs = jax.nn.softmax(matmul(normed, router), axis=-1)
    count = routes.shape[0]
    experts = router.shape[1]
    hot = (routes[:, None] == jnp.arange(experts).astype(jnp.int32)[None, :]).astype(jnp.int32)
    ranks = jnp.cumsum(hot.reshape(nblock, -1, experts), axis=1).reshape(count, experts)
    slots = (lax.optimization_barrier(jnp.sum(hot * ranks, axis=1)) - 1).astype(jnp.int32)
    blocks = (jnp.arange(count).astype(jnp.int32) // (count // nblock)).astype(jnp.int32)
    buffer = jnp.zeros((experts, nblock, cap, D), jnp.float32).at[routes, blocks, slots].set(low_back(normed))

    def expert(parts):
        hidden = low(jax.nn.gelu(low_back(matmul(parts[0], parts[1])), approximate=True))
        return low_back(low(matmul(hidden, parts[2].T)))
    outputs = lax.map(jax.checkpoint(expert), (buffer.reshape(experts, nblock * cap, D), w_in, w_out))
    outputs = outputs.reshape(experts, nblock, cap, D)[routes, blocks, slots]
    gate = lax.optimization_barrier(jnp.sum(probs * hot.astype(jnp.float32), axis=1))
    frac = lax.optimization_barrier(jnp.sum(hot, axis=0)).astype(jnp.float32) / count
    aux = aux_weight * experts * jnp.sum(frac * lax.optimization_barrier(jnp.mean(probs, axis=0)))
    return (resid + gate[:, None] * outputs, aux)

def forward(params, src_ids, targets, loss_pos, loss_mask, routes_src, routes_tgt):
    dense = low(params['dense'])
    expert = low(params['expert'])
    table = low(params['table'])
    gains = params['gains']
    router = params['router']
    bias = params['bias']
    nseq = src_ids.shape[0]
    dec_ids = jnp.concatenate([jnp.zeros((nseq, 1), jnp.int32), targets[:, :-1]], axis=1)
    enc = low_back(table[src_ids.reshape(-1)])
    dec = low_back(table[dec_ids.reshape(-1)])
    normed = low(normalize(enc, gains[0]))
    enc = attention(enc, normed, normed, dense[0:4], bias[0], False, nseq)
    enc, aux_src = experts_layer(enc, gains[1], router[0], expert[0, 0], expert[0, 1], routes_src.reshape(-1), CAP_ENC, DEVICES)
    memory = low(normalize(enc, gains[2]))
    normed = low(normalize(dec, gains[3]))
    dec = attention(dec, normed, normed, dense[4:8], bias[1], True, nseq)
    normed = low(normalize(dec, gains[4]))
    dec = attention(dec, normed, memory, dense[8:12], None, False, nseq)
    dec, aux_tgt = experts_layer(dec, gains[5], router[1], expert[1, 0], expert[1, 1], routes_tgt.reshape(-1), CAP_DEC, DEVICES)
    final = low(normalize(dec, gains[6]))
    chosen = final[(jnp.arange(nseq).astype(jnp.int32)[:, None] * TGT + loss_pos).reshape(-1)]
    wanted = jnp.take_along_axis(targets, loss_pos, axis=1).reshape(-1)
    weights = loss_mask.reshape(-1).astype(jnp.float32)

    def head(parts):
        logits = low_back(matmul(parts[0], table.T) * D ** (-0.5))
        logsum = jax.nn.logsumexp(logits, axis=-1)
        picked = jnp.take_along_axis(logits, parts[1][:, None], axis=1)[:, 0]
        return jnp.sum(parts[2] * (logsum - picked))
    span = 4 * NPOS
    losses = lax.map(jax.checkpoint(head), (chosen.reshape(-1, span, D), wanted.reshape(-1, span), weights.reshape(-1, span)))
    return jnp.sum(losses) + aux_src + aux_tgt

def gram(matrix):
    blocks = matrix.reshape(matrix.shape[0], N_MP, -1)
    parts = jnp.einsum('dnc,enc->nde', blocks, blocks, precision=highest)
    return low(lax.optimization_barrier(jnp.sum(low(parts), axis=0)))

def orthogonalize(momentum):
    start = gram(low(momentum))
    scale = jnp.trace(start) + eps_gram
    current = low(momentum * lax.rsqrt(scale))
    product = low(start / scale)
    for turn in range(NS_ITERS):
        if turn:
            product = gram(current)
        once = low(matmul(product, current))
        twice = matmul(product, once)
        current = low(coef_a * current + coef_b * once + coef_c * twice)
    return current

def muon(weight, momentum, grad, columns):
    moment = 0.5 * momentum + grad
    ortho = lax.map(orthogonalize, moment.reshape(-1, D, columns)).reshape(moment.shape)
    new_weight = weight * (1 - rate_matrix * decay_matrix) - rate_matrix * 0.2 * math.sqrt(max(D, columns)) * ortho
    return (new_weight, moment, new_weight.astype(jnp.bfloat16))

def adam(weight, first, second, grad, rate, decay):
    first = beta_one * first + (1 - beta_one) * grad
    second = beta_two * second + (1 - beta_two) * grad * grad
    update = first / (1 - beta_one ** STEP) / (jnp.sqrt(second / (1 - beta_two ** STEP)) + eps_adam)
    return (weight - rate * (update + decay * weight), first, second)

def unflat(stored):
    return jnp.transpose(stored.reshape(12, D, D), (0, 2, 1))

def flat(matrices):
    return jnp.transpose(matrices, (0, 2, 1)).reshape(12, D * D)

def reference(src_ids, targets, loss_pos, loss_mask, routes_src, routes_tgt, dense_w, dense_m, expert_w, expert_m, table_w, table_m, table_v, gains_w, gains_m, gains_v, router_w, router_m, router_v, bias_w, bias_m, bias_v):
    params = {'dense': unflat(dense_w.astype(jnp.float32)), 'expert': expert_w.astype(jnp.float32), 'table': table_w.astype(jnp.float32), 'gains': gains_w.astype(jnp.float32), 'router': router_w.astype(jnp.float32), 'bias': bias_w.astype(jnp.float32)}

    def objective(values):
        return forward(values, src_ids, targets, loss_pos, loss_mask, routes_src, routes_tgt)
    value, pullback = jax.vjp(objective, params)
    grads = pullback(jnp.ones_like(value))[0]
    squares = sum((jnp.sum(part * part) for part in jax.tree.leaves(grads)))
    grad_norm = jnp.sqrt(squares)
    clip = 1.0 / jnp.maximum(grad_norm, 1.0)
    dense_new, dense_moment, dense_low = muon(params['dense'], unflat(dense_m), clip * grads['dense'], D)
    expert_new, expert_moment, expert_low = muon(params['expert'], expert_m, clip * grads['expert'], FF)
    table_clipped = clip * grads['table']
    table_new, table_first, table_second = adam(params['table'], table_m, table_v, table_clipped, 1.5, 0.01)
    gains_new, gains_first, gains_second = adam(params['gains'], gains_m, gains_v, clip * grads['gains'], 0.5, 0.0)
    router_new, router_first, router_second = adam(params['router'], router_m, router_v, clip * grads['router'], 0.02, 0.01)
    bias_new, bias_first, bias_second = adam(params['bias'], bias_m, bias_v, clip * grads['bias'], 0.5, 0.0)
    loss = jnp.stack([value, jnp.sum(loss_mask).astype(jnp.float32)])
    return (loss, grad_norm, flat(dense_new), flat(dense_moment), flat(dense_low), expert_new, expert_moment, expert_low, table_new, table_clipped, table_second, gains_new, gains_first, gains_second, router_new, router_first, router_second, bias_new, bias_first, bias_second)
```

```python
from functools import partial
import math

import jax
import jax.numpy as jnp
from jax import lax
from jax.experimental import pallas as pl
from jax.experimental.pallas import tpu as pltpu
from jax.sharding import PartitionSpec as P

D = 768
HEADS = 12
HD = 64
FF = 3072
NS_ITERS = 5
STEP = 10


eps_norm = 1e-06
eps_gram = 1e-07
eps_adam = 1e-08
neg_fill = -1000000000.0
coef_a = 3.4445
coef_b = -4.775
coef_c = 2.0315
beta_one = 0.9
beta_two = 0.95
rate_matrix = 0.2
decay_matrix = 0.01
aux_weight = 0.01
enc_edges = (12, 16, 23, 32, 46, 64, 91)
dec_edges = (19, 21, 24, 27, 31, 35, 40, 46, 52, 59, 67, 77, 87, 99, 113)
highest = lax.Precision.HIGHEST


def normalize(rows, gain):
    inverse = lax.rsqrt(jnp.mean(rows * rows, axis=-1, keepdims=True) + eps_norm)
    return (rows * inverse * gain, inverse)


def normalize_back(rows, inverse, gain, grad):
    scaled = grad * gain
    d_rows = inverse * scaled - rows * inverse**3 * jnp.mean(scaled * rows, axis=-1, keepdims=True)
    return (d_rows, jnp.sum(grad * rows * inverse, axis=0))


def bucket_of(relative, causal):
    if causal:
        distance = jnp.maximum(-relative, 0)
        far = 16 + sum(((distance >= edge).astype(jnp.int32) for edge in dec_edges))
        return jnp.where(distance < 16, distance, far)
    distance = jnp.abs(relative)
    far = 8 + sum(((distance >= edge).astype(jnp.int32) for edge in enc_edges))
    return jnp.where(distance < 8, distance, far) + 16 * (relative > 0).astype(jnp.int32)


LANES = 128
CHUNK = 256
VMEM_LIMIT = 60 * 1024 * 1024


def params(count=1, **more):
    return pltpu.CompilerParams(
        dimension_semantics=("arbitrary",) * count, vmem_limit_bytes=VMEM_LIMIT, **more
    )


def dot_nn(left, right):
    return lax.dot_general(
        left, right, (((1,), (0,)), ((), ())), preferred_element_type=jnp.float32
    )


def dot_nt(left, right):
    return lax.dot_general(
        left, right, (((1,), (1,)), ((), ())), preferred_element_type=jnp.float32
    )


def dot_tn(left, right):
    return lax.dot_general(
        left, right, (((0,), (0,)), ((), ())), preferred_element_type=jnp.float32
    )


def own_lanes(rows, half):
    lane = lax.broadcasted_iota(jnp.int32, rows.shape, 1)
    keep = lane >= HD if half else lane < HD
    return jnp.where(keep, rows, jnp.zeros_like(rows))


def band_offsets():
    place = jnp.arange(4 * LANES, dtype=jnp.int32)
    return LANES - jnp.where(place < 3 * LANES, place, place - 4 * LANES)


def bias_parts(table, causal):
    count = table.shape[0]
    hot = (
        bucket_of(band_offsets(), causal)[:, None] == jnp.arange(count, dtype=jnp.int32)[None, :]
    ).astype(jnp.float32)
    band = jnp.dot(hot, table, precision=highest).T[:, None, :]
    ends = bucket_of(jnp.array([-2 * LANES, 2 * LANES], jnp.int32), causal)
    hot_ends = (ends[:, None] == jnp.arange(count, dtype=jnp.int32)[None, :]).astype(jnp.float32)
    far = jnp.dot(hot_ends, table, precision=highest)
    return band, far, hot, hot_ends


def bias_sums(sums, hot, hot_ends):
    per_place = sums[:, 0, :]
    near = per_place[:, : 4 * LANES]
    far = jnp.sum(per_place[:, 4 * LANES :].reshape(-1, 2, LANES), axis=2)
    return jnp.dot(hot.T, near.T, precision=highest) + jnp.dot(
        hot_ends.T, far.T, precision=highest
    )


def scores_of(keys, queries, head, chunk, far_ref, band, causal):
    scores = dot_nt(keys, queries) * HD ** (-0.5)
    len_k, width = scores.shape
    if band is not None:
        rows = []
        for a in range(len_k // LANES):
            columns = []
            for b in range(width // LANES):
                apart = a - (chunk * (width // LANES) + b)
                if apart < -1:
                    bias = far_ref[0, head]
                elif apart > 1:
                    bias = far_ref[1, head]
                else:
                    bias = band[:, LANES * (1 - apart) : LANES * (2 - apart)]
                columns.append(
                    scores[LANES * a : LANES * a + LANES, LANES * b : LANES * b + LANES] + bias
                )
            rows.append(jnp.concatenate(columns, axis=1))
        scores = jnp.concatenate(rows, axis=0)
    if causal:
        allowed = lax.broadcasted_iota(jnp.int32, scores.shape, 0) <= (
            lax.broadcasted_iota(jnp.int32, scores.shape, 1) + chunk * width
        )
        scores = jnp.where(allowed, scores, neg_fill)
    return scores


def band_of(band_ref, half):
    row = jnp.broadcast_to(band_ref[half], (LANES, 4 * LANES))
    return pltpu.roll(row, 0, 1, stride=1, stride_axis=0)


def unband(sums):
    row = lax.broadcasted_iota(jnp.int32, sums.shape, 0)
    step = 1
    while step < LANES:
        sums = jnp.where(
            (row & step) != 0, pltpu.roll(sums, sums.shape[1] - step, 1), sums
        )
        step *= 2
    return jnp.sum(sums, axis=0, keepdims=True)


def attend_kernel(biased, causal, *refs):
    if biased:
        far_ref, band_ref, *refs = refs
    q_ref, k_ref, v_ref, out_ref, lse_ref = refs
    pair = pl.program_id(0)
    keys = k_ref[...]
    values_t = v_ref[...].T
    len_q = q_ref.shape[0]
    width = min(CHUNK, len_q)
    bands = [band_of(band_ref, half) if biased else None for half in range(2)]
    for chunk in range(len_q // width):
        span = pl.ds(chunk * width, width)
        queries = q_ref[span, :]
        parts = []
        for half in range(2):
            scores = scores_of(
                keys,
                own_lanes(queries, half),
                2 * pair + half,
                chunk,
                far_ref if biased else None,
                bands[half],
                causal,
            )
            top = jnp.max(scores, axis=0, keepdims=True)
            expo = jnp.exp(scores - top)
            total = jnp.sum(expo, axis=0, keepdims=True)
            probs = (expo * (1.0 / total)).astype(jnp.bfloat16)
            parts.append(dot_nn(values_t[HD * half : HD * half + HD], probs))
            lse_ref[half, :, span] = top + jnp.log(total)
        out_ref[span, :] = jnp.concatenate(parts, axis=0).T.astype(jnp.bfloat16)


def attend_back_kernel(biased, causal, *refs):
    if biased:
        far_ref, band_ref, *refs = refs
    q_ref, k_ref, v_ref, g_ref, lse_ref, dq_ref, dk_ref, dv_ref, *refs = refs
    if biased:
        sums_ref, dk_acc, dv_acc, near_acc, far_acc = refs
    else:
        dk_acc, dv_acc = refs
    pair = pl.program_id(0)
    keys = k_ref[...]
    keys_t = keys.T
    values = v_ref[...]
    len_q, len_k = q_ref.shape[0], k_ref.shape[0]
    width = min(CHUNK, len_q)
    scale = HD ** (-0.5)
    dk_acc[...] = jnp.zeros_like(dk_acc)
    dv_acc[...] = jnp.zeros_like(dv_acc)
    bands = [band_of(band_ref, half) if biased else None for half in range(2)]
    if biased:
        near_acc[...] = jnp.zeros_like(near_acc)
        far_acc[...] = jnp.zeros_like(far_acc)
    for chunk in range(len_q // width):
        span = pl.ds(chunk * width, width)
        parts = []
        for half in range(2):
            queries = own_lanes(q_ref[span, :], half)
            grads = own_lanes(g_ref[span, :], half)
            scores = scores_of(
                keys,
                queries,
                2 * pair + half,
                chunk,
                far_ref if biased else None,
                bands[half],
                causal,
            )
            probs = jnp.exp(scores - lse_ref[half, :, span])
            d_probs = dot_nt(values, grads)
            delta = jnp.sum(probs * d_probs, axis=0, keepdims=True)
            d_scores = (probs * (d_probs - delta)).astype(jnp.bfloat16)
            dk_acc[...] += dot_nn(d_scores, queries)
            dv_acc[...] += dot_nn(probs.astype(jnp.bfloat16), grads)
            parts.append(dot_nn(keys_t[HD * half : HD * half + HD], d_scores))
            if biased:
                groups = {}
                for a in range(len_k // LANES):
                    for b in range(width // LANES):
                        apart = a - (chunk * (width // LANES) + b)
                        if causal and apart > 0:
                            continue
                        groups.setdefault(max(-2, min(2, apart)), []).append(
                            d_scores[
                                LANES * a : LANES * a + LANES, LANES * b : LANES * b + LANES
                            ].astype(jnp.float32)
                        )
                for apart, blocks in groups.items():
                    total = sum(blocks[1:], blocks[0])
                    if abs(apart) < 2:
                        near_acc[half, :, LANES * (1 - apart) : LANES * (2 - apart)] += total
                    else:
                        side = 0 if apart < 0 else 1
                        far_acc[half, :, LANES * side : LANES * side + LANES] += total
        dq_ref[span, :] = (jnp.concatenate(parts, axis=0).T * scale).astype(jnp.bfloat16)
    dk_ref[...] = (dk_acc[...] * scale).astype(jnp.bfloat16)
    dv_ref[...] = dv_acc[...].astype(jnp.bfloat16)
    if biased:
        for half in range(2):
            sums_ref[half, :, : 4 * LANES] = unband(near_acc[half])
            sums_ref[half, :, 4 * LANES :] = jnp.sum(far_acc[half], axis=0, keepdims=True)


def pair_spec(rows, shift):
    return pl.BlockSpec((rows, LANES), lambda pair, shift=shift: (0, shift + pair))


def row_spec(width):
    return pl.BlockSpec((2, 1, width), lambda pair: (pair, 0, 0))


def attend_cost(len_q, len_k, dots):
    return pl.CostEstimate(
        flops=2 * dots * HEADS * len_q * len_k * HD,
        bytes_accessed=8 * D * (len_q + len_k),
        transcendentals=HEADS * len_q * len_k,
    )


def attend(query, keys, values, parts, causal):
    len_q, len_k = query[0].shape[0], keys[0].shape[0]
    biased = parts is not None
    pairs = D // LANES
    first = [parts[1], parts[0]] if biased else []
    first_specs = [pl.BlockSpec(memory_space=pltpu.SMEM), row_spec(4 * LANES)] if biased else []
    return pl.pallas_call(
        partial(attend_kernel, biased, causal),
        grid=(pairs,),
        in_specs=first_specs
        + [
            pair_spec(len_q, query[1] * pairs),
            pair_spec(len_k, keys[1] * pairs),
            pair_spec(len_k, values[1] * pairs),
        ],
        out_specs=[pair_spec(len_q, 0), row_spec(len_q)],
        out_shape=[
            jax.ShapeDtypeStruct((len_q, D), jnp.bfloat16),
            jax.ShapeDtypeStruct((HEADS, 1, len_q), jnp.float32),
        ],
        compiler_params=params(),
        cost_estimate=attend_cost(len_q, len_k, 2),
    )(*first, query[0], keys[0], values[0])


def attend_back(query, keys, values, parts, causal, logsum, d_mixed):
    len_q, len_k = query[0].shape[0], keys[0].shape[0]
    biased = parts is not None
    pairs = D // LANES
    first = [parts[1], parts[0]] if biased else []
    first_specs = [pl.BlockSpec(memory_space=pltpu.SMEM), row_spec(4 * LANES)] if biased else []
    low = jnp.bfloat16
    return pl.pallas_call(
        partial(attend_back_kernel, biased, causal),
        grid=(pairs,),
        in_specs=first_specs
        + [
            pair_spec(len_q, query[1] * pairs),
            pair_spec(len_k, keys[1] * pairs),
            pair_spec(len_k, values[1] * pairs),
            pair_spec(len_q, 0),
            row_spec(len_q),
        ],
        out_specs=[pair_spec(len_q, 0), pair_spec(len_k, 0), pair_spec(len_k, 0)]
        + ([row_spec(6 * LANES)] if biased else []),
        out_shape=[
            jax.ShapeDtypeStruct((len_q, D), low),
            jax.ShapeDtypeStruct((len_k, D), low),
            jax.ShapeDtypeStruct((len_k, D), low),
        ]
        + ([jax.ShapeDtypeStruct((HEADS, 1, 6 * LANES), jnp.float32)] if biased else []),
        scratch_shapes=[
            pltpu.VMEM((len_k, LANES), jnp.float32),
            pltpu.VMEM((len_k, LANES), jnp.float32),
        ]
        + (
            [
                pltpu.VMEM((2, LANES, 4 * LANES), jnp.float32),
                pltpu.VMEM((2, LANES, 2 * LANES), jnp.float32),
            ]
            if biased
            else []
        ),
        compiler_params=params(),
        cost_estimate=attend_cost(len_q, len_k, 5),
    )(*first, query[0], keys[0], values[0], d_mixed, logsum)


gelu_scale = math.sqrt(2.0 / math.pi)
gelu_cube = 0.044715


def expert_kernel(x_ref, wi_ref, wo_ref, pre_ref, out_ref, acc_ref):
    block = pl.program_id(0)
    pre = dot_nn(x_ref[...], wi_ref[0, 0])
    pre_ref[0] = pre
    bend = jnp.tanh(gelu_scale * (pre + gelu_cube * (pre * pre * pre)))
    hidden = (0.5 * pre * (1.0 + bend)).astype(jnp.bfloat16)
    part = dot_nt(hidden, wo_ref[0, 0])

    @pl.when(block == 0)
    def _():
        acc_ref[...] = part

    @pl.when(block > 0)
    def _():
        acc_ref[...] += part

    @pl.when(block == pl.num_programs(0) - 1)
    def _():
        out_ref[...] = acc_ref[...].astype(jnp.bfloat16)


def expert_forward(arrived, weights):
    rows = arrived.shape[0]
    blocks, unused, unused_too, cols = weights.shape
    whole = pl.BlockSpec((rows, D), lambda j: (0, 0))
    return pl.pallas_call(
        expert_kernel,
        grid=(blocks,),
        in_specs=[
            whole,
            pl.BlockSpec((1, 1, D, cols), lambda j: (j, 0, 0, 0)),
            pl.BlockSpec((1, 1, D, cols), lambda j: (j, 1, 0, 0)),
        ],
        out_specs=[pl.BlockSpec((1, rows, cols), lambda j: (j, 0, 0)), whole],
        out_shape=[
            jax.ShapeDtypeStruct((blocks, rows, cols), jnp.float32),
            jax.ShapeDtypeStruct((rows, D), jnp.bfloat16),
        ],
        scratch_shapes=[pltpu.VMEM((rows, D), jnp.float32)],
        compiler_params=params(),
        cost_estimate=pl.CostEstimate(
            flops=4 * rows * D * FF,
            bytes_accessed=4 * D * FF + 4 * rows * (FF + D),
            transcendentals=rows * FF,
        ),
    )(arrived, weights, weights)


def expert_back_kernel(x_ref, g_ref, pre_ref, wi_ref, wo_ref, dw_ref, back_ref, acc_ref):
    block = pl.program_id(0)
    arrived = x_ref[...]
    grads = g_ref[...]
    pre = pre_ref[0]
    square = pre * pre
    bend = jnp.tanh(gelu_scale * (pre + gelu_cube * (square * pre)))
    half = 0.5 * (1.0 + bend)
    hidden = (pre * half).astype(jnp.bfloat16)
    slope = half + 0.5 * pre * (1.0 - bend * bend) * (
        gelu_scale * (1.0 + 3.0 * gelu_cube * square)
    )
    d_pre = (dot_nn(grads, wo_ref[0, 0]) * slope).astype(jnp.bfloat16)
    dw_ref[0, 0] = dot_tn(arrived, d_pre).astype(jnp.bfloat16)
    dw_ref[0, 1] = dot_tn(grads, hidden).astype(jnp.bfloat16)
    part = dot_nt(d_pre, wi_ref[0, 0])

    @pl.when(block == 0)
    def _():
        acc_ref[...] = part

    @pl.when(block > 0)
    def _():
        acc_ref[...] += part

    @pl.when(block == pl.num_programs(0) - 1)
    def _():
        back_ref[...] = acc_ref[...].astype(jnp.bfloat16)


def expert_backward(arrived, d_arrived, pre, weights):
    rows = arrived.shape[0]
    blocks, unused, unused_too, cols = weights.shape
    whole = pl.BlockSpec((rows, D), lambda j: (0, 0))
    return pl.pallas_call(
        expert_back_kernel,
        grid=(blocks,),
        in_specs=[
            whole,
            whole,
            pl.BlockSpec((1, rows, cols), lambda j: (j, 0, 0)),
            pl.BlockSpec((1, 1, D, cols), lambda j: (j, 0, 0, 0)),
            pl.BlockSpec((1, 1, D, cols), lambda j: (j, 1, 0, 0)),
        ],
        out_specs=[pl.BlockSpec((1, 2, D, cols), lambda j: (j, 0, 0, 0)), whole],
        out_shape=[
            jax.ShapeDtypeStruct((blocks, 2, D, cols), jnp.bfloat16),
            jax.ShapeDtypeStruct((rows, D), jnp.bfloat16),
        ],
        scratch_shapes=[pltpu.VMEM((rows, D), jnp.float32)],
        compiler_params=params(),
        cost_estimate=pl.CostEstimate(
            flops=8 * rows * D * FF,
            bytes_accessed=8 * D * FF + 4 * rows * (FF + 2 * D),
            transcendentals=rows * FF,
        ),
    )(arrived, d_arrived, pre, weights, weights)


def embed_kernel(unroll, ids_ref, table_ref, out_ref, list_ref, count_ref, held, rows, sem):
    chunk = pl.program_id(0)
    vocab = table_ref.shape[0]
    span = out_ref.shape[0]

    @pl.when(chunk == 0)
    def _():
        copy = pltpu.make_async_copy(table_ref, held.at[pl.ds(0, vocab)], sem)
        copy.start()
        held[pl.ds(vocab, 8), :] = jnp.zeros((8, D), jnp.float32)
        copy.wait()

    def some(step, found):
        for inner in range(unroll):
            row = step * unroll + inner
            source = ids_ref[chunk * span + row]
            rows[pl.ds(row, 1), :] = held[pl.ds(source, 1), :]
            list_ref[chunk * span + found] = row
            found = found + (source < vocab).astype(jnp.int32)
        return found

    count_ref[chunk] = lax.fori_loop(0, span // unroll, some, jnp.int32(0))
    out_ref[...] = rows[...].astype(jnp.bfloat16)


def embed(ids, table, span):
    count = ids.shape[0]
    vocab = table.shape[0]
    smem = pl.BlockSpec(memory_space=pltpu.SMEM)
    return pl.pallas_call(
        partial(embed_kernel, 8),
        grid=(count // span,),
        in_specs=[smem, pl.BlockSpec(memory_space=pl.ANY)],
        out_specs=[pl.BlockSpec((span, D), lambda j: (j, 0)), smem, smem],
        out_shape=[
            jax.ShapeDtypeStruct((count, D), jnp.bfloat16),
            jax.ShapeDtypeStruct((count,), jnp.int32),
            jax.ShapeDtypeStruct((count // span,), jnp.int32),
        ],
        scratch_shapes=[
            pltpu.VMEM((vocab + 8, D), jnp.float32),
            pltpu.VMEM((span, D), jnp.float32),
            pltpu.SemaphoreType.DMA,
        ],
        compiler_params=params(),
        cost_estimate=pl.CostEstimate(
            flops=0, bytes_accessed=4 * vocab * D + 2 * count * D, transcendentals=0
        ),
    )(ids, table)


def unembed_kernel(
    ids_ref, list_ref, count_ref, first_ref, enc_ref, dec_ref, out_ref, total, rows, sem
):
    chunk = pl.program_id(0)
    span = rows.shape[0]
    enc_rows = enc_ref.shape[1]

    @pl.when(chunk == 0)
    def _():
        copy = pltpu.make_async_copy(first_ref, total, sem)
        copy.start()
        copy.wait()

    rows[pl.ds(0, enc_rows), :] = enc_ref[0].astype(jnp.float32)
    rows[pl.ds(enc_rows, span - enc_rows), :] = dec_ref[0].astype(jnp.float32)

    def one(step, carry):
        row = list_ref[chunk * span + step]
        place = ids_ref[chunk * span + row]
        total[pl.ds(place, 1), :] += rows[pl.ds(row, 1), :]
        return carry

    lax.fori_loop(0, count_ref[chunk], one, 0)

    @pl.when(chunk == pl.num_programs(0) - 1)
    def _():
        out_ref[...] = total[...].astype(jnp.bfloat16)


def unembed(ids, listed, counts, first, enc, dec):
    chunks, enc_rows, unused = enc.shape
    dec_rows = dec.shape[1]
    vocab = first.shape[0]
    smem = pl.BlockSpec(memory_space=pltpu.SMEM)
    return pl.pallas_call(
        unembed_kernel,
        grid=(chunks,),
        in_specs=[
            smem,
            smem,
            smem,
            pl.BlockSpec(memory_space=pl.ANY),
            pl.BlockSpec((1, enc_rows, D), lambda j: (j, 0, 0)),
            pl.BlockSpec((1, dec_rows, D), lambda j: (j, 0, 0)),
        ],
        out_specs=pl.BlockSpec((vocab, D), lambda j: (0, 0)),
        out_shape=jax.ShapeDtypeStruct((vocab, D), jnp.bfloat16),
        scratch_shapes=[
            pltpu.VMEM((vocab, D), jnp.float32),
            pltpu.VMEM((enc_rows + dec_rows, D), jnp.float32),
            pltpu.SemaphoreType.DMA,
        ],
        compiler_params=params(),
        cost_estimate=pl.CostEstimate(
            flops=0,
            bytes_accessed=6 * vocab * D + 2 * chunks * (enc_rows + dec_rows) * D,
            transcendentals=0,
        ),
    )(ids, listed, counts, first, enc, dec)


def newton_kernel(x_ref, out_ref, gram_ref, poly_ref):
    blocks = x_ref.shape[1] // D

    def gram(source):
        for j in range(blocks):
            part = source[:, D * j : D * j + D]
            product = dot_nt(part, part)
            if j:
                gram_ref[...] += product
            else:
                gram_ref[...] = product

    gram(x_ref)
    row = lax.broadcasted_iota(jnp.int32, (D, D), 0)
    column = lax.broadcasted_iota(jnp.int32, (D, D), 1)
    whole = gram_ref[...].astype(jnp.bfloat16).astype(jnp.float32)
    scale = jnp.sum(jnp.where(row == column, whole, 0.0), keepdims=True) + eps_gram
    root = lax.rsqrt(scale)
    inverse = 1.0 / scale

    def step(source, factor, outer):
        product = gram_ref[...].astype(jnp.bfloat16)
        if factor is not None:
            product = (product.astype(jnp.float32) * factor).astype(jnp.bfloat16)
        poly_ref[...] = (
            coef_b * product.astype(jnp.float32) + coef_c * dot_nn(product, product)
        ).astype(jnp.bfloat16)
        for j in range(blocks):
            part = source[:, D * j : D * j + D]
            fresh = coef_a * part.astype(jnp.float32) + dot_nn(poly_ref[...], part)
            if outer is not None:
                fresh = fresh * outer
            out_ref[:, D * j : D * j + D] = fresh.astype(jnp.bfloat16)

    step(x_ref, inverse, root)

    def turn(index, carry):
        gram(out_ref)
        step(out_ref, None, None)
        return carry

    lax.fori_loop(1, NS_ITERS, turn, 0)


def newton(matrix):
    cols = matrix.shape[1]
    vmem = pl.BlockSpec(memory_space=pltpu.VMEM)
    return pl.pallas_call(
        newton_kernel,
        in_specs=[vmem],
        out_specs=vmem,
        out_shape=jax.ShapeDtypeStruct(matrix.shape, jnp.bfloat16),
        scratch_shapes=[pltpu.VMEM((D, D), jnp.float32), pltpu.VMEM((D, D), jnp.bfloat16)],
        compiler_params=pltpu.CompilerParams(vmem_limit_bytes=VMEM_LIMIT),
        cost_estimate=pl.CostEstimate(
            flops=NS_ITERS * (4 * D * D * cols + 2 * D * D * D),
            bytes_accessed=4 * D * cols,
            transcendentals=0,
        ),
    )(matrix)


def project(rows, stored):
    flat = stored.reshape(-1, D)
    return dot_nt(rows, flat)


def swap_owners(buffer):
    return lax.all_to_all(buffer, "dp", split_axis=0, concat_axis=0, tiled=True)


def dispatch(places, count):
    slot = lax.broadcasted_iota(jnp.int32, (count, places.shape[0]), 0)
    return (slot == places[None, :]).astype(jnp.bfloat16)


def route_places(routes, experts, cap):
    hot = (routes[:, None] == jnp.arange(experts, dtype=jnp.int32)[None, :]).astype(jnp.float32)
    rows = routes.shape[0]
    earlier = (
        lax.broadcasted_iota(jnp.int32, (rows, rows), 1)
        < lax.broadcasted_iota(jnp.int32, (rows, rows), 0)
    ).astype(jnp.bfloat16)
    ranks = dot_nn(earlier, hot.astype(jnp.bfloat16))
    slots = jnp.sum(hot * ranks, axis=1).astype(jnp.int32)
    return hot, routes * cap + slots


def moe_forward(resid, gain, router, weights, hot, places, cap):
    experts = router.shape[1]
    normed, inverse = normalize(resid, gain)
    normed_low = normed.astype(jnp.bfloat16)
    probs = jax.nn.softmax(
        jnp.dot(normed_low.astype(jnp.float32), router, precision=highest), axis=-1
    )
    spread = dispatch(places, experts * cap)
    buffer = dot_nn(spread, normed_low).astype(jnp.bfloat16)
    arrived = swap_owners(buffer.reshape(experts, cap, D)).reshape(-1, D)
    pre, result = expert_forward(arrived, weights)
    returned = swap_owners(result.reshape(experts, cap, D)).reshape(-1, D)
    outputs = dot_tn(spread, returned)
    gate = jnp.sum(probs * hot, axis=1)
    kept = (normed_low, inverse, probs, gate, arrived, pre, outputs)
    return (resid + gate[:, None] * outputs, kept)


def moe_backward(resid, gain, router, weights, hot, places, cap, kept, grad, aux_scale, frac):
    normed_low, inverse, probs, gate, arrived, pre, outputs = kept
    experts = router.shape[1]
    d_gate = jnp.sum(grad * outputs, axis=1)
    d_rows = (gate[:, None] * grad).astype(jnp.bfloat16)
    spread = dispatch(places, experts * cap)
    buffer = dot_nn(spread, d_rows).astype(jnp.bfloat16)
    d_arrived = swap_owners(buffer.reshape(experts, cap, D)).reshape(-1, D)
    d_weights, d_back = expert_backward(arrived, d_arrived, pre, weights)
    returned = swap_owners(d_back.reshape(experts, cap, D)).reshape(-1, D)
    d_normed = dot_tn(spread, returned)
    d_probs = hot * d_gate[:, None] + aux_scale * frac[None, :]
    d_logits = probs * (d_probs - jnp.sum(probs * d_probs, axis=-1, keepdims=True))
    d_router = jnp.dot(normed_low.astype(jnp.float32).T, d_logits, precision=highest)
    d_normed = d_normed + jnp.dot(d_logits, router.T, precision=highest)
    d_resid, d_gain = normalize_back(resid, inverse, gain, d_normed)
    return (grad + d_resid, d_gain, d_router, d_weights)


def self_forward(resid, gain, weights, parts, causal):
    normed, inverse = normalize(resid, gain)
    normed = normed.astype(jnp.bfloat16)
    joined = project(normed, weights[0:3]).astype(jnp.bfloat16)
    mixed, logsum = attend((joined, 0), (joined, 1), (joined, 2), parts, causal)
    return (resid + project(mixed, weights[3]), (resid, inverse, normed, joined, mixed, logsum))


def self_backward(gain, weights, parts, causal, kept, grad):
    resid, inverse, normed, joined, mixed, logsum = kept
    grad_low = grad.astype(jnp.bfloat16)
    d_mixed = dot_nn(grad_low, weights[3]).astype(jnp.bfloat16)
    d_query, d_key, d_value, sums = attend_back(
        (joined, 0), (joined, 1), (joined, 2), parts, causal, logsum, d_mixed
    )
    d_normed = (
        dot_nn(d_query, weights[0]) + dot_nn(d_key, weights[1]) + dot_nn(d_value, weights[2])
    )
    d_weights = [
        dot_tn(d_query, normed),
        dot_tn(d_key, normed),
        dot_tn(d_value, normed),
        dot_tn(grad_low, mixed),
    ]
    d_resid, d_gain = normalize_back(resid, inverse, gain, d_normed)
    return (grad + d_resid, d_gain, d_weights, bias_sums(sums, parts[2], parts[3]))


def cross_forward(resid, gain, weights, memory):
    normed, inverse = normalize(resid, gain)
    normed = normed.astype(jnp.bfloat16)
    query = project(normed, weights[0]).astype(jnp.bfloat16)
    joined = project(memory, weights[1:3]).astype(jnp.bfloat16)
    mixed, logsum = attend((query, 0), (joined, 0), (joined, 1), None, False)
    kept = (resid, inverse, normed, query, joined, mixed, logsum)
    return (resid + project(mixed, weights[3]), kept)


def cross_backward(gain, weights, memory, kept, grad):
    resid, inverse, normed, query, joined, mixed, logsum = kept
    grad_low = grad.astype(jnp.bfloat16)
    d_mixed = dot_nn(grad_low, weights[3]).astype(jnp.bfloat16)
    d_query, d_key, d_value = attend_back(
        (query, 0), (joined, 0), (joined, 1), None, False, logsum, d_mixed
    )
    d_normed = dot_nn(d_query, weights[0])
    d_memory = dot_nn(d_key, weights[1]) + dot_nn(d_value, weights[2])
    d_weights = [
        dot_tn(d_query, normed),
        dot_tn(d_key, memory),
        dot_tn(d_value, memory),
        dot_tn(grad_low, mixed),
    ]
    d_resid, d_gain = normalize_back(resid, inverse, gain, d_normed)
    return (grad + d_resid, d_gain, d_weights, d_memory)


def route_share(routes, experts):
    flat_routes = routes.reshape(-1)
    hot = (flat_routes[None, :] == jnp.arange(experts, dtype=jnp.int32)[:, None]).astype(
        jnp.float32
    )
    return jnp.sum(hot, axis=1) / flat_routes.shape[0]


def adam(weight, first, second, grad, rate, decay):
    first = beta_one * first + (1 - beta_one) * grad
    second = beta_two * second + (1 - beta_two) * grad * grad
    update = first / (1 - beta_one**STEP) / (jnp.sqrt(second / (1 - beta_two**STEP)) + eps_adam)
    return (weight - rate * (update + decay * weight), first, second)


def share_columns(d_weights, groups):
    stacked = jnp.stack([part.astype(jnp.bfloat16) for part in d_weights])
    count = stacked.shape[0]
    split = jnp.transpose(stacked.reshape(count, groups, -1, D), (1, 0, 2, 3))
    return lax.psum_scatter(split, "mp", scatter_dimension=0, tiled=False)


def orthogonalize(dense_mom, expert_mom, groups):
    cols = expert_mom.shape[2]
    cols_dense = dense_mom.shape[1]
    split = D // cols
    count_expert, count_dense = expert_mom.shape[0], dense_mom.shape[0]
    depth = cols_dense * split
    frames = jnp.transpose(
        dense_mom.astype(jnp.bfloat16).reshape(count_dense, cols_dense, split, cols), (0, 2, 1, 3)
    ).reshape(count_dense, depth, cols)
    frames = jnp.pad(frames, ((0, 0), (0, D - depth), (0, 0)))
    spare = groups - count_expert - count_dense
    sent = jnp.concatenate(
        [expert_mom.astype(jnp.bfloat16), frames, jnp.zeros((spare, D, cols), jnp.bfloat16)],
        axis=0,
    )
    arrived = lax.all_to_all(sent, "mp", split_axis=0, concat_axis=0, tiled=True)
    whole = jnp.transpose(arrived, (1, 0, 2)).reshape(D, groups * cols)
    square = jnp.transpose(
        arrived[:, :depth].reshape(groups, split, cols_dense, cols), (0, 2, 1, 3)
    ).reshape(D, D)
    square = jnp.pad(square, ((0, 0), (0, groups * cols - D)))
    is_expert = lax.axis_index("mp") < count_expert
    result = newton(jnp.where(is_expert, whole, square))
    back_expert = jnp.transpose(result.reshape(D, groups, cols), (1, 0, 2))
    back_dense = jnp.transpose(
        result[:, :D].reshape(groups, cols_dense, split, cols), (0, 2, 1, 3)
    ).reshape(groups, depth, cols)
    back_dense = jnp.pad(back_dense, ((0, 0), (0, D - depth), (0, 0)))
    returned = lax.all_to_all(
        jnp.where(is_expert, back_expert, back_dense),
        "mp",
        split_axis=0,
        concat_axis=0,
        tiled=True,
    )
    dense_orth = jnp.transpose(
        returned[count_expert : count_expert + count_dense, :depth].reshape(
            count_dense, split, cols_dense, cols
        ),
        (0, 2, 1, 3),
    ).reshape(count_dense, cols_dense, D)
    return dense_orth, returned[:count_expert]


def on_device(
    src_ids,
    targets,
    loss_pos,
    loss_mask,
    routes_src,
    routes_tgt,
    dense_w,
    dense_m,
    expert_w,
    expert_m,
    table_w,
    table_m,
    table_v,
    gains_w,
    gains_m,
    gains_v,
    router_w,
    router_m,
    router_v,
    bias_w,
    bias_m,
    bias_v,
):
    groups = lax.axis_size("mp")
    column = lax.axis_index("mp")
    experts = lax.axis_size("dp")
    src_len = src_ids.shape[1]
    tgt_len = targets.shape[1]
    npos = loss_pos.shape[1]
    vocab_dev = table_w.shape[0]
    own_seq = lax.axis_index("dp") * groups + column
    rows_dev = src_len + tgt_len
    count_dense = dense_w.shape[0]
    low = jnp.bfloat16
    dense_local = dense_w.astype(low).reshape(count_dense, -1, D)
    enc_dense = lax.all_gather(dense_local[0:4], "mp", axis=1, tiled=True)
    expert_local = expert_w[:, :, 0].astype(low)
    dec_ids = jnp.concatenate(
        [jnp.zeros((targets.shape[0], 1), jnp.int32), targets[:, :-1]], axis=1
    )
    all_ids = jnp.concatenate([src_ids, dec_ids], axis=1).reshape(-1)
    local_ids = all_ids - column * vocab_dev
    inside = (local_ids >= 0) & (local_ids < vocab_dev)
    local_ids = jnp.where(inside, local_ids, vocab_dev)
    shared, listed, counts = embed(local_ids, table_w, rows_dev)
    embedded = lax.psum_scatter(shared, "mp", scatter_dimension=0, tiled=True).astype(jnp.float32)
    enc_expert = lax.all_gather(expert_local[0], "mp", axis=0, tiled=False)
    dec_dense = lax.all_gather(dense_local[4:12], "mp", axis=1, tiled=True)
    dec_expert = lax.all_gather(expert_local[1], "mp", axis=0, tiled=False)
    table_low = table_w.astype(low)
    own_src = lax.dynamic_slice_in_dim(routes_src, own_seq, 1, 0).reshape(-1)
    own_tgt = lax.dynamic_slice_in_dim(routes_tgt, own_seq, 1, 0).reshape(-1)
    cap_src = (5 * src_len + 4 * experts - 1) // (4 * experts)
    cap_tgt = (5 * tgt_len + 4 * experts - 1) // (4 * experts)
    total_src = routes_src.shape[0] * routes_src.shape[1]
    total_tgt = routes_tgt.shape[0] * routes_tgt.shape[1]
    frac_src = route_share(routes_src, experts)
    frac_tgt = route_share(routes_tgt, experts)
    hot_src, places_src = route_places(own_src, experts, cap_src)
    hot_tgt, places_tgt = route_places(own_tgt, experts, cap_tgt)
    enc_parts = bias_parts(bias_w[0], False)
    dec_parts = bias_parts(bias_w[1], True)
    enc_mid, enc_kept = self_forward(embedded[:src_len], gains_w[0], enc_dense, enc_parts, False)
    dec_mid, dec_kept = self_forward(
        embedded[src_len:], gains_w[3], dec_dense[0:4], dec_parts, True
    )
    enc_out, enc_moe = moe_forward(
        enc_mid, gains_w[1], router_w[0], enc_expert, hot_src, places_src, cap_src
    )
    memory_float, memory_inv = normalize(enc_out, gains_w[2])
    memory = memory_float.astype(low)
    dec_crossed, cross_kept = cross_forward(dec_mid, gains_w[4], dec_dense[4:8], memory)
    dec_result, dec_moe = moe_forward(
        dec_crossed, gains_w[5], router_w[1], dec_expert, hot_tgt, places_tgt, cap_tgt
    )
    final_float, final_inv = normalize(dec_result, gains_w[6])
    final_low = final_float.astype(low)
    head_scale = D ** (-0.5)
    own_pos = lax.dynamic_slice_in_dim(loss_pos, column, 1, 0).reshape(-1)
    pick = (
        own_pos[:, None] == lax.broadcasted_iota(jnp.int32, (npos, tgt_len), 1)
    ).astype(low)
    chosen = dot_nn(pick, final_low).astype(low)
    gathered = lax.all_gather(chosen, "mp", axis=0, tiled=True)
    logits = dot_nt(gathered, table_low) * head_scale
    wanted = jnp.take_along_axis(targets, loss_pos, axis=1).reshape(-1) - column * vocab_dev
    hits = jnp.arange(vocab_dev, dtype=jnp.int32)[None, :] == wanted[:, None]
    top = jnp.max(logits, axis=1)
    stats = lax.all_gather(
        jnp.stack(
            [
                top,
                jnp.sum(jnp.exp(logits - top[:, None]), axis=1),
                jnp.sum(jnp.where(hits, logits, 0.0), axis=1),
            ]
        ),
        "mp",
        axis=0,
        tiled=False,
    )
    all_top = jnp.max(stats[:, 0], axis=0)
    expsum = jnp.sum(stats[:, 1] * jnp.exp(stats[:, 0] - all_top[None, :]), axis=0)
    picked = jnp.sum(stats[:, 2], axis=0)
    logsum = all_top + jnp.log(expsum)
    mask_rows = loss_mask.reshape(-1).astype(jnp.float32)
    own_loss = jnp.sum(
        lax.dynamic_slice_in_dim(mask_rows * (logsum - picked), column * npos, npos)
    )
    own_count = jnp.sum(lax.dynamic_slice_in_dim(mask_rows, column * npos, npos))
    d_logits = (
        mask_rows[:, None] * (jnp.exp(logits - logsum[:, None]) - hits.astype(jnp.float32))
    ).astype(low)
    d_shares = lax.all_to_all(
        (dot_nn(d_logits, table_low) * head_scale).astype(low).reshape(groups, npos, D),
        "mp",
        split_axis=0,
        concat_axis=0,
        tiled=True,
    )
    table_grad = dot_tn(d_logits, gathered) * head_scale
    d_chosen = jnp.sum(d_shares.astype(jnp.float32), axis=0).astype(low)
    d_final = dot_tn(pick, d_chosen)
    d_dec, gain_final = normalize_back(dec_result, final_inv, gains_w[6], d_final)
    d_dec, gain_dec_moe, dec_router, dec_dw = moe_backward(
        dec_crossed,
        gains_w[5],
        router_w[1],
        dec_expert,
        hot_tgt,
        places_tgt,
        cap_tgt,
        dec_moe,
        d_dec,
        aux_weight * experts / total_tgt,
        frac_tgt,
    )
    dec_share = lax.psum_scatter(dec_dw, "mp", scatter_dimension=0, tiled=False)
    d_dec, gain_cross, cross_dw, d_memory = cross_backward(
        gains_w[4], dec_dense[4:8], memory, cross_kept, d_dec
    )
    d_enc, gain_memory = normalize_back(enc_out, memory_inv, gains_w[2], d_memory)
    d_dec, gain_self, self_dw, dec_bias = self_backward(
        gains_w[3], dec_dense[0:4], dec_parts, True, dec_kept, d_dec
    )
    dec_rows = lax.all_gather(d_dec.astype(low), "mp", axis=0, tiled=False)
    dec_cols = share_columns(self_dw + cross_dw, groups)
    d_enc, gain_enc_moe, enc_router, enc_dw = moe_backward(
        enc_mid,
        gains_w[1],
        router_w[0],
        enc_expert,
        hot_src,
        places_src,
        cap_src,
        enc_moe,
        d_enc,
        aux_weight * experts / total_src,
        frac_src,
    )
    enc_share = lax.psum_scatter(enc_dw, "mp", scatter_dimension=0, tiled=False)
    d_enc, gain_enc, enc_self_dw, enc_bias = self_backward(
        gains_w[0], enc_dense, enc_parts, False, enc_kept, d_enc
    )
    enc_rows = lax.all_gather(d_enc.astype(low), "mp", axis=0, tiled=False)
    enc_cols = share_columns(enc_self_dw, groups)
    table_sum = unembed(local_ids, listed, counts, table_grad, enc_rows, dec_rows)
    table_piece = lax.psum_scatter(table_sum, "dp", scatter_dimension=0, tiled=True).astype(
        jnp.float32
    )
    dense_share = jnp.concatenate([enc_cols, dec_cols], axis=0)
    per_dev = -(-count_dense // experts)
    filler = per_dev * experts - count_dense
    dense_piece = lax.psum_scatter(
        jnp.pad(dense_share, ((0, filler), (0, 0), (0, 0))),
        "dp",
        scatter_dimension=0,
        tiled=True,
    ).astype(jnp.float32)
    expert_share = jnp.stack([enc_share, dec_share]).astype(jnp.float32)
    gains_grad = jnp.stack(
        [gain_enc, gain_enc_moe, gain_memory, gain_self, gain_cross, gain_dec_moe, gain_final]
    )
    router_grad = jnp.stack([enc_router, dec_router])
    bias_grad = jnp.stack([enc_bias, dec_bias])
    load_src = jnp.sum(enc_moe[2], axis=0)
    load_tgt = jnp.sum(dec_moe[2], axis=0)
    gains_grad, router_grad, bias_grad, loss_sum, count, load_src, load_tgt = lax.psum(
        (gains_grad, router_grad, bias_grad, own_loss, own_count, load_src, load_tgt),
        ("dp", "mp"),
    )
    squares = (
        jnp.sum(dense_piece * dense_piece)
        + jnp.sum(expert_share * expert_share)
        + jnp.sum(table_piece * table_piece)
    )
    squares = lax.psum(squares, ("dp", "mp"))
    squares = squares + sum(
        (jnp.sum(part * part) for part in (gains_grad, router_grad, bias_grad))
    )
    grad_norm = jnp.sqrt(squares)
    clip = 1.0 / jnp.maximum(grad_norm, 1.0)
    aux = (
        aux_weight
        * experts
        * (jnp.sum(frac_src * load_src) / total_src + jnp.sum(frac_tgt * load_tgt) / total_tgt)
    )
    loss = jnp.stack([loss_sum + aux, count])
    old_piece = lax.dynamic_slice_in_dim(
        jnp.pad(dense_m, ((0, filler), (0, 0))), lax.axis_index("dp") * per_dev, per_dev, 0
    ).reshape(per_dev, -1, D)
    piece_moment = 0.5 * old_piece + clip * dense_piece
    expert_moment = 0.5 * expert_m + clip * expert_share[:, :, None]
    moment_flat = lax.all_gather(piece_moment.astype(low), "dp", axis=0, tiled=True)[:count_dense]
    dense_moment = moment_flat.reshape(count_dense, -1).astype(jnp.float32)
    cols = expert_w.shape[4]
    piece_orth, expert_orth = orthogonalize(
        piece_moment, expert_moment.reshape(-1, D, cols), groups
    )
    dense_orth = lax.all_gather(piece_orth, "dp", axis=0, tiled=True)[:count_dense]
    dense_orth = dense_orth.reshape(count_dense, -1).astype(jnp.float32)
    keep_rate = 1 - rate_matrix * decay_matrix
    dense_new = dense_w * keep_rate - rate_matrix * 0.2 * math.sqrt(D) * dense_orth
    expert_new = expert_w * keep_rate - rate_matrix * 0.2 * math.sqrt(
        max(D, FF)
    ) * expert_orth.astype(jnp.float32).reshape(expert_w.shape)
    piece_rows = table_m.shape[0]
    table_clipped = clip * table_piece
    table_new, table_first, table_second = adam(
        lax.dynamic_slice_in_dim(table_w, lax.axis_index("dp") * piece_rows, piece_rows, 0),
        table_m,
        table_v,
        table_clipped,
        1.5,
        0.01,
    )

    def part_of(array, like):
        size = like.shape[1]
        return lax.dynamic_slice_in_dim(array, column * size, size, 1)

    gains_new, gains_first, gains_second = adam(
        part_of(gains_w, gains_m), gains_m, gains_v, clip * part_of(gains_grad, gains_m), 0.5, 0.0
    )
    router_new, router_first, router_second = adam(
        part_of(router_w, router_m),
        router_m,
        router_v,
        clip * part_of(router_grad, router_m),
        0.02,
        0.01,
    )
    bias_new, bias_first, bias_second = adam(
        part_of(bias_w, bias_m), bias_m, bias_v, clip * part_of(bias_grad, bias_m), 0.5, 0.0
    )
    return (
        loss,
        grad_norm,
        dense_new,
        dense_moment,
        dense_new.astype(low),
        expert_new,
        expert_moment,
        expert_new.astype(low),
        table_new,
        table_clipped,
        table_second,
        gains_new,
        gains_first,
        gains_second,
        router_new,
        router_first,
        router_second,
        bias_new,
        bias_first,
        bias_second,
    )


def solution(mesh):
    in_specs = (
        P("dp", None),
        P("dp", None),
        P("dp", None),
        P("dp", None),
        P(),
        P(),
        P(None, "mp"),
        P(None, "mp"),
        P(None, None, "dp", None, "mp"),
        P(None, None, "dp", None, "mp"),
        P("mp", None),
        P(("mp", "dp"), None),
        P(("mp", "dp"), None),
        P(),
        P(None, "mp"),
        P(None, "mp"),
        P(),
        P(None, "mp", None),
        P(None, "mp", None),
        P(),
        P(None, "mp", None),
        P(None, "mp", None),
    )
    out_specs = (
        P(),
        P(),
        P(None, "mp"),
        P(None, "mp"),
        P(None, "mp"),
        P(None, None, "dp", None, "mp"),
        P(None, None, "dp", None, "mp"),
        P(None, None, "dp", None, "mp"),
        P(("mp", "dp"), None),
        P(("mp", "dp"), None),
        P(("mp", "dp"), None),
        P(None, "mp"),
        P(None, "mp"),
        P(None, "mp"),
        P(None, "mp", None),
        P(None, "mp", None),
        P(None, "mp", None),
        P(None, "mp", None),
        P(None, "mp", None),
        P(None, "mp", None),
    )
    return jax.shard_map(
        on_device, mesh=mesh, in_specs=in_specs, out_specs=out_specs, check_vma=False
    )
```

```python
from functools import partial
import math

import jax
import jax.numpy as jnp
from jax import lax
from jax.experimental import pallas as pl
from jax.experimental.pallas import tpu as pltpu
from jax.sharding import PartitionSpec as P

D = 768
HEADS = 12
HD = 64
FF = 3072
NS_ITERS = 5
STEP = 10


eps_norm = 1e-06
eps_gram = 1e-07
eps_adam = 1e-08
neg_fill = -1000000000.0
coef_a = 3.4445
coef_b = -4.775
coef_c = 2.0315
beta_one = 0.9
beta_two = 0.95
rate_matrix = 0.2
decay_matrix = 0.01
aux_weight = 0.01
enc_edges = (12, 16, 23, 32, 46, 64, 91)
dec_edges = (19, 21, 24, 27, 31, 35, 40, 46, 52, 59, 67, 77, 87, 99, 113)
highest = lax.Precision.HIGHEST


def normalize(rows, gain):
    inverse = lax.rsqrt(jnp.mean(rows * rows, axis=-1, keepdims=True) + eps_norm)
    return (rows * inverse * gain, inverse)


def normalize_back(rows, inverse, gain, grad):
    scaled = grad * gain
    d_rows = inverse * scaled - rows * inverse**3 * jnp.mean(scaled * rows, axis=-1, keepdims=True)
    return (d_rows, jnp.sum(grad * rows * inverse, axis=0))


def bucket_of(relative, causal):
    if causal:
        distance = jnp.maximum(-relative, 0)
        far = 16 + sum(((distance >= edge).astype(jnp.int32) for edge in dec_edges))
        return jnp.where(distance < 16, distance, far)
    distance = jnp.abs(relative)
    far = 8 + sum(((distance >= edge).astype(jnp.int32) for edge in enc_edges))
    return jnp.where(distance < 8, distance, far) + 16 * (relative > 0).astype(jnp.int32)


LANES = 128
CHUNK = 768
WIDE = 768
FETCH = 128
GIVE = 48
VMEM_LIMIT = 60 * 1024 * 1024


def params(count=1, **more):
    return pltpu.CompilerParams(
        dimension_semantics=("arbitrary",) * count, vmem_limit_bytes=VMEM_LIMIT, **more
    )


def dot_nn(left, right):
    return lax.dot_general(
        left, right, (((1,), (0,)), ((), ())), preferred_element_type=jnp.float32
    )


def dot_nt(left, right):
    return lax.dot_general(
        left, right, (((1,), (1,)), ((), ())), preferred_element_type=jnp.float32
    )


def dot_tn(left, right):
    return lax.dot_general(
        left, right, (((0,), (0,)), ((), ())), preferred_element_type=jnp.float32
    )


def own_lanes(rows, half):
    lane = lax.broadcasted_iota(jnp.int32, rows.shape, 1)
    keep = lane >= HD if half else lane < HD
    return jnp.where(keep, rows, jnp.zeros_like(rows))


def band_offsets():
    place = jnp.arange(4 * LANES, dtype=jnp.int32)
    return LANES - jnp.where(place < 3 * LANES, place, place - 4 * LANES)


def bias_parts(table, causal):
    count = table.shape[0]
    hot = (
        bucket_of(band_offsets(), causal)[:, None] == jnp.arange(count, dtype=jnp.int32)[None, :]
    ).astype(jnp.float32)
    band = jnp.dot(hot, table, precision=highest).T[:, None, :]
    ends = bucket_of(jnp.array([-2 * LANES, 2 * LANES], jnp.int32), causal)
    hot_ends = (ends[:, None] == jnp.arange(count, dtype=jnp.int32)[None, :]).astype(jnp.float32)
    far = jnp.dot(hot_ends, table, precision=highest)
    return band, far, hot, hot_ends


def bias_sums(sums, hot, hot_ends):
    per_place = sums[:, 0, :]
    near = per_place[:, : 4 * LANES]
    far = jnp.sum(per_place[:, 4 * LANES :].reshape(-1, 2, LANES), axis=2)
    return jnp.dot(hot.T, near.T, precision=highest) + jnp.dot(
        hot_ends.T, far.T, precision=highest
    )


def scores_of(keys, queries, head, chunk, far_ref, band, causal):
    scores = dot_nt(keys, queries)
    len_k, width = scores.shape
    if band is not None:
        rows = []
        for a in range(len_k // LANES):
            columns = []
            for b in range(width // LANES):
                apart = a - (chunk * (width // LANES) + b)
                if apart < -1:
                    bias = far_ref[0, head]
                elif apart > 1:
                    bias = far_ref[1, head]
                else:
                    bias = band[:, LANES * (1 - apart) : LANES * (2 - apart)]
                columns.append(
                    scores[LANES * a : LANES * a + LANES, LANES * b : LANES * b + LANES] + bias
                )
            rows.append(jnp.concatenate(columns, axis=1))
        scores = jnp.concatenate(rows, axis=0)
    if causal:
        allowed = lax.broadcasted_iota(jnp.int32, scores.shape, 0) <= (
            lax.broadcasted_iota(jnp.int32, scores.shape, 1) + chunk * width
        )
        scores = jnp.where(allowed, scores, neg_fill)
    return scores


def band_of(band_ref, half):
    row = jnp.broadcast_to(band_ref[half], (LANES, 4 * LANES))
    return pltpu.roll(row, 0, 1, stride=1, stride_axis=0)


def unband(sums):
    row = lax.broadcasted_iota(jnp.int32, sums.shape, 0)
    step = 1
    while step < LANES:
        sums = jnp.where(
            (row & step) != 0, pltpu.roll(sums, sums.shape[1] - step, 1), sums
        )
        step *= 2
    return jnp.sum(sums, axis=0, keepdims=True)


def attend_kernel(biased, causal, *refs):
    if biased:
        far_ref, band_ref, *refs = refs
    q_ref, k_ref, v_ref, out_ref, lse_ref = refs
    pair = pl.program_id(0)
    keys = k_ref[...]
    values_t = v_ref[...].T
    len_q = q_ref.shape[0]
    width = min(CHUNK, len_q)
    bands = [band_of(band_ref, half) if biased else None for half in range(2)]
    for chunk in range(len_q // width):
        span = pl.ds(chunk * width, width)
        queries = q_ref[span, :] * HD ** (-0.5)
        parts = []
        for half in range(2):
            scores = scores_of(
                keys,
                own_lanes(queries, half),
                2 * pair + half,
                chunk,
                far_ref if biased else None,
                bands[half],
                causal,
            )
            top = jnp.max(scores, axis=0, keepdims=True)
            expo = jnp.exp(scores - top)
            total = jnp.sum(expo, axis=0, keepdims=True)
            mixed = dot_nn(values_t[HD * half : HD * half + HD], expo.astype(jnp.bfloat16))
            parts.append(mixed * (1.0 / total))
            lse_ref[half, :, span] = top + jnp.log(total)
        out_ref[span, :] = jnp.concatenate(parts, axis=0).T.astype(jnp.bfloat16)


def attend_back_kernel(biased, causal, *refs):
    if biased:
        far_ref, band_ref, *refs = refs
    q_ref, k_ref, v_ref, g_ref, lse_ref, dq_ref, dk_ref, dv_ref, *refs = refs
    if biased:
        sums_ref, dk_acc, dv_acc, near_acc, far_acc = refs
    else:
        dk_acc, dv_acc = refs
    pair = pl.program_id(0)
    keys = k_ref[...]
    keys_t = keys.T
    values = v_ref[...]
    len_q, len_k = q_ref.shape[0], k_ref.shape[0]
    width = min(CHUNK, len_q)
    scale = HD ** (-0.5)
    dk_acc[...] = jnp.zeros_like(dk_acc)
    dv_acc[...] = jnp.zeros_like(dv_acc)
    bands = [band_of(band_ref, half) if biased else None for half in range(2)]
    if biased:
        near_acc[...] = jnp.zeros_like(near_acc)
        far_acc[...] = jnp.zeros_like(far_acc)
    for chunk in range(len_q // width):
        span = pl.ds(chunk * width, width)
        parts = []
        for half in range(2):
            queries = own_lanes(q_ref[span, :] * HD ** (-0.5), half)
            grads = own_lanes(g_ref[span, :], half)
            scores = scores_of(
                keys,
                queries,
                2 * pair + half,
                chunk,
                far_ref if biased else None,
                bands[half],
                causal,
            )
            probs = jnp.exp(scores - lse_ref[half, :, span])
            d_probs = dot_nt(values, grads)
            delta = jnp.sum(probs * d_probs, axis=0, keepdims=True)
            d_scores = (probs * (d_probs - delta)).astype(jnp.bfloat16)
            dk_acc[...] += dot_nn(d_scores, queries)
            dv_acc[...] += dot_nn(probs.astype(jnp.bfloat16), grads)
            parts.append(dot_nn(keys_t[HD * half : HD * half + HD], d_scores))
            if biased:
                groups = {}
                for a in range(len_k // LANES):
                    for b in range(width // LANES):
                        apart = a - (chunk * (width // LANES) + b)
                        if causal and apart > 0:
                            continue
                        groups.setdefault(max(-2, min(2, apart)), []).append(
                            d_scores[
                                LANES * a : LANES * a + LANES, LANES * b : LANES * b + LANES
                            ].astype(jnp.float32)
                        )
                for apart, blocks in groups.items():
                    total = sum(blocks[1:], blocks[0])
                    if abs(apart) < 2:
                        near_acc[half, :, LANES * (1 - apart) : LANES * (2 - apart)] += total
                    else:
                        side = 0 if apart < 0 else 1
                        far_acc[half, :, LANES * side : LANES * side + LANES] += total
        dq_ref[span, :] = (jnp.concatenate(parts, axis=0).T * scale).astype(jnp.bfloat16)
    dk_ref[...] = dk_acc[...].astype(jnp.bfloat16)
    dv_ref[...] = dv_acc[...].astype(jnp.bfloat16)
    if biased:
        for half in range(2):
            sums_ref[half, :, : 4 * LANES] = unband(near_acc[half])
            sums_ref[half, :, 4 * LANES :] = jnp.sum(far_acc[half], axis=0, keepdims=True)


def pair_spec(rows, shift):
    return pl.BlockSpec((rows, LANES), lambda pair, shift=shift: (0, shift + pair))


def row_spec(width):
    return pl.BlockSpec((2, 1, width), lambda pair: (pair, 0, 0))


def attend_cost(len_q, len_k, dots):
    return pl.CostEstimate(
        flops=2 * dots * HEADS * len_q * len_k * HD,
        bytes_accessed=8 * D * (len_q + len_k),
        transcendentals=HEADS * len_q * len_k,
    )


def attend(query, keys, values, parts, causal):
    len_q, len_k = query[0].shape[0], keys[0].shape[0]
    biased = parts is not None
    pairs = D // LANES
    first = [parts[1], parts[0]] if biased else []
    first_specs = [pl.BlockSpec(memory_space=pltpu.SMEM), row_spec(4 * LANES)] if biased else []
    return pl.pallas_call(
        partial(attend_kernel, biased, causal),
        grid=(pairs,),
        in_specs=first_specs
        + [
            pair_spec(len_q, query[1] * pairs),
            pair_spec(len_k, keys[1] * pairs),
            pair_spec(len_k, values[1] * pairs),
        ],
        out_specs=[pair_spec(len_q, 0), row_spec(len_q)],
        out_shape=[
            jax.ShapeDtypeStruct((len_q, D), jnp.bfloat16),
            jax.ShapeDtypeStruct((HEADS, 1, len_q), jnp.float32),
        ],
        compiler_params=params(),
        cost_estimate=attend_cost(len_q, len_k, 2),
    )(*first, query[0], keys[0], values[0])


def attend_back(query, keys, values, parts, causal, logsum, d_mixed):
    len_q, len_k = query[0].shape[0], keys[0].shape[0]
    biased = parts is not None
    pairs = D // LANES
    first = [parts[1], parts[0]] if biased else []
    first_specs = [pl.BlockSpec(memory_space=pltpu.SMEM), row_spec(4 * LANES)] if biased else []
    low = jnp.bfloat16
    return pl.pallas_call(
        partial(attend_back_kernel, biased, causal),
        grid=(pairs,),
        in_specs=first_specs
        + [
            pair_spec(len_q, query[1] * pairs),
            pair_spec(len_k, keys[1] * pairs),
            pair_spec(len_k, values[1] * pairs),
            pair_spec(len_q, 0),
            row_spec(len_q),
        ],
        out_specs=[pair_spec(len_q, 0), pair_spec(len_k, 0), pair_spec(len_k, 0)]
        + ([row_spec(6 * LANES)] if biased else []),
        out_shape=[
            jax.ShapeDtypeStruct((len_q, D), low),
            jax.ShapeDtypeStruct((len_k, D), low),
            jax.ShapeDtypeStruct((len_k, D), low),
        ]
        + ([jax.ShapeDtypeStruct((HEADS, 1, 6 * LANES), jnp.float32)] if biased else []),
        scratch_shapes=[
            pltpu.VMEM((len_k, LANES), jnp.float32),
            pltpu.VMEM((len_k, LANES), jnp.float32),
        ]
        + (
            [
                pltpu.VMEM((2, LANES, 4 * LANES), jnp.float32),
                pltpu.VMEM((2, LANES, 2 * LANES), jnp.float32),
            ]
            if biased
            else []
        ),
        compiler_params=params(),
        cost_estimate=attend_cost(len_q, len_k, 5),
    )(*first, query[0], keys[0], values[0], d_mixed, logsum)


gelu_scale = math.sqrt(2.0 / math.pi)
gelu_cube = 0.044715


def side_by_side(ref):
    return jnp.concatenate([ref[j, 0] for j in range(ref.shape[0])], axis=1)


def expert_kernel(x_ref, wi_ref, wo_ref, pre_ref, out_ref, acc_ref):
    block = pl.program_id(0)
    pre = dot_nn(x_ref[...], side_by_side(wi_ref))
    pre_ref[0] = pre
    bend = jnp.tanh(gelu_scale * (pre + gelu_cube * (pre * pre * pre)))
    hidden = (0.5 * pre * (1.0 + bend)).astype(jnp.bfloat16)
    part = dot_nt(hidden, side_by_side(wo_ref))

    @pl.when(block == 0)
    def _():
        acc_ref[...] = part

    @pl.when(block > 0)
    def _():
        acc_ref[...] += part

    @pl.when(block == pl.num_programs(0) - 1)
    def _():
        out_ref[...] = acc_ref[...].astype(jnp.bfloat16)


def expert_forward(arrived, weights):
    rows = arrived.shape[0]
    blocks, unused, unused_too, cols = weights.shape
    per = WIDE // cols
    whole = pl.BlockSpec((rows, D), lambda j: (0, 0))
    return pl.pallas_call(
        expert_kernel,
        grid=(blocks // per,),
        in_specs=[
            whole,
            pl.BlockSpec((per, 1, D, cols), lambda j: (j, 0, 0, 0)),
            pl.BlockSpec((per, 1, D, cols), lambda j: (j, 1, 0, 0)),
        ],
        out_specs=[pl.BlockSpec((1, rows, WIDE), lambda j: (j, 0, 0)), whole],
        out_shape=[
            jax.ShapeDtypeStruct((blocks // per, rows, WIDE), jnp.float32),
            jax.ShapeDtypeStruct((rows, D), jnp.bfloat16),
        ],
        scratch_shapes=[pltpu.VMEM((rows, D), jnp.float32)],
        compiler_params=params(),
        cost_estimate=pl.CostEstimate(
            flops=4 * rows * D * FF,
            bytes_accessed=4 * D * FF + 4 * rows * (FF + D),
            transcendentals=rows * FF,
        ),
    )(arrived, weights, weights)


def expert_back_kernel(x_ref, g_ref, pre_ref, wi_ref, wo_ref, dw_ref, back_ref, acc_ref):
    block = pl.program_id(0)
    arrived = x_ref[...]
    grads = g_ref[...]
    pre = pre_ref[0]
    square = pre * pre
    bend = jnp.tanh(gelu_scale * (pre + gelu_cube * (square * pre)))
    half = 0.5 * (1.0 + bend)
    hidden = (pre * half).astype(jnp.bfloat16)
    slope = half + 0.5 * pre * (1.0 - bend * bend) * (
        gelu_scale * (1.0 + 3.0 * gelu_cube * square)
    )
    d_pre = (dot_nn(grads, side_by_side(wo_ref)) * slope).astype(jnp.bfloat16)
    d_in = dot_tn(arrived, d_pre).astype(jnp.bfloat16)
    d_out = dot_tn(grads, hidden).astype(jnp.bfloat16)
    cols = dw_ref.shape[3]
    for j in range(dw_ref.shape[0]):
        dw_ref[j, 0] = d_in[:, cols * j : cols * j + cols]
        dw_ref[j, 1] = d_out[:, cols * j : cols * j + cols]
    part = dot_nt(d_pre, side_by_side(wi_ref))

    @pl.when(block == 0)
    def _():
        acc_ref[...] = part

    @pl.when(block > 0)
    def _():
        acc_ref[...] += part

    @pl.when(block == pl.num_programs(0) - 1)
    def _():
        back_ref[...] = acc_ref[...].astype(jnp.bfloat16)


def expert_backward(arrived, d_arrived, pre, weights):
    rows = arrived.shape[0]
    blocks, unused, unused_too, cols = weights.shape
    per = WIDE // cols
    whole = pl.BlockSpec((rows, D), lambda j: (0, 0))
    return pl.pallas_call(
        expert_back_kernel,
        grid=(blocks // per,),
        in_specs=[
            whole,
            whole,
            pl.BlockSpec((1, rows, WIDE), lambda j: (j, 0, 0)),
            pl.BlockSpec((per, 1, D, cols), lambda j: (j, 0, 0, 0)),
            pl.BlockSpec((per, 1, D, cols), lambda j: (j, 1, 0, 0)),
        ],
        out_specs=[pl.BlockSpec((per, 2, D, cols), lambda j: (j, 0, 0, 0)), whole],
        out_shape=[
            jax.ShapeDtypeStruct((blocks, 2, D, cols), jnp.bfloat16),
            jax.ShapeDtypeStruct((rows, D), jnp.bfloat16),
        ],
        scratch_shapes=[pltpu.VMEM((rows, D), jnp.float32)],
        compiler_params=params(),
        cost_estimate=pl.CostEstimate(
            flops=8 * rows * D * FF,
            bytes_accessed=8 * D * FF + 4 * rows * (FF + 2 * D),
            transcendentals=rows * FF,
        ),
    )(arrived, d_arrived, pre, weights, weights)


def mirror(left, right, store):
    tile = 2 * LANES
    for a in range(0, D, tile):
        block = dot_nt(left[a : a + tile, :], right[: a + tile, :])
        store(slice(a, a + tile), slice(0, a + tile), block)
        if a:
            store(slice(0, a), slice(a, a + tile), block[:, :a].T)


def newton_gram(source, gram_ref):
    def keep(rows, columns, block):
        gram_ref[rows, columns] = block

    mirror(source, source, keep)


def newton_poly(product, poly_ref):
    def keep(rows, columns, block):
        poly_ref[rows, columns] = (
            coef_b * product[rows, columns].astype(jnp.float32) + coef_c * block
        ).astype(jnp.bfloat16)

    mirror(product, product, keep)


def newton_apply(source, poly_ref, j, outer):
    part = source[:, D * j : D * j + D]
    fresh = coef_a * part.astype(jnp.float32) + dot_nn(poly_ref[...], part)
    if outer is not None:
        fresh = fresh * outer
    source[:, D * j : D * j + D] = fresh.astype(jnp.bfloat16)


def newton_rounds(source, gram_ref, poly_ref, between, finish):
    blocks = source.shape[1] // D
    newton_gram(source, gram_ref)
    row = lax.broadcasted_iota(jnp.int32, (D, D), 0)
    column = lax.broadcasted_iota(jnp.int32, (D, D), 1)
    whole = gram_ref[...].astype(jnp.bfloat16).astype(jnp.float32)
    scale = jnp.sum(jnp.where(row == column, whole, 0.0), keepdims=True) + eps_gram
    newton_poly((whole * (1.0 / scale)).astype(jnp.bfloat16), poly_ref)
    for j in range(blocks):
        newton_apply(source, poly_ref, j, lax.rsqrt(scale))

    def turn(index, carry):
        newton_gram(source, gram_ref)
        newton_poly(gram_ref[...].astype(jnp.bfloat16), poly_ref)
        for j in range(blocks):
            newton_apply(source, poly_ref, j, None)
        return carry

    lax.fori_loop(1, NS_ITERS - 1, turn, 0)
    between()
    newton_gram(source, gram_ref)
    newton_poly(gram_ref[...].astype(jnp.bfloat16), poly_ref)
    for j in range(blocks):
        newton_apply(source, poly_ref, j, None)
        finish(j)


def newton_kernel(
    groups,
    experts,
    expert_ref,
    dense_ref,
    expert_out,
    dense_out,
    moment_out,
    held,
    held_dense,
    matrix,
    square,
    gram_ref,
    poly_ref,
    land_expert,
    land_dense,
    all_dense,
    all_moment,
    send_sem,
    in_sem,
    back_send_sem,
    back_sem,
    orth_send_sem,
    orth_sem,
    moment_send_sem,
    moment_sem,
):
    me = lax.axis_index("mp")
    along = lax.axis_index("dp")
    own = me // 2
    count_expert, count_dense = expert_ref.shape[0], dense_ref.shape[0]
    cols, cols_dense = expert_ref.shape[2], dense_ref.shape[1]
    is_expert = ((me % 2) == 0) & (own < count_expert)
    is_dense = ((me % 2) == 1) & (own < count_dense)
    per = D // cols
    barrier = pltpu.get_barrier_semaphore()
    for step in range(1, groups):
        other = lax.rem(me + step, groups)
        pl.semaphore_signal(
            barrier, inc=1, device_id={"mp": other}, device_id_type=pl.DeviceIdType.MESH
        )
    for step in range(1, experts):
        other = lax.rem(along + step, experts)
        pl.semaphore_signal(
            barrier, inc=1, device_id={"dp": other}, device_id_type=pl.DeviceIdType.MESH
        )
    pl.semaphore_wait(barrier, groups + experts - 2)

    def remote(source, target, sent, landed, device):
        return pltpu.make_async_remote_copy(
            src_ref=source,
            dst_ref=target,
            send_sem=sent,
            recv_sem=landed,
            device_id={"mp": device},
            device_id_type=pl.DeviceIdType.MESH,
        )

    def outward(index, source):
        dense = index >= count_expert
        place = index - count_expert if dense else index
        held_ref = held_dense if dense else held
        own_ref = dense_ref if dense else expert_ref
        return remote(
            own_ref.at[place],
            held_ref.at[source],
            send_sem.at[index],
            in_sem.at[source],
            2 * place + (1 if dense else 0),
        )

    def sideways(step, source, orth):
        return pltpu.make_async_remote_copy(
            src_ref=land_dense if orth else dense_ref,
            dst_ref=(all_dense if orth else all_moment).at[source],
            send_sem=(orth_send_sem if orth else moment_send_sem).at[step],
            recv_sem=(orth_sem if orth else moment_sem).at[source],
            device_id={"dp": lax.rem(along + step, experts)},
            device_id_type=pl.DeviceIdType.MESH,
        )

    total = count_expert + count_dense
    owners = [2 * e for e in range(count_expert)] + [2 * d + 1 for d in range(count_dense)]
    for index in range(total):

        @pl.when(me != owners[index])
        def _(index=index):
            outward(index, me).start()

    for step in range(1, experts):
        sideways(step, along, False).start()

    for step in range(1, groups):
        source = lax.rem(me + step, groups)

        @pl.when(is_expert)
        def _(source=source):
            outward(0, source).wait_recv()

        @pl.when(is_dense)
        def _(source=source):
            outward(count_expert, source).wait_recv()

    for index in range(total):

        @pl.when(me != owners[index])
        def _(index=index):
            outward(index, me).wait_send()

    def backward_expert(target):
        return remote(
            held.at[target],
            land_expert.at[own],
            back_send_sem.at[target],
            back_sem.at[own],
            target,
        )

    def backward_dense(target):
        return remote(
            held_dense.at[target],
            land_dense.at[own],
            back_send_sem.at[target],
            back_sem.at[count_expert + own],
            target,
        )

    def share_dense():
        for index in range(count_expert, total):

            @pl.when(me != owners[index])
            def _(index=index):
                landing = land_dense.at[index - count_expert]
                remote(
                    landing, landing, send_sem.at[index], back_sem.at[index], owners[index]
                ).wait_recv()

        for step in range(1, experts):
            sideways(step, along, True).start()

    def nothing():
        return None

    @pl.when(is_expert)
    def _():
        held[me] = expert_ref[own]
        for j in range(groups // per):
            matrix[:, D * j : D * j + D] = jnp.concatenate(
                [held[per * j + inner] for inner in range(per)], axis=1
            )

        def finish(j):
            for inner in range(per):
                target = per * j + inner
                held[target] = matrix[:, cols * target : cols * target + cols]

                @pl.when(me != target)
                def _(target=target):
                    backward_expert(target).start()

        newton_rounds(matrix, gram_ref, poly_ref, share_dense, finish)
        land_expert[own] = held[me]
        for target in range(groups):

            @pl.when(me != target)
            def _(target=target):
                backward_expert(target).wait_send()

    @pl.when(is_dense)
    def _():
        held_dense[me] = dense_ref[own]
        for source in range(groups):
            square[cols_dense * source : cols_dense * source + cols_dense, :] = held_dense[source]

        def finish(j):
            for target in range(groups):
                held_dense[target] = square[
                    cols_dense * target : cols_dense * target + cols_dense, :
                ]

                @pl.when(me != target)
                def _(target=target):
                    backward_dense(target).start()

        newton_rounds(square, gram_ref, poly_ref, nothing, finish)
        land_dense[own] = held_dense[me]
        share_dense()
        for target in range(groups):

            @pl.when(me != target)
            def _(target=target):
                backward_dense(target).wait_send()

    @pl.when(jnp.logical_not(is_expert | is_dense))
    def _():
        share_dense()

    for index in range(count_expert):

        @pl.when(me != owners[index])
        def _(index=index):
            landing = land_expert.at[index]
            remote(
                landing, landing, send_sem.at[index], back_sem.at[index], owners[index]
            ).wait_recv()

    all_dense[along] = land_dense[...]
    all_moment[along] = dense_ref[...]
    for step in range(1, experts):
        sideways(step, lax.rem(along + step, experts), True).wait_recv()
        sideways(step, lax.rem(along + step, experts), False).wait_recv()
        sideways(step, along, True).wait_send()
        sideways(step, along, False).wait_send()
    expert_out[...] = land_expert[...]
    dense_out[...] = all_dense[...]
    moment_out[...] = all_moment[...]


def newton(dense_mom, expert_mom, groups, experts):
    cols, cols_dense = expert_mom.shape[2], dense_mom.shape[1]
    count_expert, count_dense = expert_mom.shape[0], dense_mom.shape[0]
    low = jnp.bfloat16
    vmem = pl.BlockSpec(memory_space=pltpu.VMEM)
    dma = pltpu.SemaphoreType.DMA
    return pl.pallas_call(
        partial(newton_kernel, groups, experts),
        in_specs=[vmem, vmem],
        out_specs=[vmem, vmem, vmem],
        out_shape=[
            jax.ShapeDtypeStruct(expert_mom.shape, low),
            jax.ShapeDtypeStruct((experts,) + dense_mom.shape, low),
            jax.ShapeDtypeStruct((experts,) + dense_mom.shape, low),
        ],
        scratch_shapes=[
            pltpu.VMEM((groups, D, cols), low),
            pltpu.VMEM((groups, cols_dense, D), low),
            pltpu.VMEM((D, groups * cols), low),
            pltpu.VMEM((D, D), low),
            pltpu.VMEM((D, D), jnp.float32),
            pltpu.VMEM((D, D), low),
            pltpu.VMEM(expert_mom.shape, low),
            pltpu.VMEM(dense_mom.shape, low),
            pltpu.VMEM((experts,) + dense_mom.shape, low),
            pltpu.VMEM((experts,) + dense_mom.shape, low),
            dma((count_expert + count_dense,)),
            dma((groups,)),
            dma((groups,)),
            dma((count_expert + count_dense,)),
            dma((experts,)),
            dma((experts,)),
            dma((experts,)),
            dma((experts,)),
        ],
        compiler_params=pltpu.CompilerParams(
            vmem_limit_bytes=VMEM_LIMIT, collective_id=1, has_side_effects=True
        ),
        cost_estimate=pl.CostEstimate(
            flops=NS_ITERS * (4 * D * D * FF + 2 * D * D * D),
            bytes_accessed=40 * D * FF,
            transcendentals=0,
        ),
    )(expert_mom.astype(low), dense_mom.astype(low))


def total_kernel(
    groups, experts, x_ref, out_ref, land_row, land_col, send_sem, row_sem, send_col_sem, col_sem
):
    across, along = lax.axis_index("mp"), lax.axis_index("dp")
    barrier = pltpu.get_barrier_semaphore()
    mesh_id = pl.DeviceIdType.MESH
    for step in range(1, groups):
        other = lax.rem(across + step, groups)
        pl.semaphore_signal(barrier, inc=1, device_id={"mp": other}, device_id_type=mesh_id)
    for step in range(1, experts):
        other = lax.rem(along + step, experts)
        pl.semaphore_signal(barrier, inc=1, device_id={"dp": other}, device_id_type=mesh_id)
    pl.semaphore_wait(barrier, groups + experts - 2)

    def to_row(step, source):
        return pltpu.make_async_remote_copy(
            src_ref=x_ref,
            dst_ref=land_row.at[source],
            send_sem=send_sem.at[step],
            recv_sem=row_sem.at[source],
            device_id={"mp": lax.rem(across + step, groups)},
            device_id_type=mesh_id,
        )

    def to_col(step, source):
        return pltpu.make_async_remote_copy(
            src_ref=out_ref,
            dst_ref=land_col.at[source],
            send_sem=send_col_sem.at[step],
            recv_sem=col_sem.at[source],
            device_id={"dp": lax.rem(along + step, experts)},
            device_id_type=mesh_id,
        )

    for step in range(1, groups):
        to_row(step, across).start()
    land_row[across] = x_ref[...]
    for step in range(1, groups):
        to_row(step, lax.rem(across + step, groups)).wait_recv()
    total = land_row[0]
    for source in range(1, groups):
        total = total + land_row[source]
    out_ref[...] = total
    for step in range(1, experts):
        to_col(step, along).start()
    land_col[along] = total
    for step in range(1, experts):
        to_col(step, lax.rem(along + step, experts)).wait_recv()
    for step in range(1, groups):
        to_row(step, across).wait_send()
    for step in range(1, experts):
        to_col(step, along).wait_send()
    total = land_col[0]
    for source in range(1, experts):
        total = total + land_col[source]
    out_ref[...] = total


def total_of(array, groups, experts, collective):
    vmem = pl.BlockSpec(memory_space=pltpu.VMEM)
    dma = pltpu.SemaphoreType.DMA
    return pl.pallas_call(
        partial(total_kernel, groups, experts),
        in_specs=[vmem],
        out_specs=vmem,
        out_shape=jax.ShapeDtypeStruct(array.shape, array.dtype),
        scratch_shapes=[
            pltpu.VMEM((groups,) + array.shape, array.dtype),
            pltpu.VMEM((experts,) + array.shape, array.dtype),
            dma((groups,)),
            dma((groups,)),
            dma((experts,)),
            dma((experts,)),
        ],
        compiler_params=pltpu.CompilerParams(
            vmem_limit_bytes=16 * 1024 * 1024, collective_id=collective, has_side_effects=True
        ),
        cost_estimate=pl.CostEstimate(
            flops=0, bytes_accessed=30000000, transcendentals=0
        ),
    )(array)


def lookup_kernel(vocab, wanted_ref, table_ref, out_ref, acc_ref):
    block = pl.program_id(0)
    height = table_ref.shape[0]
    place = lax.broadcasted_iota(jnp.int32, (wanted_ref.shape[0], height), 1) + block * height
    pick = (wanted_ref[...] == place).astype(jnp.bfloat16)
    row = lax.broadcasted_iota(jnp.int32, table_ref.shape, 0) + block * height
    table = jnp.where(row < vocab, table_ref[...], 0.0).astype(jnp.bfloat16)
    part = dot_nn(pick, table)

    @pl.when(block == 0)
    def _():
        acc_ref[...] = part

    @pl.when(block > 0)
    def _():
        acc_ref[...] += part

    @pl.when(block == pl.num_programs(0) - 1)
    def _():
        out_ref[...] = acc_ref[...].astype(jnp.bfloat16)


def lookup(wanted, table):
    count = wanted.shape[0]
    vocab = table.shape[0]
    height = 1024
    whole = pl.BlockSpec((count, D), lambda j: (0, 0))
    return pl.pallas_call(
        partial(lookup_kernel, vocab),
        grid=(-(-vocab // height),),
        in_specs=[
            pl.BlockSpec((count, 1), lambda j: (0, 0)),
            pl.BlockSpec((height, D), lambda j: (j, 0)),
        ],
        out_specs=whole,
        out_shape=jax.ShapeDtypeStruct((count, D), jnp.bfloat16),
        scratch_shapes=[pltpu.VMEM((count, D), jnp.float32)],
        compiler_params=params(),
        cost_estimate=pl.CostEstimate(
            flops=2 * count * vocab * D, bytes_accessed=4 * vocab * D, transcendentals=0
        ),
    )(wanted[:, None], table)


def dense_kernel(
    groups,
    experts,
    enc_ref,
    dec_ref,
    out_ref,
    land,
    summed,
    land_enc,
    land_dec,
    send_sem,
    land_sem,
    enc_send_sem,
    enc_sem,
    dec_send_sem,
    dec_sem,
):
    across, along = lax.axis_index("mp"), lax.axis_index("dp")
    count = enc_ref.shape[1]
    per_enc, per_dec = land_enc.shape[1], land_dec.shape[1]
    barrier = pltpu.get_barrier_semaphore()
    mesh_id = pl.DeviceIdType.MESH
    for step in range(1, groups):
        other = lax.rem(across + step, groups)
        pl.semaphore_signal(barrier, inc=1, device_id={"mp": other}, device_id_type=mesh_id)
    for step in range(1, experts):
        other = lax.rem(along + step, experts)
        pl.semaphore_signal(barrier, inc=1, device_id={"dp": other}, device_id_type=mesh_id)
    pl.semaphore_wait(barrier, groups + experts - 2)

    def to_row(step, source):
        other = lax.rem(across + step, groups)
        return pltpu.make_async_remote_copy(
            src_ref=enc_ref.at[other],
            dst_ref=land.at[source],
            send_sem=send_sem.at[step],
            recv_sem=land_sem.at[source],
            device_id={"mp": other},
            device_id_type=mesh_id,
        )

    def to_col(step, source, dec):
        other = lax.rem(along + step, experts)
        per = per_dec if dec else per_enc
        return pltpu.make_async_remote_copy(
            src_ref=(dec_ref if dec else summed).at[pl.ds(other * per, per)],
            dst_ref=(land_dec if dec else land_enc).at[source],
            send_sem=(dec_send_sem if dec else enc_send_sem).at[step],
            recv_sem=(dec_sem if dec else enc_sem).at[source],
            device_id={"dp": other},
            device_id_type=mesh_id,
        )

    for step in range(1, groups):
        to_row(step, across).start()
    for step in range(1, experts):
        to_col(step, along, True).start()
    land[across] = enc_ref[across]
    land_dec[along] = dec_ref[pl.ds(along * per_dec, per_dec)]
    for step in range(1, groups):
        to_row(step, lax.rem(across + step, groups)).wait_recv()

    for index in range(count):
        total = land[0, index].astype(jnp.float32)
        for source in range(1, groups):
            total = total + land[source, index].astype(jnp.float32)
        summed[index] = total.astype(jnp.bfloat16)
    for index in range(count, summed.shape[0]):
        summed[index] = jnp.zeros(summed.shape[1:], jnp.bfloat16)
    for step in range(1, experts):
        to_col(step, along, False).start()
    land_enc[along] = summed[pl.ds(along * per_enc, per_enc)]
    for step in range(1, groups):
        to_row(step, across).wait_send()
    for step in range(1, experts):
        source = lax.rem(along + step, experts)
        to_col(step, source, True).wait_recv()
        to_col(step, source, False).wait_recv()
        to_col(step, along, True).wait_send()
        to_col(step, along, False).wait_send()
    for landed, per, first in ((land_enc, per_enc, 0), (land_dec, per_dec, per_enc)):
        for index in range(per):
            total = landed[0, index].astype(jnp.float32)
            for source in range(1, experts):
                total = total + landed[source, index].astype(jnp.float32)
            out_ref[first + index] = total


def dense_total(enc, dec, groups, experts):
    count, cols = enc.shape[1], enc.shape[2]
    per_enc, per_dec = -(-count // experts), -(-dec.shape[0] // experts)
    dec = jnp.pad(dec, ((0, per_dec * experts - dec.shape[0]), (0, 0), (0, 0)))
    vmem = pl.BlockSpec(memory_space=pltpu.VMEM)
    dma = pltpu.SemaphoreType.DMA
    low = jnp.bfloat16
    return pl.pallas_call(
        partial(dense_kernel, groups, experts),
        in_specs=[vmem, vmem],
        out_specs=vmem,
        out_shape=jax.ShapeDtypeStruct((per_enc + per_dec, cols, D), jnp.float32),
        scratch_shapes=[
            pltpu.VMEM(enc.shape, low),
            pltpu.VMEM((per_enc * experts, cols, D), low),
            pltpu.VMEM((experts, per_enc, cols, D), low),
            pltpu.VMEM((experts, per_dec, cols, D), low),
            dma((groups,)),
            dma((groups,)),
            dma((experts,)),
            dma((experts,)),
            dma((experts,)),
            dma((experts,)),
        ],
        compiler_params=pltpu.CompilerParams(
            vmem_limit_bytes=VMEM_LIMIT, collective_id=4, has_side_effects=True
        ),
        cost_estimate=pl.CostEstimate(
            flops=0, bytes_accessed=200000000, transcendentals=0
        ),
    )(enc, dec)


def piece_of(array, count, experts):
    along = lax.axis_index("dp")
    pieces = []
    for part in (array[:count], array[count:]):
        per = -(-part.shape[0] // experts)
        spare = per * experts - part.shape[0]
        part = jnp.pad(part, ((0, spare),) + ((0, 0),) * (part.ndim - 1))
        pieces.append(lax.dynamic_slice_in_dim(part, along * per, per, 0))
    return jnp.concatenate(pieces, axis=0)


def whole_of(pieces, count, rest):
    per = -(-count // pieces.shape[0])
    first = pieces[:, :per].reshape((-1,) + pieces.shape[2:])[:count]
    second = pieces[:, per:].reshape((-1,) + pieces.shape[2:])[:rest]
    return jnp.concatenate([first, second], axis=0)


def project(rows, stored):
    flat = stored.reshape(-1, D)
    return dot_nt(rows, flat)


def swap_owners(buffer):
    return lax.all_to_all(buffer, "dp", split_axis=0, concat_axis=0, tiled=True)


def dispatch(places, count):
    slot = lax.broadcasted_iota(jnp.int32, (count, places.shape[0]), 0)
    return (slot == places[None, :]).astype(jnp.bfloat16)


def route_places(routes, experts, cap):
    hot = (routes[:, None] == jnp.arange(experts, dtype=jnp.int32)[None, :]).astype(jnp.float32)
    rows = routes.shape[0]
    earlier = (
        lax.broadcasted_iota(jnp.int32, (rows, rows), 1)
        < lax.broadcasted_iota(jnp.int32, (rows, rows), 0)
    ).astype(jnp.bfloat16)
    ranks = dot_nn(earlier, hot.astype(jnp.bfloat16))
    slots = jnp.sum(hot * ranks, axis=1).astype(jnp.int32)
    return hot, routes * cap + slots


def moe_send(resid, gain, router, hot, places, cap):
    experts = router.shape[1]
    normed, inverse = normalize(resid, gain)
    normed_low = normed.astype(jnp.bfloat16)
    buffer = dot_nn(dispatch(places, experts * cap), normed_low).astype(jnp.bfloat16)
    arrived = swap_owners(buffer.reshape(experts, cap, D)).reshape(-1, D)
    probs = jax.nn.softmax(
        jnp.dot(normed_low.astype(jnp.float32), router, precision=highest), axis=-1
    )
    gate = jnp.sum(probs * hot, axis=1)
    return arrived, (normed_low, inverse, probs, gate)


def moe_expert(weights, cap, arrived):
    pre, result = expert_forward(arrived, weights)
    return pre, swap_owners(result.reshape(-1, cap, D)).reshape(-1, D)


def moe_receive(resid, places, arrived, pre, returned, sent):
    outputs = dot_tn(dispatch(places, returned.shape[0]), returned)
    return (resid + sent[3][:, None] * outputs, sent + (arrived, pre, outputs))


def moe_back_send(places, cap, kept, grad):
    normed_low, inverse, probs, gate, arrived, pre, outputs = kept
    experts = arrived.shape[0] // cap
    d_rows = (gate[:, None] * grad).astype(jnp.bfloat16)
    buffer = dot_nn(dispatch(places, experts * cap), d_rows).astype(jnp.bfloat16)
    return swap_owners(buffer.reshape(experts, cap, D)).reshape(-1, D)


def moe_back_expert(weights, cap, kept, d_arrived):
    normed_low, inverse, probs, gate, arrived, pre, outputs = kept
    experts = arrived.shape[0] // cap
    d_weights, d_back = expert_backward(arrived, d_arrived, pre, weights)
    return d_weights, swap_owners(d_back.reshape(experts, cap, D)).reshape(-1, D)


def moe_back_receive(resid, gain, router, hot, places, kept, grad, returned, aux_scale, frac):
    normed_low, inverse, probs, gate, arrived, pre, outputs = kept
    d_gate = jnp.sum(grad * outputs, axis=1)
    d_probs = hot * d_gate[:, None] + aux_scale * frac[None, :]
    d_logits = probs * (d_probs - jnp.sum(probs * d_probs, axis=-1, keepdims=True))
    d_router = jnp.dot(normed_low.astype(jnp.float32).T, d_logits, precision=highest)
    d_normed = dot_tn(dispatch(places, returned.shape[0]), returned) + jnp.dot(
        d_logits, router.T, precision=highest
    )
    d_resid, d_gain = normalize_back(resid, inverse, gain, d_normed)
    return (grad + d_resid, d_gain, d_router)


def ranks_of(ids, size):
    count = ids.shape[0]
    here, there = ids[:, None], ids[None, :]
    before = lax.broadcasted_iota(jnp.int32, (count, count), 1) < lax.broadcasted_iota(
        jnp.int32, (count, count), 0
    )
    again = jnp.max(((here == there) & before).astype(jnp.int32), axis=1)
    owner = ids // size
    lower = (there < here) & (there >= (owner * size)[:, None]) & (again[None, :] == 0)
    return owner, jnp.sum(lower.astype(jnp.int32), axis=1)


def slots_of(owner, rank, owners, width, turn):
    slot = owner * width + rank - turn * width
    slot = jnp.where((rank >= turn * width) & (rank < (turn + 1) * width), slot, -1)
    return lax.broadcasted_iota(jnp.int32, (owners * width, rank.shape[0]), 0) == slot[None, :]


def ids_in(hot, local, width):
    return jnp.max(jnp.where(hot, local[None, :], -1), axis=1).reshape(-1, width)


def exchange(array, axes):
    return lax.all_to_all(array, axes, split_axis=0, concat_axis=0, tiled=True)


def rows_into(landed, rows, count):
    place = landed[None, :] == lax.broadcasted_iota(jnp.int32, (count, landed.shape[0]), 0)
    return dot_nn(place.astype(jnp.bfloat16), rows)


def in_lanes(parts):
    flat = jnp.concatenate([part.reshape(-1) for part in parts])
    rows = -(-flat.shape[0] // (8 * LANES)) * 8
    return jnp.pad(flat, (0, rows * LANES - flat.shape[0])).reshape(rows, LANES)


def from_lanes(array, parts):
    flat = array.reshape(-1)
    taken, out = 0, []
    for part in parts:
        out.append(flat[taken : taken + part.size].reshape(part.shape))
        taken += part.size
    return out


def self_forward(resid, gain, weights, parts, causal):
    normed, inverse = normalize(resid, gain)
    normed = normed.astype(jnp.bfloat16)
    joined = project(normed, weights[0:3]).astype(jnp.bfloat16)
    mixed, logsum = attend((joined, 0), (joined, 1), (joined, 2), parts, causal)
    return (resid + project(mixed, weights[3]), (resid, inverse, normed, joined, mixed, logsum))


def self_backward(gain, weights, parts, causal, kept, grad):
    resid, inverse, normed, joined, mixed, logsum = kept
    grad_low = grad.astype(jnp.bfloat16)
    d_mixed = dot_nn(grad_low, weights[3]).astype(jnp.bfloat16)
    d_query, d_key, d_value, sums = attend_back(
        (joined, 0), (joined, 1), (joined, 2), parts, causal, logsum, d_mixed
    )
    d_normed = (
        dot_nn(d_query, weights[0]) + dot_nn(d_key, weights[1]) + dot_nn(d_value, weights[2])
    )
    d_weights = [
        dot_tn(d_query, normed),
        dot_tn(d_key, normed),
        dot_tn(d_value, normed),
        dot_tn(grad_low, mixed),
    ]
    d_resid, d_gain = normalize_back(resid, inverse, gain, d_normed)
    return (grad + d_resid, d_gain, d_weights, bias_sums(sums, parts[2], parts[3]))


def cross_forward(resid, gain, weights, memory):
    normed, inverse = normalize(resid, gain)
    normed = normed.astype(jnp.bfloat16)
    query = project(normed, weights[0]).astype(jnp.bfloat16)
    joined = project(memory, weights[1:3]).astype(jnp.bfloat16)
    mixed, logsum = attend((query, 0), (joined, 0), (joined, 1), None, False)
    kept = (resid, inverse, normed, query, joined, mixed, logsum)
    return (resid + project(mixed, weights[3]), kept)


def cross_backward(gain, weights, memory, kept, grad):
    resid, inverse, normed, query, joined, mixed, logsum = kept
    grad_low = grad.astype(jnp.bfloat16)
    d_mixed = dot_nn(grad_low, weights[3]).astype(jnp.bfloat16)
    d_query, d_key, d_value = attend_back(
        (query, 0), (joined, 0), (joined, 1), None, False, logsum, d_mixed
    )
    d_normed = dot_nn(d_query, weights[0])
    d_memory = dot_nn(d_key, weights[1]) + dot_nn(d_value, weights[2])
    d_weights = [
        dot_tn(d_query, normed),
        dot_tn(d_key, memory),
        dot_tn(d_value, memory),
        dot_tn(grad_low, mixed),
    ]
    d_resid, d_gain = normalize_back(resid, inverse, gain, d_normed)
    return (grad + d_resid, d_gain, d_weights, d_memory)


def route_share(routes, experts):
    flat_routes = routes.reshape(-1)
    hot = (flat_routes[None, :] == jnp.arange(experts, dtype=jnp.int32)[:, None]).astype(
        jnp.float32
    )
    return jnp.sum(hot, axis=1) / flat_routes.shape[0]


def adam(weight, first, second, grad, rate, decay):
    first = beta_one * first + (1 - beta_one) * grad
    second = beta_two * second + (1 - beta_two) * grad * grad
    update = first / (1 - beta_one**STEP) / (jnp.sqrt(second / (1 - beta_two**STEP)) + eps_adam)
    return (weight - rate * (update + decay * weight), first, second)


def share_columns(d_weights, groups):
    split = jnp.concatenate(
        [part.astype(jnp.bfloat16).reshape(groups, -1, D) for part in d_weights], axis=1
    )
    summed = lax.psum_scatter(split.reshape(-1, D), "mp", scatter_dimension=0, tiled=True)
    return summed.reshape(len(d_weights), -1, D)


def on_device(
    src_ids,
    targets,
    loss_pos,
    loss_mask,
    routes_src,
    routes_tgt,
    dense_w,
    dense_m,
    expert_w,
    expert_m,
    table_w,
    table_m,
    table_v,
    gains_w,
    gains_m,
    gains_v,
    router_w,
    router_m,
    router_v,
    bias_w,
    bias_m,
    bias_v,
):
    groups = lax.axis_size("mp")
    column = lax.axis_index("mp")
    experts = lax.axis_size("dp")
    src_len = src_ids.shape[1]
    tgt_len = targets.shape[1]
    npos = loss_pos.shape[1]
    vocab_dev = table_w.shape[0]
    own_seq = lax.axis_index("dp") * groups + column
    count_dense = dense_w.shape[0]
    low = jnp.bfloat16
    dense_local = dense_w.astype(low).reshape(count_dense, -1, D)
    enc_dense = lax.all_gather(dense_local[0:4], "mp", axis=1, tiled=True)
    expert_local = expert_w[:, :, 0].astype(low)
    devices = experts * groups
    piece_rows = table_m.shape[0]
    own_src_ids = lax.dynamic_slice_in_dim(src_ids, column, 1, 0).reshape(-1)
    own_targets = lax.dynamic_slice_in_dim(targets, column, 1, 0).reshape(-1)
    own_ids = jnp.concatenate([own_src_ids, jnp.zeros((1,), jnp.int32), own_targets[:-1]])
    shard, rank = ranks_of(own_ids, vocab_dev)
    owner, owner_rank = ranks_of(own_ids, piece_rows)
    local_ids = own_ids - shard * vocab_dev
    piece_ids = own_ids - owner * piece_rows
    owner = (owner % experts) * groups + owner // experts
    needs = jnp.stack([jnp.max(rank) // FETCH + 1, jnp.max(owner_rank) // GIVE + 1])

    def asked_of(turn):
        return ids_in(slots_of(shard, rank, groups, FETCH, turn), local_ids, FETCH)

    def fetched(turn, wanted):
        rows = lookup(wanted.reshape(-1), table_w)
        rows = exchange(rows.reshape(groups, FETCH, D), "mp")
        hot = slots_of(shard, rank, groups, FETCH, turn).astype(low)
        return dot_tn(hot, rows.reshape(-1, D))

    noted = jnp.broadcast_to(jnp.pad(needs, (0, LANES - 2))[None, :], (groups, LANES))
    asked = exchange(jnp.concatenate([asked_of(0), noted], axis=1), "mp")
    needs = jnp.max(asked[:, FETCH:], axis=0, keepdims=True)
    embedded = fetched(0, asked[:, :FETCH])
    embedded, enc_dense = lax.optimization_barrier((embedded, enc_dense))
    needs = jnp.max(lax.all_gather(jnp.tile(needs, (8, 1)), "dp", axis=0, tiled=True), axis=0)

    def fetch_more(state):
        turn, rows = state
        return turn + 1, rows + fetched(turn, exchange(asked_of(turn), "mp"))

    turns, embedded = lax.while_loop(
        lambda state: state[0] < needs[0], fetch_more, (jnp.int32(1), embedded)
    )
    enc_expert = lax.all_gather(expert_local[0], "mp", axis=0, tiled=False)
    own_src = lax.dynamic_slice_in_dim(routes_src, own_seq, 1, 0).reshape(-1)
    own_tgt = lax.dynamic_slice_in_dim(routes_tgt, own_seq, 1, 0).reshape(-1)
    cap_src = (5 * src_len + 4 * experts - 1) // (4 * experts)
    cap_tgt = (5 * tgt_len + 4 * experts - 1) // (4 * experts)
    total_src = routes_src.shape[0] * routes_src.shape[1]
    total_tgt = routes_tgt.shape[0] * routes_tgt.shape[1]
    frac_src = route_share(routes_src, experts)
    frac_tgt = route_share(routes_tgt, experts)
    hot_src, places_src = route_places(own_src, experts, cap_src)
    hot_tgt, places_tgt = route_places(own_tgt, experts, cap_tgt)
    enc_parts = bias_parts(bias_w[0], False)
    dec_parts = bias_parts(bias_w[1], True)
    enc_mid, enc_kept = self_forward(embedded[:src_len], gains_w[0], enc_dense, enc_parts, False)
    dec_local, late_table, enc_mid = lax.optimization_barrier((dense_local[4:8], table_w, enc_mid))
    arrived, enc_sent = moe_send(enc_mid, gains_w[1], router_w[0], hot_src, places_src, cap_src)
    dec_dense = lax.all_gather(dec_local, "mp", axis=1, tiled=True)
    arrived, enc_expert, cross_local, dec_expert_local = lax.optimization_barrier(
        (arrived, enc_expert, dense_local[8:12], expert_local[1])
    )
    cross_dense = lax.all_gather(cross_local, "mp", axis=1, tiled=True)
    dec_expert = lax.all_gather(dec_expert_local, "mp", axis=0, tiled=False)
    table_low = late_table.astype(low)
    pre, returned = moe_expert(enc_expert, cap_src, arrived)
    dec_mid, dec_kept = self_forward(embedded[src_len:], gains_w[3], dec_dense, dec_parts, True)
    returned, dec_mid = lax.optimization_barrier((returned, dec_mid))
    enc_out, enc_moe = moe_receive(enc_mid, places_src, arrived, pre, returned, enc_sent)
    memory_float, memory_inv = normalize(enc_out, gains_w[2])
    memory = memory_float.astype(low)
    dec_crossed, cross_kept = cross_forward(dec_mid, gains_w[4], cross_dense, memory)
    arrived, dec_sent = moe_send(
        dec_crossed, gains_w[5], router_w[1], hot_tgt, places_tgt, cap_tgt
    )
    pre, returned = moe_expert(dec_expert, cap_tgt, arrived)
    dec_result, dec_moe = moe_receive(dec_crossed, places_tgt, arrived, pre, returned, dec_sent)
    final_float, final_inv = normalize(dec_result, gains_w[6])
    final_low = final_float.astype(low)
    head_scale = D ** (-0.5)
    own_pos = lax.dynamic_slice_in_dim(loss_pos, column, 1, 0).reshape(-1)
    pick = (
        own_pos[:, None] == lax.broadcasted_iota(jnp.int32, (npos, tgt_len), 1)
    ).astype(low)
    chosen = dot_nn(pick, final_low).astype(low)
    gathered = lax.all_gather(chosen, "mp", axis=0, tiled=True)
    logits = dot_nt(gathered, table_low) * head_scale
    at_pos = loss_pos[:, :, None] == lax.broadcasted_iota(jnp.int32, (1, 1, tgt_len), 2)
    wanted = jnp.sum(jnp.where(at_pos, targets[:, None, :], 0), axis=2).reshape(-1)
    wanted = wanted - column * vocab_dev
    hits = jnp.arange(vocab_dev, dtype=jnp.int32)[None, :] == wanted[:, None]
    top = jnp.max(logits, axis=1)
    stats = lax.all_gather(
        jnp.stack(
            [
                top,
                jnp.sum(jnp.exp(logits - top[:, None]), axis=1),
                jnp.sum(jnp.where(hits, logits, 0.0), axis=1),
            ]
        ),
        "mp",
        axis=0,
        tiled=False,
    )
    all_top = jnp.max(stats[:, 0], axis=0)
    expsum = jnp.sum(stats[:, 1] * jnp.exp(stats[:, 0] - all_top[None, :]), axis=0)
    picked = jnp.sum(stats[:, 2], axis=0)
    logsum = all_top + jnp.log(expsum)
    mask_rows = loss_mask.reshape(-1).astype(jnp.float32)
    own_loss = jnp.sum(
        lax.dynamic_slice_in_dim(mask_rows * (logsum - picked), column * npos, npos)
    )
    own_count = jnp.sum(lax.dynamic_slice_in_dim(mask_rows, column * npos, npos))
    d_logits = (
        mask_rows[:, None] * (jnp.exp(logits - logsum[:, None]) - hits.astype(jnp.float32))
    ).astype(low)
    d_shares = lax.all_to_all(
        (dot_nn(d_logits, table_low) * head_scale).astype(low).reshape(groups, npos, D),
        "mp",
        split_axis=0,
        concat_axis=0,
        tiled=True,
    )
    d_logits, d_shares = lax.optimization_barrier((d_logits, d_shares))
    table_grad = (dot_tn(d_logits, gathered) * head_scale).astype(low)
    padded = -(-piece_rows // 16) * 16
    table_grad = jnp.pad(
        table_grad.reshape(experts, piece_rows, D), ((0, 0), (0, padded - piece_rows), (0, 0))
    ).reshape(-1, D)
    table_share = lax.psum_scatter(table_grad, "dp", scatter_dimension=0, tiled=True)
    d_chosen = jnp.sum(d_shares.astype(jnp.float32), axis=0).astype(low)
    d_final = dot_tn(pick, d_chosen)
    d_dec, gain_final = normalize_back(dec_result, final_inv, gains_w[6], d_final)
    d_arrived = moe_back_send(places_tgt, cap_tgt, dec_moe, d_dec)
    dec_dw, returned = moe_back_expert(dec_expert, cap_tgt, dec_moe, d_arrived)
    dec_share = lax.psum_scatter(dec_dw, "mp", scatter_dimension=0, tiled=False)
    d_dec, gain_dec_moe, dec_router = moe_back_receive(
        dec_crossed,
        gains_w[5],
        router_w[1],
        hot_tgt,
        places_tgt,
        dec_moe,
        d_dec,
        returned,
        aux_weight * experts / total_tgt,
        frac_tgt,
    )
    d_dec, gain_cross, cross_dw, d_memory = cross_backward(
        gains_w[4], cross_dense, memory, cross_kept, d_dec
    )
    d_enc, gain_memory = normalize_back(enc_out, memory_inv, gains_w[2], d_memory)
    d_arrived = moe_back_send(places_src, cap_src, enc_moe, d_enc)
    d_dec, gain_self, self_dw, dec_bias = self_backward(
        gains_w[3], dec_dense, dec_parts, True, dec_kept, d_dec
    )
    d_arrived, d_dec, table_share = lax.optimization_barrier((d_arrived, d_dec, table_share))
    enc_dw, returned = moe_back_expert(enc_expert, cap_src, enc_moe, d_arrived)
    dec_cols = share_columns(self_dw + cross_dw, groups)
    enc_share = lax.psum_scatter(enc_dw, "mp", scatter_dimension=0, tiled=False)
    d_enc, gain_enc_moe, enc_router = moe_back_receive(
        enc_mid,
        gains_w[1],
        router_w[0],
        hot_src,
        places_src,
        enc_moe,
        d_enc,
        returned,
        aux_weight * experts / total_src,
        frac_src,
    )
    d_enc, dec_share = lax.optimization_barrier((d_enc, dec_share))
    d_enc, gain_enc, enc_self_dw, enc_bias = self_backward(
        gains_w[0], enc_dense, enc_parts, False, enc_kept, d_enc
    )
    enc_parts = jnp.stack(
        [part.astype(low).reshape(groups, -1, D) for part in enc_self_dw], axis=1
    )
    d_embedded = jnp.concatenate([d_enc, d_dec], axis=0).astype(low)

    def given_ids(turn):
        hot = slots_of(owner, owner_rank, devices, GIVE, turn)
        return exchange(ids_in(hot, piece_ids, GIVE), ("dp", "mp")).reshape(-1)

    def given_rows(turn):
        hot = slots_of(owner, owner_rank, devices, GIVE, turn).astype(low)
        rows = dot_nn(hot, d_embedded).astype(low).reshape(devices, GIVE, D)
        return exchange(rows, ("dp", "mp")).reshape(-1, D)

    landed, d_embedded = lax.optimization_barrier((given_ids(0), d_embedded))
    arrived = given_rows(0)
    gains_grad = jnp.stack(
        [gain_enc, gain_enc_moe, gain_memory, gain_self, gain_cross, gain_dec_moe, gain_final]
    )
    router_grad = jnp.stack([enc_router, dec_router])
    bias_grad = jnp.stack([enc_bias, dec_bias])
    load_src = jnp.sum(enc_moe[2], axis=0)
    load_tgt = jnp.sum(dec_moe[2], axis=0)
    small = [gains_grad, router_grad, bias_grad, load_src, load_tgt, own_loss, own_count]
    summed = total_of(in_lanes(small), groups, experts, 2)
    dense_piece = dense_total(enc_parts, dec_cols, groups, experts)
    arrived, summed, dense_piece = lax.optimization_barrier((arrived, summed, dense_piece))
    table_piece = rows_into(landed, arrived, piece_rows)
    gains_grad, router_grad, bias_grad, load_src, load_tgt, loss_sum, count = from_lanes(
        summed, small
    )

    def give_more(state):
        turn, total = state
        return turn + 1, total + rows_into(given_ids(turn), given_rows(turn), piece_rows)

    turns, table_piece = lax.while_loop(
        lambda state: state[0] < needs[1], give_more, (jnp.int32(1), table_piece)
    )
    table_piece = table_piece + table_share[:piece_rows].astype(jnp.float32)
    expert_share = jnp.stack([enc_share, dec_share]).astype(jnp.float32)
    squares = jnp.zeros((8, LANES), jnp.float32)
    for part in (dense_piece, expert_share, table_piece):
        lanes = jnp.sum((part * part).reshape(-1, part.shape[-1]), axis=0)
        squares = squares + jnp.pad(
            jnp.sum(lanes.reshape(-1, min(LANES, math.gcd(lanes.shape[0], LANES))), axis=0),
            (0, LANES - math.gcd(lanes.shape[0], LANES)),
        )[None, :] * 0.125
    squares = jnp.sum(total_of(squares, groups, experts, 3))
    squares = squares + sum(
        (jnp.sum(part * part) for part in (gains_grad, router_grad, bias_grad))
    )
    grad_norm = jnp.sqrt(squares)
    clip = 1.0 / jnp.maximum(grad_norm, 1.0)
    aux = (
        aux_weight
        * experts
        * (jnp.sum(frac_src * load_src) / total_src + jnp.sum(frac_tgt * load_tgt) / total_tgt)
    )
    loss = jnp.stack([loss_sum + aux, count])
    old_piece = piece_of(dense_m, 4, experts).reshape(dense_piece.shape)
    piece_moment = 0.5 * old_piece + clip * dense_piece
    expert_moment = 0.5 * expert_m + clip * expert_share[:, :, None]
    cols = expert_w.shape[4]
    expert_orth, dense_orth, dense_moment = newton(
        piece_moment, expert_moment.reshape(-1, D, cols), groups, experts
    )

    def as_stored(pieces):
        return whole_of(pieces, 4, count_dense - 4).reshape(count_dense, -1).astype(jnp.float32)

    dense_moment, dense_orth = as_stored(dense_moment), as_stored(dense_orth)
    keep_rate = 1 - rate_matrix * decay_matrix
    dense_new = dense_w * keep_rate - rate_matrix * 0.2 * math.sqrt(D) * dense_orth
    expert_new = expert_w * keep_rate - rate_matrix * 0.2 * math.sqrt(
        max(D, FF)
    ) * expert_orth.astype(jnp.float32).reshape(expert_w.shape)
    table_clipped = clip * table_piece
    table_new, table_first, table_second = adam(
        lax.dynamic_slice_in_dim(table_w, lax.axis_index("dp") * piece_rows, piece_rows, 0),
        table_m,
        table_v,
        table_clipped,
        1.5,
        0.01,
    )

    def part_of(array, like):
        size = like.shape[1]
        return lax.dynamic_slice_in_dim(array, column * size, size, 1)

    gains_new, gains_first, gains_second = adam(
        part_of(gains_w, gains_m), gains_m, gains_v, clip * part_of(gains_grad, gains_m), 0.5, 0.0
    )
    router_new, router_first, router_second = adam(
        part_of(router_w, router_m),
        router_m,
        router_v,
        clip * part_of(router_grad, router_m),
        0.02,
        0.01,
    )
    bias_new, bias_first, bias_second = adam(
        part_of(bias_w, bias_m), bias_m, bias_v, clip * part_of(bias_grad, bias_m), 0.5, 0.0
    )
    return (
        loss,
        grad_norm,
        dense_new,
        dense_moment,
        dense_new.astype(low),
        expert_new,
        expert_moment,
        expert_new.astype(low),
        table_new,
        table_clipped,
        table_second,
        gains_new,
        gains_first,
        gains_second,
        router_new,
        router_first,
        router_second,
        bias_new,
        bias_first,
        bias_second,
    )


def solution(mesh):
    in_specs = (
        P("dp", None),
        P("dp", None),
        P("dp", None),
        P("dp", None),
        P(),
        P(),
        P(None, "mp"),
        P(None, "mp"),
        P(None, None, "dp", None, "mp"),
        P(None, None, "dp", None, "mp"),
        P("mp", None),
        P(("mp", "dp"), None),
        P(("mp", "dp"), None),
        P(),
        P(None, "mp"),
        P(None, "mp"),
        P(),
        P(None, "mp", None),
        P(None, "mp", None),
        P(),
        P(None, "mp", None),
        P(None, "mp", None),
    )
    out_specs = (
        P(),
        P(),
        P(None, "mp"),
        P(None, "mp"),
        P(None, "mp"),
        P(None, None, "dp", None, "mp"),
        P(None, None, "dp", None, "mp"),
        P(None, None, "dp", None, "mp"),
        P(("mp", "dp"), None),
        P(("mp", "dp"), None),
        P(("mp", "dp"), None),
        P(None, "mp"),
        P(None, "mp"),
        P(None, "mp"),
        P(None, "mp", None),
        P(None, "mp", None),
        P(None, "mp", None),
        P(None, "mp", None),
        P(None, "mp", None),
        P(None, "mp", None),
    )
    return jax.shard_map(
        on_device, mesh=mesh, in_specs=in_specs, out_specs=out_specs, check_vma=False
    )
```

```python
from functools import partial
import math

import jax
import jax.numpy as jnp
from jax import lax
from jax.experimental import pallas as pl
from jax.experimental.pallas import tpu as pltpu
from jax.sharding import PartitionSpec as P

D = 768
HEADS = 12
HD = 64
FF = 3072
NS_ITERS = 5
STEP = 10


eps_norm = 1e-06
eps_gram = 1e-07
eps_adam = 1e-08
neg_fill = -1000000000.0
coef_a = 3.4445
coef_b = -4.775
coef_c = 2.0315
beta_one = 0.9
beta_two = 0.95
rate_matrix = 0.2
decay_matrix = 0.01
aux_weight = 0.01
enc_edges = (12, 16, 23, 32, 46, 64, 91)
dec_edges = (19, 21, 24, 27, 31, 35, 40, 46, 52, 59, 67, 77, 87, 99, 113)
highest = lax.Precision.HIGHEST


def normalize(rows, gain):
    inverse = lax.rsqrt(jnp.mean(rows * rows, axis=-1, keepdims=True) + eps_norm)
    return (rows * inverse * gain, inverse)


def normalize_back(rows, inverse, gain, grad):
    scaled = grad * gain
    d_rows = inverse * scaled - rows * inverse**3 * jnp.mean(scaled * rows, axis=-1, keepdims=True)
    return (d_rows, jnp.sum(grad * rows * inverse, axis=0))


def bucket_of(relative, causal):
    if causal:
        distance = jnp.maximum(-relative, 0)
        far = 16 + sum(((distance >= edge).astype(jnp.int32) for edge in dec_edges))
        return jnp.where(distance < 16, distance, far)
    distance = jnp.abs(relative)
    far = 8 + sum(((distance >= edge).astype(jnp.int32) for edge in enc_edges))
    return jnp.where(distance < 8, distance, far) + 16 * (relative > 0).astype(jnp.int32)


LANES = 128
CHUNK = 768
WIDE = 768
FETCH = 128
GIVE = 48
VMEM_LIMIT = 60 * 1024 * 1024


def params(count=1, **more):
    return pltpu.CompilerParams(
        dimension_semantics=("arbitrary",) * count, vmem_limit_bytes=VMEM_LIMIT, **more
    )


def dot_nn(left, right):
    return lax.dot_general(
        left, right, (((1,), (0,)), ((), ())), preferred_element_type=jnp.float32
    )


def dot_nt(left, right):
    return lax.dot_general(
        left, right, (((1,), (1,)), ((), ())), preferred_element_type=jnp.float32
    )


def dot_tn(left, right):
    return lax.dot_general(
        left, right, (((0,), (0,)), ((), ())), preferred_element_type=jnp.float32
    )


def own_lanes(rows, half):
    lane = lax.broadcasted_iota(jnp.int32, rows.shape, 1)
    keep = lane >= HD if half else lane < HD
    return jnp.where(keep, rows, jnp.zeros_like(rows))


def band_offsets():
    place = jnp.arange(4 * LANES, dtype=jnp.int32)
    return LANES - jnp.where(place < 3 * LANES, place, place - 4 * LANES)


def bias_parts(table, causal):
    count = table.shape[0]
    hot = (
        bucket_of(band_offsets(), causal)[:, None] == jnp.arange(count, dtype=jnp.int32)[None, :]
    ).astype(jnp.float32)
    band = jnp.dot(hot, table, precision=highest).T[:, None, :]
    ends = bucket_of(jnp.array([-2 * LANES, 2 * LANES], jnp.int32), causal)
    hot_ends = (ends[:, None] == jnp.arange(count, dtype=jnp.int32)[None, :]).astype(jnp.float32)
    far = jnp.dot(hot_ends, table, precision=highest)
    return band, far, hot, hot_ends


def bias_sums(sums, hot, hot_ends):
    per_place = sums[:, 0, :]
    near = per_place[:, : 4 * LANES]
    far = jnp.sum(per_place[:, 4 * LANES :].reshape(-1, 2, LANES), axis=2)
    return jnp.dot(hot.T, near.T, precision=highest) + jnp.dot(
        hot_ends.T, far.T, precision=highest
    )


def scores_of(keys, queries, head, chunk, far_ref, band, causal):
    scores = dot_nt(keys, queries)
    len_k, width = scores.shape
    if band is not None:
        rows = []
        for a in range(len_k // LANES):
            columns = []
            for b in range(width // LANES):
                apart = a - (chunk * (width // LANES) + b)
                if apart < -1:
                    bias = far_ref[0, head]
                elif apart > 1:
                    bias = far_ref[1, head]
                else:
                    bias = band[:, LANES * (1 - apart) : LANES * (2 - apart)]
                columns.append(
                    scores[LANES * a : LANES * a + LANES, LANES * b : LANES * b + LANES] + bias
                )
            rows.append(jnp.concatenate(columns, axis=1))
        scores = jnp.concatenate(rows, axis=0)
    if causal:
        allowed = lax.broadcasted_iota(jnp.int32, scores.shape, 0) <= (
            lax.broadcasted_iota(jnp.int32, scores.shape, 1) + chunk * width
        )
        scores = jnp.where(allowed, scores, neg_fill)
    return scores


def band_of(band_ref, half):
    row = jnp.broadcast_to(band_ref[half], (LANES, 4 * LANES))
    return pltpu.roll(row, 0, 1, stride=1, stride_axis=0)


def unband(sums):
    row = lax.broadcasted_iota(jnp.int32, sums.shape, 0)
    step = 1
    while step < LANES:
        sums = jnp.where(
            (row & step) != 0, pltpu.roll(sums, sums.shape[1] - step, 1), sums
        )
        step *= 2
    return jnp.sum(sums, axis=0, keepdims=True)


def attend_kernel(biased, causal, *refs):
    if biased:
        far_ref, band_ref, *refs = refs
    q_ref, k_ref, v_ref, out_ref, lse_ref = refs
    pair = pl.program_id(0)
    keys = k_ref[...]
    values_t = v_ref[...].T
    len_q = q_ref.shape[0]
    width = min(CHUNK, len_q)
    bands = [band_of(band_ref, half) if biased else None for half in range(2)]
    for chunk in range(len_q // width):
        span = pl.ds(chunk * width, width)
        queries = q_ref[span, :] * HD ** (-0.5)
        parts = []
        for half in range(2):
            scores = scores_of(
                keys,
                own_lanes(queries, half),
                2 * pair + half,
                chunk,
                far_ref if biased else None,
                bands[half],
                causal,
            )
            top = jnp.max(scores, axis=0, keepdims=True)
            expo = jnp.exp(scores - top)
            total = jnp.sum(expo, axis=0, keepdims=True)
            mixed = dot_nn(values_t[HD * half : HD * half + HD], expo.astype(jnp.bfloat16))
            parts.append(mixed * (1.0 / total))
            lse_ref[half, :, span] = top + jnp.log(total)
        out_ref[span, :] = jnp.concatenate(parts, axis=0).T.astype(jnp.bfloat16)


def attend_back_kernel(biased, causal, *refs):
    if biased:
        far_ref, band_ref, *refs = refs
    q_ref, k_ref, v_ref, g_ref, lse_ref, dq_ref, dk_ref, dv_ref, *refs = refs
    if biased:
        sums_ref, dk_acc, dv_acc, near_acc, far_acc = refs
    else:
        dk_acc, dv_acc = refs
    pair = pl.program_id(0)
    keys = k_ref[...]
    keys_t = keys.T
    values = v_ref[...]
    len_q, len_k = q_ref.shape[0], k_ref.shape[0]
    width = min(CHUNK, len_q)
    scale = HD ** (-0.5)
    dk_acc[...] = jnp.zeros_like(dk_acc)
    dv_acc[...] = jnp.zeros_like(dv_acc)
    bands = [band_of(band_ref, half) if biased else None for half in range(2)]
    if biased:
        near_acc[...] = jnp.zeros_like(near_acc)
        far_acc[...] = jnp.zeros_like(far_acc)
    for chunk in range(len_q // width):
        span = pl.ds(chunk * width, width)
        parts = []
        for half in range(2):
            queries = own_lanes(q_ref[span, :] * HD ** (-0.5), half)
            grads = own_lanes(g_ref[span, :], half)
            scores = scores_of(
                keys,
                queries,
                2 * pair + half,
                chunk,
                far_ref if biased else None,
                bands[half],
                causal,
            )
            probs = jnp.exp(scores - lse_ref[half, :, span])
            d_probs = dot_nt(values, grads)
            delta = jnp.sum(probs * d_probs, axis=0, keepdims=True)
            d_scores = (probs * (d_probs - delta)).astype(jnp.bfloat16)
            dk_acc[...] += dot_nn(d_scores, queries)
            dv_acc[...] += dot_nn(probs.astype(jnp.bfloat16), grads)
            parts.append(dot_nn(keys_t[HD * half : HD * half + HD], d_scores))
            if biased:
                groups = {}
                for a in range(len_k // LANES):
                    for b in range(width // LANES):
                        apart = a - (chunk * (width // LANES) + b)
                        if causal and apart > 0:
                            continue
                        groups.setdefault(max(-2, min(2, apart)), []).append(
                            d_scores[
                                LANES * a : LANES * a + LANES, LANES * b : LANES * b + LANES
                            ].astype(jnp.float32)
                        )
                for apart, blocks in groups.items():
                    total = sum(blocks[1:], blocks[0])
                    if abs(apart) < 2:
                        near_acc[half, :, LANES * (1 - apart) : LANES * (2 - apart)] += total
                    else:
                        side = 0 if apart < 0 else 1
                        far_acc[half, :, LANES * side : LANES * side + LANES] += total
        dq_ref[span, :] = (jnp.concatenate(parts, axis=0).T * scale).astype(jnp.bfloat16)
    dk_ref[...] = dk_acc[...].astype(jnp.bfloat16)
    dv_ref[...] = dv_acc[...].astype(jnp.bfloat16)
    if biased:
        for half in range(2):
            sums_ref[half, :, : 4 * LANES] = unband(near_acc[half])
            sums_ref[half, :, 4 * LANES :] = jnp.sum(far_acc[half], axis=0, keepdims=True)


def pair_spec(rows, shift):
    return pl.BlockSpec((rows, LANES), lambda pair, shift=shift: (0, shift + pair))


def row_spec(width):
    return pl.BlockSpec((2, 1, width), lambda pair: (pair, 0, 0))


def attend_cost(len_q, len_k, dots):
    return pl.CostEstimate(
        flops=2 * dots * HEADS * len_q * len_k * HD,
        bytes_accessed=8 * D * (len_q + len_k),
        transcendentals=HEADS * len_q * len_k,
    )


def attend(query, keys, values, parts, causal):
    len_q, len_k = query[0].shape[0], keys[0].shape[0]
    biased = parts is not None
    pairs = D // LANES
    first = [parts[1], parts[0]] if biased else []
    first_specs = [pl.BlockSpec(memory_space=pltpu.SMEM), row_spec(4 * LANES)] if biased else []
    return pl.pallas_call(
        partial(attend_kernel, biased, causal),
        grid=(pairs,),
        in_specs=first_specs
        + [
            pair_spec(len_q, query[1] * pairs),
            pair_spec(len_k, keys[1] * pairs),
            pair_spec(len_k, values[1] * pairs),
        ],
        out_specs=[pair_spec(len_q, 0), row_spec(len_q)],
        out_shape=[
            jax.ShapeDtypeStruct((len_q, D), jnp.bfloat16),
            jax.ShapeDtypeStruct((HEADS, 1, len_q), jnp.float32),
        ],
        compiler_params=params(),
        cost_estimate=attend_cost(len_q, len_k, 2),
    )(*first, query[0], keys[0], values[0])


def attend_back(query, keys, values, parts, causal, logsum, d_mixed):
    len_q, len_k = query[0].shape[0], keys[0].shape[0]
    biased = parts is not None
    pairs = D // LANES
    first = [parts[1], parts[0]] if biased else []
    first_specs = [pl.BlockSpec(memory_space=pltpu.SMEM), row_spec(4 * LANES)] if biased else []
    low = jnp.bfloat16
    return pl.pallas_call(
        partial(attend_back_kernel, biased, causal),
        grid=(pairs,),
        in_specs=first_specs
        + [
            pair_spec(len_q, query[1] * pairs),
            pair_spec(len_k, keys[1] * pairs),
            pair_spec(len_k, values[1] * pairs),
            pair_spec(len_q, 0),
            row_spec(len_q),
        ],
        out_specs=[pair_spec(len_q, 0), pair_spec(len_k, 0), pair_spec(len_k, 0)]
        + ([row_spec(6 * LANES)] if biased else []),
        out_shape=[
            jax.ShapeDtypeStruct((len_q, D), low),
            jax.ShapeDtypeStruct((len_k, D), low),
            jax.ShapeDtypeStruct((len_k, D), low),
        ]
        + ([jax.ShapeDtypeStruct((HEADS, 1, 6 * LANES), jnp.float32)] if biased else []),
        scratch_shapes=[
            pltpu.VMEM((len_k, LANES), jnp.float32),
            pltpu.VMEM((len_k, LANES), jnp.float32),
        ]
        + (
            [
                pltpu.VMEM((2, LANES, 4 * LANES), jnp.float32),
                pltpu.VMEM((2, LANES, 2 * LANES), jnp.float32),
            ]
            if biased
            else []
        ),
        compiler_params=params(),
        cost_estimate=attend_cost(len_q, len_k, 5),
    )(*first, query[0], keys[0], values[0], d_mixed, logsum)


gelu_scale = math.sqrt(2.0 / math.pi)
gelu_cube = 0.044715


def side_by_side(ref):
    return jnp.concatenate([ref[j, 0] for j in range(ref.shape[0])], axis=1)


def expert_kernel(x_ref, wi_ref, wo_ref, pre_ref, out_ref, acc_ref):
    block = pl.program_id(0)
    pre = dot_nn(x_ref[...], side_by_side(wi_ref))
    pre_ref[0] = pre
    bend = jnp.tanh(gelu_scale * (pre + gelu_cube * (pre * pre * pre)))
    hidden = (0.5 * pre * (1.0 + bend)).astype(jnp.bfloat16)
    part = dot_nt(hidden, side_by_side(wo_ref))

    @pl.when(block == 0)
    def _():
        acc_ref[...] = part

    @pl.when(block > 0)
    def _():
        acc_ref[...] += part

    @pl.when(block == pl.num_programs(0) - 1)
    def _():
        out_ref[...] = acc_ref[...].astype(jnp.bfloat16)


def expert_forward(arrived, weights):
    rows = arrived.shape[0]
    blocks, unused, unused_too, cols = weights.shape
    per = WIDE // cols
    whole = pl.BlockSpec((rows, D), lambda j: (0, 0))
    return pl.pallas_call(
        expert_kernel,
        grid=(blocks // per,),
        in_specs=[
            whole,
            pl.BlockSpec((per, 1, D, cols), lambda j: (j, 0, 0, 0)),
            pl.BlockSpec((per, 1, D, cols), lambda j: (j, 1, 0, 0)),
        ],
        out_specs=[pl.BlockSpec((1, rows, WIDE), lambda j: (j, 0, 0)), whole],
        out_shape=[
            jax.ShapeDtypeStruct((blocks // per, rows, WIDE), jnp.float32),
            jax.ShapeDtypeStruct((rows, D), jnp.bfloat16),
        ],
        scratch_shapes=[pltpu.VMEM((rows, D), jnp.float32)],
        compiler_params=params(),
        cost_estimate=pl.CostEstimate(
            flops=4 * rows * D * FF,
            bytes_accessed=4 * D * FF + 4 * rows * (FF + D),
            transcendentals=rows * FF,
        ),
    )(arrived, weights, weights)


def expert_back_kernel(x_ref, g_ref, pre_ref, wi_ref, wo_ref, dw_ref, back_ref, acc_ref):
    block = pl.program_id(0)
    arrived = x_ref[...]
    grads = g_ref[...]
    pre = pre_ref[0]
    square = pre * pre
    bend = jnp.tanh(gelu_scale * (pre + gelu_cube * (square * pre)))
    half = 0.5 * (1.0 + bend)
    hidden = (pre * half).astype(jnp.bfloat16)
    slope = half + 0.5 * pre * (1.0 - bend * bend) * (
        gelu_scale * (1.0 + 3.0 * gelu_cube * square)
    )
    d_pre = (dot_nn(grads, side_by_side(wo_ref)) * slope).astype(jnp.bfloat16)
    d_in = dot_tn(arrived, d_pre).astype(jnp.bfloat16)
    d_out = dot_tn(grads, hidden).astype(jnp.bfloat16)
    cols = dw_ref.shape[3]
    for j in range(dw_ref.shape[0]):
        dw_ref[j, 0] = d_in[:, cols * j : cols * j + cols]
        dw_ref[j, 1] = d_out[:, cols * j : cols * j + cols]
    part = dot_nt(d_pre, side_by_side(wi_ref))

    @pl.when(block == 0)
    def _():
        acc_ref[...] = part

    @pl.when(block > 0)
    def _():
        acc_ref[...] += part

    @pl.when(block == pl.num_programs(0) - 1)
    def _():
        back_ref[...] = acc_ref[...].astype(jnp.bfloat16)


def expert_backward(arrived, d_arrived, pre, weights):
    rows = arrived.shape[0]
    blocks, unused, unused_too, cols = weights.shape
    per = WIDE // cols
    whole = pl.BlockSpec((rows, D), lambda j: (0, 0))
    return pl.pallas_call(
        expert_back_kernel,
        grid=(blocks // per,),
        in_specs=[
            whole,
            whole,
            pl.BlockSpec((1, rows, WIDE), lambda j: (j, 0, 0)),
            pl.BlockSpec((per, 1, D, cols), lambda j: (j, 0, 0, 0)),
            pl.BlockSpec((per, 1, D, cols), lambda j: (j, 1, 0, 0)),
        ],
        out_specs=[pl.BlockSpec((per, 2, D, cols), lambda j: (j, 0, 0, 0)), whole],
        out_shape=[
            jax.ShapeDtypeStruct((blocks, 2, D, cols), jnp.bfloat16),
            jax.ShapeDtypeStruct((rows, D), jnp.bfloat16),
        ],
        scratch_shapes=[pltpu.VMEM((rows, D), jnp.float32)],
        compiler_params=params(),
        cost_estimate=pl.CostEstimate(
            flops=8 * rows * D * FF,
            bytes_accessed=8 * D * FF + 4 * rows * (FF + 2 * D),
            transcendentals=rows * FF,
        ),
    )(arrived, d_arrived, pre, weights, weights)


def mirror(left, right, store):
    tile = 2 * LANES
    for a in range(0, D, tile):
        block = dot_nt(left[a : a + tile, :], right[: a + tile, :])
        store(slice(a, a + tile), slice(0, a + tile), block)
        if a:
            store(slice(0, a), slice(a, a + tile), block[:, :a].T)


def newton_gram(source, gram_ref):
    def keep(rows, columns, block):
        gram_ref[rows, columns] = block

    mirror(source, source, keep)


def newton_poly(product, poly_ref):
    def keep(rows, columns, block):
        poly_ref[rows, columns] = (
            coef_b * product[rows, columns].astype(jnp.float32) + coef_c * block
        ).astype(jnp.bfloat16)

    mirror(product, product, keep)


def newton_apply(source, poly_ref, j, outer):
    part = source[:, D * j : D * j + D]
    fresh = coef_a * part.astype(jnp.float32) + dot_nn(poly_ref[...], part)
    if outer is not None:
        fresh = fresh * outer
    source[:, D * j : D * j + D] = fresh.astype(jnp.bfloat16)


def newton_rounds(source, gram_ref, poly_ref, between, finish):
    blocks = source.shape[1] // D
    newton_gram(source, gram_ref)
    row = lax.broadcasted_iota(jnp.int32, (D, D), 0)
    column = lax.broadcasted_iota(jnp.int32, (D, D), 1)
    whole = gram_ref[...].astype(jnp.bfloat16).astype(jnp.float32)
    scale = jnp.sum(jnp.where(row == column, whole, 0.0), keepdims=True) + eps_gram
    newton_poly((whole * (1.0 / scale)).astype(jnp.bfloat16), poly_ref)
    for j in range(blocks):
        newton_apply(source, poly_ref, j, lax.rsqrt(scale))

    def turn(index, carry):
        newton_gram(source, gram_ref)
        newton_poly(gram_ref[...].astype(jnp.bfloat16), poly_ref)
        for j in range(blocks):
            newton_apply(source, poly_ref, j, None)
        return carry

    lax.fori_loop(1, NS_ITERS - 1, turn, 0)
    between()
    newton_gram(source, gram_ref)
    newton_poly(gram_ref[...].astype(jnp.bfloat16), poly_ref)
    for j in range(blocks):
        newton_apply(source, poly_ref, j, None)
        finish(j)


def newton_kernel(
    groups,
    experts,
    squares_ref,
    expert_old_ref,
    expert_grad_ref,
    dense_old_ref,
    dense_grad_ref,
    squares_out,
    expert_moment_out,
    expert_out,
    dense_out,
    moment_out,
    expert_ref,
    dense_ref,
    squares_row,
    squares_sum,
    squares_col,
    held,
    held_dense,
    matrix,
    square,
    gram_ref,
    poly_ref,
    land_expert,
    land_dense,
    all_dense,
    all_moment,
    send_sem,
    in_sem,
    back_send_sem,
    back_sem,
    orth_send_sem,
    orth_sem,
    moment_send_sem,
    moment_sem,
    row_send_sem,
    row_sem,
    col_send_sem,
    col_sem,
):
    me = lax.axis_index("mp")
    along = lax.axis_index("dp")
    own = me // 2
    count_expert, count_dense = expert_ref.shape[0], dense_ref.shape[0]
    cols, cols_dense = expert_ref.shape[2], dense_ref.shape[1]
    is_expert = ((me % 2) == 0) & (own < count_expert)
    is_dense = ((me % 2) == 1) & (own < count_dense)
    per = D // cols
    barrier = pltpu.get_barrier_semaphore()
    for step in range(1, groups):
        other = lax.rem(me + step, groups)
        pl.semaphore_signal(
            barrier, inc=1, device_id={"mp": other}, device_id_type=pl.DeviceIdType.MESH
        )
    for step in range(1, experts):
        other = lax.rem(along + step, experts)
        pl.semaphore_signal(
            barrier, inc=1, device_id={"dp": other}, device_id_type=pl.DeviceIdType.MESH
        )
    pl.semaphore_wait(barrier, groups + experts - 2)

    def remote(source, target, sent, landed, device):
        return pltpu.make_async_remote_copy(
            src_ref=source,
            dst_ref=target,
            send_sem=sent,
            recv_sem=landed,
            device_id={"mp": device},
            device_id_type=pl.DeviceIdType.MESH,
        )

    def to_row(step, source):
        return remote(
            squares_ref,
            squares_row.at[source],
            row_send_sem.at[step],
            row_sem.at[source],
            lax.rem(me + step, groups),
        )

    def to_col(step, source):
        return pltpu.make_async_remote_copy(
            src_ref=squares_sum,
            dst_ref=squares_col.at[source],
            send_sem=col_send_sem.at[step],
            recv_sem=col_sem.at[source],
            device_id={"dp": lax.rem(along + step, experts)},
            device_id_type=pl.DeviceIdType.MESH,
        )

    for step in range(1, groups):
        to_row(step, me).start()
    squares_row[me] = squares_ref[...]
    for step in range(1, groups):
        to_row(step, lax.rem(me + step, groups)).wait_recv()
    squares = squares_row[0]
    for source in range(1, groups):
        squares = squares + squares_row[source]
    squares_sum[...] = squares
    squares_col[along] = squares
    for step in range(1, experts):
        to_col(step, along).start()
    for step in range(1, experts):
        to_col(step, lax.rem(along + step, experts)).wait_recv()
    squares = squares_col[0]
    for source in range(1, experts):
        squares = squares + squares_col[source]
    squares_out[...] = squares
    norm = jnp.sqrt(jnp.sum(squares, keepdims=True))
    clip = 1.0 / jnp.maximum(norm, 1.0)
    for index in range(count_dense):
        moment = 0.5 * dense_old_ref[index] + clip * dense_grad_ref[index]
        dense_ref[index] = moment.astype(jnp.bfloat16)
    for index in range(count_expert):
        moment = 0.5 * expert_old_ref[index] + clip * expert_grad_ref[index].astype(jnp.float32)
        expert_moment_out[index] = moment
        expert_ref[index] = moment.astype(jnp.bfloat16)
    for step in range(1, groups):
        to_row(step, me).wait_send()
    for step in range(1, experts):
        to_col(step, along).wait_send()

    def outward(index, source):
        dense = index >= count_expert
        place = index - count_expert if dense else index
        held_ref = held_dense if dense else held
        own_ref = dense_ref if dense else expert_ref
        return remote(
            own_ref.at[place],
            held_ref.at[source],
            send_sem.at[index],
            in_sem.at[source],
            2 * place + (1 if dense else 0),
        )

    def sideways(step, source, orth):
        return pltpu.make_async_remote_copy(
            src_ref=land_dense if orth else dense_ref,
            dst_ref=(all_dense if orth else all_moment).at[source],
            send_sem=(orth_send_sem if orth else moment_send_sem).at[step],
            recv_sem=(orth_sem if orth else moment_sem).at[source],
            device_id={"dp": lax.rem(along + step, experts)},
            device_id_type=pl.DeviceIdType.MESH,
        )

    total = count_expert + count_dense
    owners = [2 * e for e in range(count_expert)] + [2 * d + 1 for d in range(count_dense)]
    for index in range(total):

        @pl.when(me != owners[index])
        def _(index=index):
            outward(index, me).start()

    for step in range(1, experts):
        sideways(step, along, False).start()

    for step in range(1, groups):
        source = lax.rem(me + step, groups)

        @pl.when(is_expert)
        def _(source=source):
            outward(0, source).wait_recv()

        @pl.when(is_dense)
        def _(source=source):
            outward(count_expert, source).wait_recv()

    for index in range(total):

        @pl.when(me != owners[index])
        def _(index=index):
            outward(index, me).wait_send()

    def backward_expert(target):
        return remote(
            held.at[target],
            land_expert.at[own],
            back_send_sem.at[target],
            back_sem.at[own],
            target,
        )

    def backward_dense(target):
        return remote(
            held_dense.at[target],
            land_dense.at[own],
            back_send_sem.at[target],
            back_sem.at[count_expert + own],
            target,
        )

    def share_dense():
        for index in range(count_expert, total):

            @pl.when(me != owners[index])
            def _(index=index):
                landing = land_dense.at[index - count_expert]
                remote(
                    landing, landing, send_sem.at[index], back_sem.at[index], owners[index]
                ).wait_recv()

        for step in range(1, experts):
            sideways(step, along, True).start()

    def nothing():
        return None

    @pl.when(is_expert)
    def _():
        held[me] = expert_ref[own]
        for j in range(groups // per):
            matrix[:, D * j : D * j + D] = jnp.concatenate(
                [held[per * j + inner] for inner in range(per)], axis=1
            )

        def finish(j):
            for inner in range(per):
                target = per * j + inner
                held[target] = matrix[:, cols * target : cols * target + cols]

                @pl.when(me != target)
                def _(target=target):
                    backward_expert(target).start()

        newton_rounds(matrix, gram_ref, poly_ref, share_dense, finish)
        land_expert[own] = held[me]
        for target in range(groups):

            @pl.when(me != target)
            def _(target=target):
                backward_expert(target).wait_send()

    @pl.when(is_dense)
    def _():
        held_dense[me] = dense_ref[own]
        for source in range(groups):
            square[cols_dense * source : cols_dense * source + cols_dense, :] = held_dense[source]

        def finish(j):
            for target in range(groups):
                held_dense[target] = square[
                    cols_dense * target : cols_dense * target + cols_dense, :
                ]

                @pl.when(me != target)
                def _(target=target):
                    backward_dense(target).start()

        newton_rounds(square, gram_ref, poly_ref, nothing, finish)
        land_dense[own] = held_dense[me]
        share_dense()
        for target in range(groups):

            @pl.when(me != target)
            def _(target=target):
                backward_dense(target).wait_send()

    @pl.when(jnp.logical_not(is_expert | is_dense))
    def _():
        share_dense()

    for index in range(count_expert):

        @pl.when(me != owners[index])
        def _(index=index):
            landing = land_expert.at[index]
            remote(
                landing, landing, send_sem.at[index], back_sem.at[index], owners[index]
            ).wait_recv()

    all_dense[along] = land_dense[...]
    all_moment[along] = dense_ref[...]
    for step in range(1, experts):
        sideways(step, lax.rem(along + step, experts), True).wait_recv()
        sideways(step, lax.rem(along + step, experts), False).wait_recv()
        sideways(step, along, True).wait_send()
        sideways(step, along, False).wait_send()
    expert_out[...] = land_expert[...]
    dense_out[...] = all_dense[...]
    moment_out[...] = all_moment[...]


def newton(squares, expert_old, expert_grad, dense_old, dense_grad, groups, experts):
    cols, cols_dense = expert_old.shape[2], dense_old.shape[1]
    count_expert, count_dense = expert_old.shape[0], dense_old.shape[0]
    low = jnp.bfloat16
    vmem = pl.BlockSpec(memory_space=pltpu.VMEM)
    dma = pltpu.SemaphoreType.DMA
    return pl.pallas_call(
        partial(newton_kernel, groups, experts),
        in_specs=[vmem] * 5,
        out_specs=[vmem] * 5,
        out_shape=[
            jax.ShapeDtypeStruct(squares.shape, jnp.float32),
            jax.ShapeDtypeStruct(expert_old.shape, jnp.float32),
            jax.ShapeDtypeStruct(expert_old.shape, low),
            jax.ShapeDtypeStruct((experts,) + dense_old.shape, low),
            jax.ShapeDtypeStruct((experts,) + dense_old.shape, low),
        ],
        scratch_shapes=[
            pltpu.VMEM(expert_old.shape, low),
            pltpu.VMEM(dense_old.shape, low),
            pltpu.VMEM((groups,) + squares.shape, jnp.float32),
            pltpu.VMEM(squares.shape, jnp.float32),
            pltpu.VMEM((experts,) + squares.shape, jnp.float32),
            pltpu.VMEM((groups, D, cols), low),
            pltpu.VMEM((groups, cols_dense, D), low),
            pltpu.VMEM((D, groups * cols), low),
            pltpu.VMEM((D, D), low),
            pltpu.VMEM((D, D), jnp.float32),
            pltpu.VMEM((D, D), low),
            pltpu.VMEM(expert_old.shape, low),
            pltpu.VMEM(dense_old.shape, low),
            pltpu.VMEM((experts,) + dense_old.shape, low),
            pltpu.VMEM((experts,) + dense_old.shape, low),
            dma((count_expert + count_dense,)),
            dma((groups,)),
            dma((groups,)),
            dma((count_expert + count_dense,)),
            dma((experts,)),
            dma((experts,)),
            dma((experts,)),
            dma((experts,)),
            dma((groups,)),
            dma((groups,)),
            dma((experts,)),
            dma((experts,)),
        ],
        compiler_params=pltpu.CompilerParams(
            vmem_limit_bytes=VMEM_LIMIT, collective_id=1, has_side_effects=True
        ),
        cost_estimate=pl.CostEstimate(
            flops=NS_ITERS * (4 * D * D * FF + 2 * D * D * D),
            bytes_accessed=40 * D * FF,
            transcendentals=0,
        ),
    )(squares, expert_old, expert_grad, dense_old, dense_grad)


def gather_kernel(groups, x_ref, out_ref, land, send_sem, pass_sem, land_sem):
    me = lax.axis_index("mp")
    half, side = me // 2, me % 2
    halves = groups // 2
    sibling = me + 1 - 2 * side
    barrier = pltpu.get_barrier_semaphore()
    mesh_id = pl.DeviceIdType.MESH
    for step in range(1, halves):
        other = 2 * lax.rem(half + step, halves) + side
        pl.semaphore_signal(barrier, inc=1, device_id={"mp": other}, device_id_type=mesh_id)
    pl.semaphore_signal(barrier, inc=1, device_id={"mp": sibling}, device_id_type=mesh_id)
    pl.semaphore_wait(barrier, halves)

    def remote(source, index, sent, device):
        return pltpu.make_async_remote_copy(
            src_ref=source,
            dst_ref=land.at[index],
            send_sem=sent,
            recv_sem=land_sem.at[index],
            device_id={"mp": device},
            device_id_type=mesh_id,
        )

    def direct(step):
        return remote(x_ref, me, send_sem.at[step], 2 * lax.rem(half + step, halves) + side)

    def passed(step):
        index = 2 * lax.rem(half + step, halves) + side
        return remote(land.at[index], index, pass_sem.at[step], sibling)

    for step in range(1, halves):
        direct(step).start()
    to_sibling = remote(x_ref, me, send_sem.at[0], sibling)
    to_sibling.start()
    land[me] = x_ref[...]
    for step in range(1, halves):
        index = 2 * lax.rem(half + step, halves) + side
        remote(x_ref, index, send_sem.at[step], sibling).wait_recv()
        passed(step).start()
    for step in range(halves):
        index = 2 * lax.rem(half + step, halves) + 1 - side
        remote(x_ref, index, send_sem.at[step], sibling).wait_recv()
    to_sibling.wait_send()
    for step in range(1, halves):
        direct(step).wait_send()
        passed(step).wait_send()
    out_ref[...] = land[...]


def gathered_over(array, groups, collective):
    vmem = pl.BlockSpec(memory_space=pltpu.VMEM)
    dma = pltpu.SemaphoreType.DMA
    shape = (groups,) + array.shape
    return pl.pallas_call(
        partial(gather_kernel, groups),
        in_specs=[vmem],
        out_specs=vmem,
        out_shape=jax.ShapeDtypeStruct(shape, array.dtype),
        scratch_shapes=[
            pltpu.VMEM(shape, array.dtype),
            dma((groups // 2,)),
            dma((groups // 2,)),
            dma((groups,)),
        ],
        compiler_params=pltpu.CompilerParams(
            vmem_limit_bytes=(
                4 * math.prod(shape) * array.dtype.itemsize + 2 * 1024 * 1024
            ),
            collective_id=collective,
            has_side_effects=True,
        ),
        cost_estimate=pl.CostEstimate(flops=0, bytes_accessed=20000000, transcendentals=0),
    )(array)


def lookup_kernel(vocab, wanted_ref, table_ref, out_ref, acc_ref):
    block = pl.program_id(0)
    height = table_ref.shape[0]
    place = lax.broadcasted_iota(jnp.int32, (wanted_ref.shape[0], height), 1) + block * height
    pick = (wanted_ref[...] == place).astype(jnp.bfloat16)
    row = lax.broadcasted_iota(jnp.int32, table_ref.shape, 0) + block * height
    table = jnp.where(row < vocab, table_ref[...], 0.0).astype(jnp.bfloat16)
    part = dot_nn(pick, table)

    @pl.when(block == 0)
    def _():
        acc_ref[...] = part

    @pl.when(block > 0)
    def _():
        acc_ref[...] += part

    @pl.when(block == pl.num_programs(0) - 1)
    def _():
        out_ref[...] = acc_ref[...].astype(jnp.bfloat16)


def lookup(wanted, table):
    count = wanted.shape[0]
    vocab = table.shape[0]
    height = 1024
    whole = pl.BlockSpec((count, D), lambda j: (0, 0))
    return pl.pallas_call(
        partial(lookup_kernel, vocab),
        grid=(-(-vocab // height),),
        in_specs=[
            pl.BlockSpec((count, 1), lambda j: (0, 0)),
            pl.BlockSpec((height, D), lambda j: (j, 0)),
        ],
        out_specs=whole,
        out_shape=jax.ShapeDtypeStruct((count, D), jnp.bfloat16),
        scratch_shapes=[pltpu.VMEM((count, D), jnp.float32)],
        compiler_params=params(),
        cost_estimate=pl.CostEstimate(
            flops=2 * count * vocab * D, bytes_accessed=4 * vocab * D, transcendentals=0
        ),
    )(wanted[:, None], table)


def dense_kernel(
    groups,
    experts,
    enc_ref,
    dec_ref,
    small_ref,
    out_ref,
    small_out,
    land_pair,
    paired,
    land,
    summed,
    land_enc,
    land_dec,
    small_row,
    small_sum,
    small_col,
    pair_send_sem,
    pair_sem,
    send_sem,
    land_sem,
    enc_send_sem,
    enc_sem,
    dec_send_sem,
    dec_sem,
    row_send_sem,
    row_sem,
    col_send_sem,
    col_sem,
):
    across, along = lax.axis_index("mp"), lax.axis_index("dp")
    half, side = across // 2, across % 2
    halves = groups // 2
    count = enc_ref.shape[2]
    per_enc, per_dec = land_enc.shape[1], land_dec.shape[1]
    barrier = pltpu.get_barrier_semaphore()
    mesh_id = pl.DeviceIdType.MESH
    for step in range(1, groups):
        other = lax.rem(across + step, groups)
        pl.semaphore_signal(barrier, inc=1, device_id={"mp": other}, device_id_type=mesh_id)
    for step in range(1, experts):
        other = lax.rem(along + step, experts)
        pl.semaphore_signal(barrier, inc=1, device_id={"dp": other}, device_id_type=mesh_id)
    pl.semaphore_wait(barrier, groups + experts - 2)

    def remote(source, target, sent, landed, device):
        return pltpu.make_async_remote_copy(
            src_ref=source,
            dst_ref=target,
            send_sem=sent,
            recv_sem=landed,
            device_id=device,
            device_id_type=mesh_id,
        )

    def to_small_row(step, source):
        return remote(
            small_ref,
            small_row.at[source],
            row_send_sem.at[step],
            row_sem.at[source],
            {"mp": lax.rem(across + step, groups)},
        )

    def to_small_col(step, source):
        return remote(
            small_sum,
            small_col.at[source],
            col_send_sem.at[step],
            col_sem.at[source],
            {"dp": lax.rem(along + step, experts)},
        )

    def to_half(step, source):
        other = lax.rem(half + step, halves)
        return remote(
            paired.at[other],
            land.at[source],
            send_sem.at[step],
            land_sem.at[source],
            {"mp": 2 * other + side},
        )

    def to_col(step, source, dec):
        other = lax.rem(along + step, experts)
        per = per_dec if dec else per_enc
        return remote(
            (dec_ref if dec else summed).at[pl.ds(other * per, per)],
            (land_dec if dec else land_enc).at[source],
            (dec_send_sem if dec else enc_send_sem).at[step],
            (dec_sem if dec else enc_sem).at[source],
            {"dp": other},
        )

    to_pair = remote(
        enc_ref.at[1 - side],
        land_pair,
        pair_send_sem.at[0],
        pair_sem.at[0],
        {"mp": across + 1 - 2 * side},
    )
    to_pair.start()
    for step in range(1, groups):
        to_small_row(step, across).start()
    for step in range(1, experts):
        to_col(step, along, True).start()
    small_row[across] = small_ref[...]
    land_dec[along] = dec_ref[pl.ds(along * per_dec, per_dec)]
    to_pair.wait_recv()
    for step in range(1, halves + 1):
        other = lax.rem(half + step, halves)
        for index in range(count):
            paired[other, index] = (
                enc_ref[side, other, index].astype(jnp.float32)
                + land_pair[other, index].astype(jnp.float32)
            ).astype(jnp.bfloat16)
        if step < halves:
            to_half(step, half).start()
    land[half] = paired[half]
    for step in range(1, groups):
        to_small_row(step, lax.rem(across + step, groups)).wait_recv()
    total = small_row[0]
    for source in range(1, groups):
        total = total + small_row[source]
    small_sum[...] = total
    small_col[along] = total
    for step in range(1, experts):
        to_small_col(step, along).start()
    for step in range(1, halves):
        to_half(step, lax.rem(half + step, halves)).wait_recv()
    for index in range(count):
        total = land[0, index].astype(jnp.float32)
        for source in range(1, halves):
            total = total + land[source, index].astype(jnp.float32)
        summed[index] = total.astype(jnp.bfloat16)
    for index in range(count, summed.shape[0]):
        summed[index] = jnp.zeros(summed.shape[1:], jnp.bfloat16)
    for step in range(1, experts):
        to_col(step, along, False).start()
    land_enc[along] = summed[pl.ds(along * per_enc, per_enc)]
    to_pair.wait_send()
    for step in range(1, groups):
        to_small_row(step, across).wait_send()
    for step in range(1, halves):
        to_half(step, half).wait_send()
    for step in range(1, experts):
        source = lax.rem(along + step, experts)
        to_small_col(step, source).wait_recv()
        to_col(step, source, True).wait_recv()
        to_col(step, source, False).wait_recv()
        to_small_col(step, along).wait_send()
        to_col(step, along, True).wait_send()
        to_col(step, along, False).wait_send()
    total = small_col[0]
    for source in range(1, experts):
        total = total + small_col[source]
    small_out[...] = total
    for landed, per, first in ((land_enc, per_enc, 0), (land_dec, per_dec, per_enc)):
        for index in range(per):
            total = landed[0, index].astype(jnp.float32)
            for source in range(1, experts):
                total = total + landed[source, index].astype(jnp.float32)
            out_ref[first + index] = total


def dense_total(enc, dec, small, groups, experts):
    count, cols = enc.shape[2], enc.shape[3]
    per_enc, per_dec = -(-count // experts), -(-dec.shape[0] // experts)
    dec = jnp.pad(dec, ((0, per_dec * experts - dec.shape[0]), (0, 0), (0, 0)))
    vmem = pl.BlockSpec(memory_space=pltpu.VMEM)
    dma = pltpu.SemaphoreType.DMA
    low = jnp.bfloat16
    halves = groups // 2
    return pl.pallas_call(
        partial(dense_kernel, groups, experts),
        in_specs=[vmem, vmem, vmem],
        out_specs=[vmem, vmem],
        out_shape=[
            jax.ShapeDtypeStruct((per_enc + per_dec, cols, D), jnp.float32),
            jax.ShapeDtypeStruct(small.shape, jnp.float32),
        ],
        scratch_shapes=[
            pltpu.VMEM(enc.shape[1:], low),
            pltpu.VMEM(enc.shape[1:], low),
            pltpu.VMEM(enc.shape[1:], low),
            pltpu.VMEM((per_enc * experts, cols, D), low),
            pltpu.VMEM((experts, per_enc, cols, D), low),
            pltpu.VMEM((experts, per_dec, cols, D), low),
            pltpu.VMEM((groups,) + small.shape, jnp.float32),
            pltpu.VMEM(small.shape, jnp.float32),
            pltpu.VMEM((experts,) + small.shape, jnp.float32),
            dma((1,)),
            dma((1,)),
            dma((halves,)),
            dma((halves,)),
            dma((experts,)),
            dma((experts,)),
            dma((experts,)),
            dma((experts,)),
            dma((groups,)),
            dma((groups,)),
            dma((experts,)),
            dma((experts,)),
        ],
        compiler_params=pltpu.CompilerParams(
            vmem_limit_bytes=VMEM_LIMIT, collective_id=4, has_side_effects=True
        ),
        cost_estimate=pl.CostEstimate(
            flops=0, bytes_accessed=200000000, transcendentals=0
        ),
    )(enc, dec, small)


def piece_of(array, count, experts):
    along = lax.axis_index("dp")
    pieces = []
    for part in (array[:count], array[count:]):
        per = -(-part.shape[0] // experts)
        spare = per * experts - part.shape[0]
        part = jnp.pad(part, ((0, spare),) + ((0, 0),) * (part.ndim - 1))
        pieces.append(lax.dynamic_slice_in_dim(part, along * per, per, 0))
    return jnp.concatenate(pieces, axis=0)


def whole_of(pieces, count, rest):
    per = -(-count // pieces.shape[0])
    first = pieces[:, :per].reshape((-1,) + pieces.shape[2:])[:count]
    second = pieces[:, per:].reshape((-1,) + pieces.shape[2:])[:rest]
    return jnp.concatenate([first, second], axis=0)


def project(rows, stored):
    flat = stored.reshape(-1, D)
    return dot_nt(rows, flat)


def swap_owners(buffer):
    return lax.all_to_all(buffer, "dp", split_axis=0, concat_axis=0, tiled=True)


def dispatch(places, count):
    slot = lax.broadcasted_iota(jnp.int32, (count, places.shape[0]), 0)
    return (slot == places[None, :]).astype(jnp.bfloat16)


def route_places(routes, experts, cap):
    hot = (routes[:, None] == jnp.arange(experts, dtype=jnp.int32)[None, :]).astype(jnp.float32)
    rows = routes.shape[0]
    earlier = (
        lax.broadcasted_iota(jnp.int32, (rows, rows), 1)
        < lax.broadcasted_iota(jnp.int32, (rows, rows), 0)
    ).astype(jnp.bfloat16)
    ranks = dot_nn(earlier, hot.astype(jnp.bfloat16))
    slots = jnp.sum(hot * ranks, axis=1).astype(jnp.int32)
    return hot, routes * cap + slots


def moe_send(resid, gain, router, hot, places, cap):
    experts = router.shape[1]
    normed, inverse = normalize(resid, gain)
    normed_low = normed.astype(jnp.bfloat16)
    buffer = dot_nn(dispatch(places, experts * cap), normed_low).astype(jnp.bfloat16)
    arrived = swap_owners(buffer.reshape(experts, cap, D)).reshape(-1, D)
    probs = jax.nn.softmax(
        jnp.dot(normed_low.astype(jnp.float32), router, precision=highest), axis=-1
    )
    gate = jnp.sum(probs * hot, axis=1)
    return arrived, (normed_low, inverse, probs, gate)


def moe_expert(weights, cap, arrived):
    pre, result = expert_forward(arrived, weights)
    return pre, swap_owners(result.reshape(-1, cap, D)).reshape(-1, D)


def moe_receive(resid, places, arrived, pre, returned, sent):
    outputs = dot_tn(dispatch(places, returned.shape[0]), returned)
    return (resid + sent[3][:, None] * outputs, sent + (arrived, pre, outputs))


def moe_back_send(places, cap, kept, grad):
    normed_low, inverse, probs, gate, arrived, pre, outputs = kept
    experts = arrived.shape[0] // cap
    d_rows = (gate[:, None] * grad).astype(jnp.bfloat16)
    buffer = dot_nn(dispatch(places, experts * cap), d_rows).astype(jnp.bfloat16)
    return swap_owners(buffer.reshape(experts, cap, D)).reshape(-1, D)


def moe_back_expert(weights, cap, kept, d_arrived):
    normed_low, inverse, probs, gate, arrived, pre, outputs = kept
    experts = arrived.shape[0] // cap
    d_weights, d_back = expert_backward(arrived, d_arrived, pre, weights)
    return d_weights, swap_owners(d_back.reshape(experts, cap, D)).reshape(-1, D)


def moe_back_receive(resid, gain, router, hot, places, kept, grad, returned, aux_scale, frac):
    normed_low, inverse, probs, gate, arrived, pre, outputs = kept
    d_gate = jnp.sum(grad * outputs, axis=1)
    d_probs = hot * d_gate[:, None] + aux_scale * frac[None, :]
    d_logits = probs * (d_probs - jnp.sum(probs * d_probs, axis=-1, keepdims=True))
    d_router = jnp.dot(normed_low.astype(jnp.float32).T, d_logits, precision=highest)
    d_normed = dot_tn(dispatch(places, returned.shape[0]), returned) + jnp.dot(
        d_logits, router.T, precision=highest
    )
    d_resid, d_gain = normalize_back(resid, inverse, gain, d_normed)
    return (grad + d_resid, d_gain, d_router)


def ranks_of(ids, size):
    count = ids.shape[0]
    here, there = ids[:, None], ids[None, :]
    before = lax.broadcasted_iota(jnp.int32, (count, count), 1) < lax.broadcasted_iota(
        jnp.int32, (count, count), 0
    )
    again = jnp.max(((here == there) & before).astype(jnp.int32), axis=1)
    owner = ids // size
    lower = (there < here) & (there >= (owner * size)[:, None]) & (again[None, :] == 0)
    return owner, jnp.sum(lower.astype(jnp.int32), axis=1)


def slots_of(owner, rank, owners, width, turn):
    slot = owner * width + rank - turn * width
    slot = jnp.where((rank >= turn * width) & (rank < (turn + 1) * width), slot, -1)
    return lax.broadcasted_iota(jnp.int32, (owners * width, rank.shape[0]), 0) == slot[None, :]


def ids_in(hot, local, width):
    return jnp.max(jnp.where(hot, local[None, :], -1), axis=1).reshape(-1, width)


def exchange(array, axes):
    return lax.all_to_all(array, axes, split_axis=0, concat_axis=0, tiled=True)


def rows_into(landed, rows, count):
    place = landed[None, :] == lax.broadcasted_iota(jnp.int32, (count, landed.shape[0]), 0)
    return dot_nn(place.astype(jnp.bfloat16), rows)


def in_lanes(parts):
    flat = jnp.concatenate([part.reshape(-1) for part in parts])
    rows = -(-flat.shape[0] // (8 * LANES)) * 8
    return jnp.pad(flat, (0, rows * LANES - flat.shape[0])).reshape(rows, LANES)


def from_lanes(array, parts):
    flat = array.reshape(-1)
    taken, out = 0, []
    for part in parts:
        out.append(flat[taken : taken + part.size].reshape(part.shape))
        taken += part.size
    return out


def self_forward(resid, gain, weights, parts, causal):
    normed, inverse = normalize(resid, gain)
    normed = normed.astype(jnp.bfloat16)
    joined = project(normed, weights[0:3]).astype(jnp.bfloat16)
    mixed, logsum = attend((joined, 0), (joined, 1), (joined, 2), parts, causal)
    return (resid + project(mixed, weights[3]), (resid, inverse, normed, joined, mixed, logsum))


def self_backward(gain, weights, parts, causal, kept, grad):
    resid, inverse, normed, joined, mixed, logsum = kept
    grad_low = grad.astype(jnp.bfloat16)
    d_mixed = dot_nn(grad_low, weights[3]).astype(jnp.bfloat16)
    d_query, d_key, d_value, sums = attend_back(
        (joined, 0), (joined, 1), (joined, 2), parts, causal, logsum, d_mixed
    )
    d_normed = (
        dot_nn(d_query, weights[0]) + dot_nn(d_key, weights[1]) + dot_nn(d_value, weights[2])
    )
    d_weights = [
        dot_tn(d_query, normed),
        dot_tn(d_key, normed),
        dot_tn(d_value, normed),
        dot_tn(grad_low, mixed),
    ]
    d_resid, d_gain = normalize_back(resid, inverse, gain, d_normed)
    return (grad + d_resid, d_gain, d_weights, bias_sums(sums, parts[2], parts[3]))


def cross_forward(resid, gain, weights, memory):
    normed, inverse = normalize(resid, gain)
    normed = normed.astype(jnp.bfloat16)
    query = project(normed, weights[0]).astype(jnp.bfloat16)
    joined = project(memory, weights[1:3]).astype(jnp.bfloat16)
    mixed, logsum = attend((query, 0), (joined, 0), (joined, 1), None, False)
    kept = (resid, inverse, normed, query, joined, mixed, logsum)
    return (resid + project(mixed, weights[3]), kept)


def cross_backward(gain, weights, memory, kept, grad):
    resid, inverse, normed, query, joined, mixed, logsum = kept
    grad_low = grad.astype(jnp.bfloat16)
    d_mixed = dot_nn(grad_low, weights[3]).astype(jnp.bfloat16)
    d_query, d_key, d_value = attend_back(
        (query, 0), (joined, 0), (joined, 1), None, False, logsum, d_mixed
    )
    d_normed = dot_nn(d_query, weights[0])
    d_memory = dot_nn(d_key, weights[1]) + dot_nn(d_value, weights[2])
    d_weights = [
        dot_tn(d_query, normed),
        dot_tn(d_key, memory),
        dot_tn(d_value, memory),
        dot_tn(grad_low, mixed),
    ]
    d_resid, d_gain = normalize_back(resid, inverse, gain, d_normed)
    return (grad + d_resid, d_gain, d_weights, d_memory)


def route_share(routes, experts):
    flat_routes = routes.reshape(-1)
    hot = (flat_routes[None, :] == jnp.arange(experts, dtype=jnp.int32)[:, None]).astype(
        jnp.float32
    )
    return jnp.sum(hot, axis=1) / flat_routes.shape[0]


def adam(weight, first, second, grad, rate, decay):
    first = beta_one * first + (1 - beta_one) * grad
    second = beta_two * second + (1 - beta_two) * grad * grad
    update = first / (1 - beta_one**STEP) / (jnp.sqrt(second / (1 - beta_two**STEP)) + eps_adam)
    return (weight - rate * (update + decay * weight), first, second)


def share_columns(d_weights, groups):
    split = jnp.concatenate(
        [part.astype(jnp.bfloat16).reshape(groups, -1, D) for part in d_weights], axis=1
    )
    summed = lax.psum_scatter(split.reshape(-1, D), "mp", scatter_dimension=0, tiled=True)
    return summed.reshape(len(d_weights), -1, D)


def on_device(
    src_ids,
    targets,
    loss_pos,
    loss_mask,
    routes_src,
    routes_tgt,
    dense_w,
    dense_m,
    expert_w,
    expert_m,
    table_w,
    table_m,
    table_v,
    gains_w,
    gains_m,
    gains_v,
    router_w,
    router_m,
    router_v,
    bias_w,
    bias_m,
    bias_v,
):
    groups = lax.axis_size("mp")
    column = lax.axis_index("mp")
    experts = lax.axis_size("dp")
    src_len = src_ids.shape[1]
    tgt_len = targets.shape[1]
    npos = loss_pos.shape[1]
    vocab_dev = table_w.shape[0]
    own_seq = lax.axis_index("dp") * groups + column
    count_dense = dense_w.shape[0]
    low = jnp.bfloat16
    dense_local = dense_w.astype(low).reshape(count_dense, -1, D)
    enc_dense = lax.all_gather(dense_local[0:4], "mp", axis=1, tiled=True)
    expert_local = expert_w[:, :, 0].astype(low)
    devices = experts * groups
    piece_rows = table_m.shape[0]
    own_src_ids = lax.dynamic_slice_in_dim(src_ids, column, 1, 0).reshape(-1)
    own_targets = lax.dynamic_slice_in_dim(targets, column, 1, 0).reshape(-1)
    own_ids = jnp.concatenate([own_src_ids, jnp.zeros((1,), jnp.int32), own_targets[:-1]])
    shard, rank = ranks_of(own_ids, vocab_dev)
    owner, owner_rank = ranks_of(own_ids, piece_rows)
    local_ids = own_ids - shard * vocab_dev
    piece_ids = own_ids - owner * piece_rows
    owner = (owner % experts) * groups + owner // experts
    fetch_turns = jnp.max(rank) // FETCH + 1
    give_turns = jnp.max(owner_rank) // GIVE + 1
    give_hot = (jnp.arange(piece_rows // GIVE + 2, dtype=jnp.int32) == give_turns).astype(
        jnp.float32
    )

    def asked_of(turn):
        return ids_in(slots_of(shard, rank, groups, FETCH, turn), local_ids, FETCH)

    def fetched(wanted):
        rows = lookup(wanted.reshape(-1), table_w)
        return exchange(rows.reshape(groups, FETCH, D), "mp").reshape(-1, D)

    def placed(turn, rows):
        hot = slots_of(shard, rank, groups, FETCH, turn).astype(low)
        return dot_tn(hot, rows).astype(low)

    noted = jnp.full((groups, LANES), fetch_turns)
    asked = exchange(jnp.concatenate([asked_of(0), noted], axis=1), "mp")
    fetch_turns = jnp.max(asked[:, FETCH:])
    rows = fetched(asked[:, :FETCH])

    def fetch_more(state):
        turn, more = state
        return turn + 1, more + placed(turn, fetched(exchange(asked_of(turn), "mp")))

    nothing = jnp.zeros((own_ids.shape[0], D), low)
    more = lax.cond(
        fetch_turns > 1,
        lambda: lax.while_loop(
            lambda state: state[0] < fetch_turns, fetch_more, (jnp.int32(1), nothing)
        )[1],
        lambda: nothing,
    )
    rows, more, enc_dense = lax.optimization_barrier((rows, more, enc_dense))
    embedded = (placed(0, rows) + more).astype(jnp.float32)
    enc_expert = lax.all_gather(expert_local[0], "mp", axis=0, tiled=False)
    own_src = lax.dynamic_slice_in_dim(routes_src, own_seq, 1, 0).reshape(-1)
    own_tgt = lax.dynamic_slice_in_dim(routes_tgt, own_seq, 1, 0).reshape(-1)
    cap_src = (5 * src_len + 4 * experts - 1) // (4 * experts)
    cap_tgt = (5 * tgt_len + 4 * experts - 1) // (4 * experts)
    total_src = routes_src.shape[0] * routes_src.shape[1]
    total_tgt = routes_tgt.shape[0] * routes_tgt.shape[1]
    frac_src = route_share(routes_src, experts)
    frac_tgt = route_share(routes_tgt, experts)
    hot_src, places_src = route_places(own_src, experts, cap_src)
    hot_tgt, places_tgt = route_places(own_tgt, experts, cap_tgt)
    enc_parts = bias_parts(bias_w[0], False)
    dec_parts = bias_parts(bias_w[1], True)
    enc_mid, enc_kept = self_forward(embedded[:src_len], gains_w[0], enc_dense, enc_parts, False)
    dec_local, late_table, enc_mid = lax.optimization_barrier((dense_local[4:8], table_w, enc_mid))
    arrived, enc_sent = moe_send(enc_mid, gains_w[1], router_w[0], hot_src, places_src, cap_src)
    dec_dense = lax.all_gather(dec_local, "mp", axis=1, tiled=True)
    arrived, enc_expert, cross_local, dec_expert_local = lax.optimization_barrier(
        (arrived, enc_expert, dense_local[8:12], expert_local[1])
    )
    cross_dense = lax.all_gather(cross_local, "mp", axis=1, tiled=True)
    dec_expert = lax.all_gather(dec_expert_local, "mp", axis=0, tiled=False)
    padded = -(-piece_rows // 16) * 16
    table_low = jnp.pad(
        late_table.astype(low).reshape(experts, piece_rows, D),
        ((0, 0), (0, padded - piece_rows), (0, 0)),
    ).reshape(-1, D)
    pre, returned = moe_expert(enc_expert, cap_src, arrived)
    dec_mid, dec_kept = self_forward(embedded[src_len:], gains_w[3], dec_dense, dec_parts, True)
    returned, dec_mid, table_low = lax.optimization_barrier((returned, dec_mid, table_low))
    enc_out, enc_moe = moe_receive(enc_mid, places_src, arrived, pre, returned, enc_sent)
    memory_float, memory_inv = normalize(enc_out, gains_w[2])
    memory = memory_float.astype(low)
    dec_crossed, cross_kept = cross_forward(dec_mid, gains_w[4], cross_dense, memory)
    arrived, dec_sent = moe_send(
        dec_crossed, gains_w[5], router_w[1], hot_tgt, places_tgt, cap_tgt
    )
    pre, returned = moe_expert(dec_expert, cap_tgt, arrived)
    dec_result, dec_moe = moe_receive(dec_crossed, places_tgt, arrived, pre, returned, dec_sent)
    final_float, final_inv = normalize(dec_result, gains_w[6])
    final_low = final_float.astype(low)
    head_scale = D ** (-0.5)
    own_pos = lax.dynamic_slice_in_dim(loss_pos, column, 1, 0).reshape(-1)
    pick = (
        own_pos[:, None] == lax.broadcasted_iota(jnp.int32, (npos, tgt_len), 1)
    ).astype(low)
    chosen = dot_nn(pick, final_low).astype(low)
    gathered = gathered_over(chosen, groups, 5).reshape(-1, D)
    place = jnp.arange(experts * padded, dtype=jnp.int32)
    logits = jnp.where(
        (place % padded < piece_rows)[None, :], dot_nt(gathered, table_low) * head_scale, -1e30
    )
    at_pos = loss_pos[:, :, None] == lax.broadcasted_iota(jnp.int32, (1, 1, tgt_len), 2)
    wanted = jnp.sum(jnp.where(at_pos, targets[:, None, :], 0), axis=2).reshape(-1)
    wanted = wanted - column * vocab_dev
    here = (wanted >= 0) & (wanted < vocab_dev)
    wanted = jnp.where(here, wanted + wanted // piece_rows * (padded - piece_rows), -1)
    hits = place[None, :] == wanted[:, None]
    top = jnp.max(logits, axis=1)
    stats = gathered_over(
        jnp.stack(
            [
                top,
                jnp.sum(jnp.exp(logits - top[:, None]), axis=1),
                jnp.sum(jnp.where(hits, logits, 0.0), axis=1),
            ]
            + [jnp.zeros_like(top)] * 5
        ),
        groups,
        6,
    )
    all_top = jnp.max(stats[:, 0], axis=0)
    expsum = jnp.sum(stats[:, 1] * jnp.exp(stats[:, 0] - all_top[None, :]), axis=0)
    picked = jnp.sum(stats[:, 2], axis=0)
    logsum = all_top + jnp.log(expsum)
    mask_rows = loss_mask.reshape(-1).astype(jnp.float32)
    own_loss = jnp.sum(
        lax.dynamic_slice_in_dim(mask_rows * (logsum - picked), column * npos, npos)
    )
    own_count = jnp.sum(lax.dynamic_slice_in_dim(mask_rows, column * npos, npos))
    d_logits = (
        mask_rows[:, None] * (jnp.exp(logits - logsum[:, None]) - hits.astype(jnp.float32))
    ).astype(low)
    d_gathered = (dot_nn(d_logits, table_low) * head_scale).astype(low)
    d_gathered, d_logits = lax.optimization_barrier((d_gathered, d_logits))
    d_shares = exchange(d_gathered.reshape(groups, npos, D), "mp")
    table_grad = (dot_tn(d_logits, gathered) * head_scale).astype(low)
    d_shares, table_grad = lax.optimization_barrier((d_shares, table_grad))
    table_share = lax.psum_scatter(table_grad, "dp", scatter_dimension=0, tiled=True)
    d_chosen = jnp.sum(d_shares.astype(jnp.float32), axis=0).astype(low)
    d_final = dot_tn(pick, d_chosen)
    d_dec, gain_final = normalize_back(dec_result, final_inv, gains_w[6], d_final)
    d_arrived = moe_back_send(places_tgt, cap_tgt, dec_moe, d_dec)
    dec_dw, returned = moe_back_expert(dec_expert, cap_tgt, dec_moe, d_arrived)
    dec_share = lax.psum_scatter(dec_dw, "mp", scatter_dimension=0, tiled=False)
    d_dec, gain_dec_moe, dec_router = moe_back_receive(
        dec_crossed,
        gains_w[5],
        router_w[1],
        hot_tgt,
        places_tgt,
        dec_moe,
        d_dec,
        returned,
        aux_weight * experts / total_tgt,
        frac_tgt,
    )
    d_dec, gain_cross, cross_dw, d_memory = cross_backward(
        gains_w[4], cross_dense, memory, cross_kept, d_dec
    )
    d_enc, gain_memory = normalize_back(enc_out, memory_inv, gains_w[2], d_memory)
    d_arrived = moe_back_send(places_src, cap_src, enc_moe, d_enc)
    d_dec, gain_self, self_dw, dec_bias = self_backward(
        gains_w[3], dec_dense, dec_parts, True, dec_kept, d_dec
    )
    d_arrived, d_dec, table_share = lax.optimization_barrier((d_arrived, d_dec, table_share))
    enc_dw, returned = moe_back_expert(enc_expert, cap_src, enc_moe, d_arrived)
    dec_cols = share_columns(self_dw + cross_dw, groups)
    enc_share = lax.psum_scatter(enc_dw, "mp", scatter_dimension=0, tiled=False)
    d_enc, gain_enc_moe, enc_router = moe_back_receive(
        enc_mid,
        gains_w[1],
        router_w[0],
        hot_src,
        places_src,
        enc_moe,
        d_enc,
        returned,
        aux_weight * experts / total_src,
        frac_src,
    )
    d_enc, dec_share = lax.optimization_barrier((d_enc, dec_share))
    d_enc, gain_enc, enc_self_dw, enc_bias = self_backward(
        gains_w[0], enc_dense, enc_parts, False, enc_kept, d_enc
    )
    enc_parts = jnp.stack(
        [
            jnp.swapaxes(part.astype(low).reshape(groups // 2, 2, -1, D), 0, 1)
            for part in enc_self_dw
        ],
        axis=2,
    )
    d_embedded = jnp.concatenate([d_enc, d_dec], axis=0).astype(low)

    def given_ids(turn):
        hot = slots_of(owner, owner_rank, devices, GIVE, turn)
        return exchange(ids_in(hot, piece_ids, GIVE), ("dp", "mp")).reshape(-1)

    def given_rows(turn):
        hot = slots_of(owner, owner_rank, devices, GIVE, turn).astype(low)
        rows = dot_nn(hot, d_embedded).astype(low).reshape(devices, GIVE, D)
        return exchange(rows, ("dp", "mp")).reshape(-1, D)

    landed, d_embedded = lax.optimization_barrier((given_ids(0), d_embedded))
    arrived = given_rows(0)
    gains_grad = jnp.stack(
        [gain_enc, gain_enc_moe, gain_memory, gain_self, gain_cross, gain_dec_moe, gain_final]
    )
    router_grad = jnp.stack([enc_router, dec_router])
    bias_grad = jnp.stack([enc_bias, dec_bias])
    load_src = jnp.sum(enc_moe[2], axis=0)
    load_tgt = jnp.sum(dec_moe[2], axis=0)
    small = [
        gains_grad,
        router_grad,
        bias_grad,
        load_src,
        load_tgt,
        own_loss,
        own_count,
        give_hot,
    ]
    dense_piece, summed = dense_total(enc_parts, dec_cols, in_lanes(small), groups, experts)
    arrived, summed, dense_piece = lax.optimization_barrier((arrived, summed, dense_piece))
    table_piece = rows_into(landed, arrived, piece_rows)
    gains_grad, router_grad, bias_grad, load_src, load_tgt, loss_sum, count, give_hot = from_lanes(
        summed, small
    )
    give_turns = jnp.max(
        jnp.where(give_hot > 0.0, jnp.arange(give_hot.shape[0], dtype=jnp.int32), 0)
    )

    def give_more(state):
        turn, total = state
        return turn + 1, total + rows_into(given_ids(turn), given_rows(turn), piece_rows)

    turns, table_piece = lax.while_loop(
        lambda state: state[0] < give_turns, give_more, (jnp.int32(1), table_piece)
    )

    table_piece = table_piece + table_share[:piece_rows].astype(jnp.float32)
    expert_share = jnp.stack([enc_share, dec_share])
    own_squares = sum((jnp.sum(part * part) for part in (gains_grad, router_grad, bias_grad)))
    squares = jnp.full((8, LANES), own_squares / (8 * LANES * devices))
    for part in (dense_piece, expert_share, table_piece):
        lanes = jnp.sum(jnp.square(part.astype(jnp.float32)).reshape(-1, part.shape[-1]), axis=0)
        width = math.gcd(lanes.shape[0], LANES)
        lanes = jnp.pad(jnp.sum(lanes.reshape(-1, width), axis=0), (0, LANES - width))
        squares = squares + lanes[None, :] * 0.125
    cols = expert_w.shape[4]
    old_piece = piece_of(dense_m, 4, experts).reshape(dense_piece.shape)
    squares, expert_moment, expert_orth, dense_orth, dense_moment = newton(
        squares,
        expert_m.reshape(-1, D, cols),
        expert_share.reshape(-1, D, cols),
        old_piece,
        dense_piece,
        groups,
        experts,
    )
    expert_moment = expert_moment.reshape(expert_w.shape)
    squares = jnp.sum(squares)
    grad_norm = jnp.sqrt(squares)
    clip = 1.0 / jnp.maximum(grad_norm, 1.0)
    aux = (
        aux_weight
        * experts
        * (jnp.sum(frac_src * load_src) / total_src + jnp.sum(frac_tgt * load_tgt) / total_tgt)
    )
    loss = jnp.stack([loss_sum + aux, count])

    def as_stored(pieces):
        return whole_of(pieces, 4, count_dense - 4).reshape(count_dense, -1).astype(jnp.float32)

    dense_moment, dense_orth = as_stored(dense_moment), as_stored(dense_orth)
    keep_rate = 1 - rate_matrix * decay_matrix
    dense_new = dense_w * keep_rate - rate_matrix * 0.2 * math.sqrt(D) * dense_orth
    expert_new = expert_w * keep_rate - rate_matrix * 0.2 * math.sqrt(
        max(D, FF)
    ) * expert_orth.astype(jnp.float32).reshape(expert_w.shape)
    table_clipped = clip * table_piece
    table_new, table_first, table_second = adam(
        lax.dynamic_slice_in_dim(table_w, lax.axis_index("dp") * piece_rows, piece_rows, 0),
        table_m,
        table_v,
        table_clipped,
        1.5,
        0.01,
    )

    def part_of(array, like):
        size = like.shape[1]
        return lax.dynamic_slice_in_dim(array, column * size, size, 1)

    gains_new, gains_first, gains_second = adam(
        part_of(gains_w, gains_m), gains_m, gains_v, clip * part_of(gains_grad, gains_m), 0.5, 0.0
    )
    router_new, router_first, router_second = adam(
        part_of(router_w, router_m),
        router_m,
        router_v,
        clip * part_of(router_grad, router_m),
        0.02,
        0.01,
    )
    bias_new, bias_first, bias_second = adam(
        part_of(bias_w, bias_m), bias_m, bias_v, clip * part_of(bias_grad, bias_m), 0.5, 0.0
    )
    return (
        loss,
        grad_norm,
        dense_new,
        dense_moment,
        dense_new.astype(low),
        expert_new,
        expert_moment,
        expert_new.astype(low),
        table_new,
        table_clipped,
        table_second,
        gains_new,
        gains_first,
        gains_second,
        router_new,
        router_first,
        router_second,
        bias_new,
        bias_first,
        bias_second,
    )


def solution(mesh):
    in_specs = (
        P("dp", None),
        P("dp", None),
        P("dp", None),
        P("dp", None),
        P(),
        P(),
        P(None, "mp"),
        P(None, "mp"),
        P(None, None, "dp", None, "mp"),
        P(None, None, "dp", None, "mp"),
        P("mp", None),
        P(("mp", "dp"), None),
        P(("mp", "dp"), None),
        P(),
        P(None, "mp"),
        P(None, "mp"),
        P(),
        P(None, "mp", None),
        P(None, "mp", None),
        P(),
        P(None, "mp", None),
        P(None, "mp", None),
    )
    out_specs = (
        P(),
        P(),
        P(None, "mp"),
        P(None, "mp"),
        P(None, "mp"),
        P(None, None, "dp", None, "mp"),
        P(None, None, "dp", None, "mp"),
        P(None, None, "dp", None, "mp"),
        P(("mp", "dp"), None),
        P(("mp", "dp"), None),
        P(("mp", "dp"), None),
        P(None, "mp"),
        P(None, "mp"),
        P(None, "mp"),
        P(None, "mp", None),
        P(None, "mp", None),
        P(None, "mp", None),
        P(None, "mp", None),
        P(None, "mp", None),
        P(None, "mp", None),
    )
    return jax.shard_map(
        on_device, mesh=mesh, in_specs=in_specs, out_specs=out_specs, check_vma=False
    )
```

```python
from functools import partial
import math

import jax
import jax.numpy as jnp
from jax import lax
from jax.experimental import pallas as pl
from jax.experimental.pallas import tpu as pltpu
from jax.sharding import PartitionSpec as P

D = 768
HEADS = 12
HD = 64
FF = 3072
NS_ITERS = 5
STEP = 10


eps_norm = 1e-06
eps_gram = 1e-07
eps_adam = 1e-08
neg_fill = -1000000000.0
coef_a = 3.4445
coef_b = -4.775
coef_c = 2.0315
beta_one = 0.9
beta_two = 0.95
rate_matrix = 0.2
decay_matrix = 0.01
aux_weight = 0.01
enc_edges = (12, 16, 23, 32, 46, 64, 91)
dec_edges = (19, 21, 24, 27, 31, 35, 40, 46, 52, 59, 67, 77, 87, 99, 113)
highest = lax.Precision.HIGHEST


def normalize(rows, gain):
    inverse = lax.rsqrt(jnp.mean(rows * rows, axis=-1, keepdims=True) + eps_norm)
    return (rows * inverse * gain, inverse)


def normalize_back(rows, inverse, gain, grad):
    scaled = grad * gain
    d_rows = inverse * scaled - rows * inverse**3 * jnp.mean(scaled * rows, axis=-1, keepdims=True)
    return (d_rows, jnp.sum(grad * rows * inverse, axis=0))


def bucket_of(relative, causal):
    if causal:
        distance = jnp.maximum(-relative, 0)
        far = 16 + sum(((distance >= edge).astype(jnp.int32) for edge in dec_edges))
        return jnp.where(distance < 16, distance, far)
    distance = jnp.abs(relative)
    far = 8 + sum(((distance >= edge).astype(jnp.int32) for edge in enc_edges))
    return jnp.where(distance < 8, distance, far) + 16 * (relative > 0).astype(jnp.int32)


LANES = 128
CHUNK = 768
WIDE = 768
FETCH = 128
GIVE = 48
VMEM_LIMIT = 60 * 1024 * 1024


def params(count=1, **more):
    return pltpu.CompilerParams(
        dimension_semantics=("arbitrary",) * count, vmem_limit_bytes=VMEM_LIMIT, **more
    )


def dot_nn(left, right):
    return lax.dot_general(
        left, right, (((1,), (0,)), ((), ())), preferred_element_type=jnp.float32
    )


def dot_nt(left, right):
    return lax.dot_general(
        left, right, (((1,), (1,)), ((), ())), preferred_element_type=jnp.float32
    )


def dot_tn(left, right):
    return lax.dot_general(
        left, right, (((0,), (0,)), ((), ())), preferred_element_type=jnp.float32
    )


def own_lanes(rows, half):
    lane = lax.broadcasted_iota(jnp.int32, rows.shape, 1)
    keep = lane >= HD if half else lane < HD
    return jnp.where(keep, rows, jnp.zeros_like(rows))


def band_offsets():
    place = jnp.arange(4 * LANES, dtype=jnp.int32)
    return LANES - jnp.where(place < 3 * LANES, place, place - 4 * LANES)


def bias_parts(table, causal):
    count = table.shape[0]
    hot = (
        bucket_of(band_offsets(), causal)[:, None] == jnp.arange(count, dtype=jnp.int32)[None, :]
    ).astype(jnp.float32)
    band = jnp.dot(hot, table, precision=highest).T[:, None, :]
    ends = bucket_of(jnp.array([-2 * LANES, 2 * LANES], jnp.int32), causal)
    hot_ends = (ends[:, None] == jnp.arange(count, dtype=jnp.int32)[None, :]).astype(jnp.float32)
    far = jnp.dot(hot_ends, table, precision=highest)
    return band, far, hot, hot_ends


def bias_sums(sums, hot, hot_ends):
    per_place = sums[:, 0, :]
    near = per_place[:, : 4 * LANES]
    far = jnp.sum(per_place[:, 4 * LANES :].reshape(-1, 2, LANES), axis=2)
    return jnp.dot(hot.T, near.T, precision=highest) + jnp.dot(
        hot_ends.T, far.T, precision=highest
    )


def scores_of(keys, queries, head, chunk, far_ref, band, causal):
    scores = dot_nt(keys, queries)
    len_k, width = scores.shape
    if band is not None:
        rows = []
        for a in range(len_k // LANES):
            columns = []
            for b in range(width // LANES):
                apart = a - (chunk * (width // LANES) + b)
                if apart < -1:
                    bias = far_ref[0, head]
                elif apart > 1:
                    bias = far_ref[1, head]
                else:
                    bias = band[:, LANES * (1 - apart) : LANES * (2 - apart)]
                columns.append(
                    scores[LANES * a : LANES * a + LANES, LANES * b : LANES * b + LANES] + bias
                )
            rows.append(jnp.concatenate(columns, axis=1))
        scores = jnp.concatenate(rows, axis=0)
    if causal:
        allowed = lax.broadcasted_iota(jnp.int32, scores.shape, 0) <= (
            lax.broadcasted_iota(jnp.int32, scores.shape, 1) + chunk * width
        )
        scores = jnp.where(allowed, scores, neg_fill)
    return scores


def band_of(band_ref, half):
    row = jnp.broadcast_to(band_ref[half], (LANES, 4 * LANES))
    return pltpu.roll(row, 0, 1, stride=1, stride_axis=0)


def unband(sums):
    row = lax.broadcasted_iota(jnp.int32, sums.shape, 0)
    step = 1
    while step < LANES:
        sums = jnp.where(
            (row & step) != 0, pltpu.roll(sums, sums.shape[1] - step, 1), sums
        )
        step *= 2
    return jnp.sum(sums, axis=0, keepdims=True)


def attend_kernel(biased, causal, *refs):
    if biased:
        far_ref, band_ref, *refs = refs
    q_ref, k_ref, v_ref, out_ref, lse_ref = refs
    pair = pl.program_id(0)
    keys = k_ref[...]
    values_t = v_ref[...].T
    len_q = q_ref.shape[0]
    width = min(CHUNK, len_q)
    bands = [band_of(band_ref, half) if biased else None for half in range(2)]
    for chunk in range(len_q // width):
        span = pl.ds(chunk * width, width)
        queries = q_ref[span, :] * HD ** (-0.5)
        parts = []
        for half in range(2):
            scores = scores_of(
                keys,
                own_lanes(queries, half),
                2 * pair + half,
                chunk,
                far_ref if biased else None,
                bands[half],
                causal,
            )
            top = jnp.max(scores, axis=0, keepdims=True)
            expo = jnp.exp(scores - top)
            total = jnp.sum(expo, axis=0, keepdims=True)
            mixed = dot_nn(values_t[HD * half : HD * half + HD], expo.astype(jnp.bfloat16))
            parts.append(mixed * (1.0 / total))
            lse_ref[half, :, span] = top + jnp.log(total)
        out_ref[span, :] = jnp.concatenate(parts, axis=0).T.astype(jnp.bfloat16)


def attend_back_kernel(biased, causal, *refs):
    if biased:
        far_ref, band_ref, *refs = refs
    q_ref, k_ref, v_ref, g_ref, lse_ref, dq_ref, dk_ref, dv_ref, *refs = refs
    if biased:
        sums_ref, dk_acc, dv_acc, near_acc, far_acc = refs
    else:
        dk_acc, dv_acc = refs
    pair = pl.program_id(0)
    keys = k_ref[...]
    keys_t = keys.T
    values = v_ref[...]
    len_q, len_k = q_ref.shape[0], k_ref.shape[0]
    width = min(CHUNK, len_q)
    scale = HD ** (-0.5)
    dk_acc[...] = jnp.zeros_like(dk_acc)
    dv_acc[...] = jnp.zeros_like(dv_acc)
    bands = [band_of(band_ref, half) if biased else None for half in range(2)]
    if biased:
        near_acc[...] = jnp.zeros_like(near_acc)
        far_acc[...] = jnp.zeros_like(far_acc)
    for chunk in range(len_q // width):
        span = pl.ds(chunk * width, width)
        parts = []
        for half in range(2):
            queries = own_lanes(q_ref[span, :] * HD ** (-0.5), half)
            grads = own_lanes(g_ref[span, :], half)
            scores = scores_of(
                keys,
                queries,
                2 * pair + half,
                chunk,
                far_ref if biased else None,
                bands[half],
                causal,
            )
            probs = jnp.exp(scores - lse_ref[half, :, span])
            d_probs = dot_nt(values, grads)
            delta = jnp.sum(probs * d_probs, axis=0, keepdims=True)
            d_scores = (probs * (d_probs - delta)).astype(jnp.bfloat16)
            dk_acc[...] += dot_nn(d_scores, queries)
            dv_acc[...] += dot_nn(probs.astype(jnp.bfloat16), grads)
            parts.append(dot_nn(keys_t[HD * half : HD * half + HD], d_scores))
            if biased:
                groups = {}
                for a in range(len_k // LANES):
                    for b in range(width // LANES):
                        apart = a - (chunk * (width // LANES) + b)
                        if causal and apart > 0:
                            continue
                        groups.setdefault(max(-2, min(2, apart)), []).append(
                            d_scores[
                                LANES * a : LANES * a + LANES, LANES * b : LANES * b + LANES
                            ].astype(jnp.float32)
                        )
                for apart, blocks in groups.items():
                    total = sum(blocks[1:], blocks[0])
                    if abs(apart) < 2:
                        near_acc[half, :, LANES * (1 - apart) : LANES * (2 - apart)] += total
                    else:
                        side = 0 if apart < 0 else 1
                        far_acc[half, :, LANES * side : LANES * side + LANES] += total
        dq_ref[span, :] = (jnp.concatenate(parts, axis=0).T * scale).astype(jnp.bfloat16)
    dk_ref[...] = dk_acc[...].astype(jnp.bfloat16)
    dv_ref[...] = dv_acc[...].astype(jnp.bfloat16)
    if biased:
        for half in range(2):
            sums_ref[half, :, : 4 * LANES] = unband(near_acc[half])
            sums_ref[half, :, 4 * LANES :] = jnp.sum(far_acc[half], axis=0, keepdims=True)


def pair_spec(rows, shift):
    return pl.BlockSpec((rows, LANES), lambda pair, shift=shift: (0, shift + pair))


def row_spec(width):
    return pl.BlockSpec((2, 1, width), lambda pair: (pair, 0, 0))


def attend_cost(len_q, len_k, dots):
    return pl.CostEstimate(
        flops=2 * dots * HEADS * len_q * len_k * HD,
        bytes_accessed=8 * D * (len_q + len_k),
        transcendentals=HEADS * len_q * len_k,
    )


def attend(query, keys, values, parts, causal):
    len_q, len_k = query[0].shape[0], keys[0].shape[0]
    biased = parts is not None
    pairs = D // LANES
    first = [parts[1], parts[0]] if biased else []
    first_specs = [pl.BlockSpec(memory_space=pltpu.SMEM), row_spec(4 * LANES)] if biased else []
    return pl.pallas_call(
        partial(attend_kernel, biased, causal),
        grid=(pairs,),
        in_specs=first_specs
        + [
            pair_spec(len_q, query[1] * pairs),
            pair_spec(len_k, keys[1] * pairs),
            pair_spec(len_k, values[1] * pairs),
        ],
        out_specs=[pair_spec(len_q, 0), row_spec(len_q)],
        out_shape=[
            jax.ShapeDtypeStruct((len_q, D), jnp.bfloat16),
            jax.ShapeDtypeStruct((HEADS, 1, len_q), jnp.float32),
        ],
        compiler_params=params(),
        cost_estimate=attend_cost(len_q, len_k, 2),
    )(*first, query[0], keys[0], values[0])


def attend_back(query, keys, values, parts, causal, logsum, d_mixed):
    len_q, len_k = query[0].shape[0], keys[0].shape[0]
    biased = parts is not None
    pairs = D // LANES
    first = [parts[1], parts[0]] if biased else []
    first_specs = [pl.BlockSpec(memory_space=pltpu.SMEM), row_spec(4 * LANES)] if biased else []
    low = jnp.bfloat16
    return pl.pallas_call(
        partial(attend_back_kernel, biased, causal),
        grid=(pairs,),
        in_specs=first_specs
        + [
            pair_spec(len_q, query[1] * pairs),
            pair_spec(len_k, keys[1] * pairs),
            pair_spec(len_k, values[1] * pairs),
            pair_spec(len_q, 0),
            row_spec(len_q),
        ],
        out_specs=[pair_spec(len_q, 0), pair_spec(len_k, 0), pair_spec(len_k, 0)]
        + ([row_spec(6 * LANES)] if biased else []),
        out_shape=[
            jax.ShapeDtypeStruct((len_q, D), low),
            jax.ShapeDtypeStruct((len_k, D), low),
            jax.ShapeDtypeStruct((len_k, D), low),
        ]
        + ([jax.ShapeDtypeStruct((HEADS, 1, 6 * LANES), jnp.float32)] if biased else []),
        scratch_shapes=[
            pltpu.VMEM((len_k, LANES), jnp.float32),
            pltpu.VMEM((len_k, LANES), jnp.float32),
        ]
        + (
            [
                pltpu.VMEM((2, LANES, 4 * LANES), jnp.float32),
                pltpu.VMEM((2, LANES, 2 * LANES), jnp.float32),
            ]
            if biased
            else []
        ),
        compiler_params=params(),
        cost_estimate=attend_cost(len_q, len_k, 5),
    )(*first, query[0], keys[0], values[0], d_mixed, logsum)


gelu_scale = math.sqrt(2.0 / math.pi)
gelu_cube = 0.044715


def side_by_side(ref):
    return jnp.concatenate([ref[j, 0] for j in range(ref.shape[0])], axis=1)


def expert_kernel(x_ref, wi_ref, wo_ref, pre_ref, out_ref, acc_ref):
    block = pl.program_id(0)
    pre = dot_nn(x_ref[...], side_by_side(wi_ref))
    pre_ref[0] = pre
    bend = jnp.tanh(gelu_scale * (pre + gelu_cube * (pre * pre * pre)))
    hidden = (0.5 * pre * (1.0 + bend)).astype(jnp.bfloat16)
    part = dot_nt(hidden, side_by_side(wo_ref))

    @pl.when(block == 0)
    def _():
        acc_ref[...] = part

    @pl.when(block > 0)
    def _():
        acc_ref[...] += part

    @pl.when(block == pl.num_programs(0) - 1)
    def _():
        out_ref[...] = acc_ref[...].astype(jnp.bfloat16)


def expert_forward(arrived, weights):
    rows = arrived.shape[0]
    blocks, unused, unused_too, cols = weights.shape
    per = WIDE // cols
    whole = pl.BlockSpec((rows, D), lambda j: (0, 0))
    return pl.pallas_call(
        expert_kernel,
        grid=(blocks // per,),
        in_specs=[
            whole,
            pl.BlockSpec((per, 1, D, cols), lambda j: (j, 0, 0, 0)),
            pl.BlockSpec((per, 1, D, cols), lambda j: (j, 1, 0, 0)),
        ],
        out_specs=[pl.BlockSpec((1, rows, WIDE), lambda j: (j, 0, 0)), whole],
        out_shape=[
            jax.ShapeDtypeStruct((blocks // per, rows, WIDE), jnp.float32),
            jax.ShapeDtypeStruct((rows, D), jnp.bfloat16),
        ],
        scratch_shapes=[pltpu.VMEM((rows, D), jnp.float32)],
        compiler_params=params(),
        cost_estimate=pl.CostEstimate(
            flops=4 * rows * D * FF,
            bytes_accessed=4 * D * FF + 4 * rows * (FF + D),
            transcendentals=rows * FF,
        ),
    )(arrived, weights, weights)


def expert_back_kernel(x_ref, g_ref, pre_ref, wi_ref, wo_ref, dw_ref, back_ref, acc_ref):
    block = pl.program_id(0)
    arrived = x_ref[...]
    grads = g_ref[...]
    pre = pre_ref[0]
    square = pre * pre
    bend = jnp.tanh(gelu_scale * (pre + gelu_cube * (square * pre)))
    half = 0.5 * (1.0 + bend)
    hidden = (pre * half).astype(jnp.bfloat16)
    slope = half + 0.5 * pre * (1.0 - bend * bend) * (
        gelu_scale * (1.0 + 3.0 * gelu_cube * square)
    )
    d_pre = (dot_nn(grads, side_by_side(wo_ref)) * slope).astype(jnp.bfloat16)
    d_in = dot_tn(arrived, d_pre).astype(jnp.bfloat16)
    d_out = dot_tn(grads, hidden).astype(jnp.bfloat16)
    cols = dw_ref.shape[3]
    for j in range(dw_ref.shape[0]):
        dw_ref[j, 0] = d_in[:, cols * j : cols * j + cols]
        dw_ref[j, 1] = d_out[:, cols * j : cols * j + cols]
    part = dot_nt(d_pre, side_by_side(wi_ref))

    @pl.when(block == 0)
    def _():
        acc_ref[...] = part

    @pl.when(block > 0)
    def _():
        acc_ref[...] += part

    @pl.when(block == pl.num_programs(0) - 1)
    def _():
        back_ref[...] = acc_ref[...].astype(jnp.bfloat16)


def expert_backward(arrived, d_arrived, pre, weights):
    rows = arrived.shape[0]
    blocks, unused, unused_too, cols = weights.shape
    per = WIDE // cols
    whole = pl.BlockSpec((rows, D), lambda j: (0, 0))
    return pl.pallas_call(
        expert_back_kernel,
        grid=(blocks // per,),
        in_specs=[
            whole,
            whole,
            pl.BlockSpec((1, rows, WIDE), lambda j: (j, 0, 0)),
            pl.BlockSpec((per, 1, D, cols), lambda j: (j, 0, 0, 0)),
            pl.BlockSpec((per, 1, D, cols), lambda j: (j, 1, 0, 0)),
        ],
        out_specs=[pl.BlockSpec((per, 2, D, cols), lambda j: (j, 0, 0, 0)), whole],
        out_shape=[
            jax.ShapeDtypeStruct((blocks, 2, D, cols), jnp.bfloat16),
            jax.ShapeDtypeStruct((rows, D), jnp.bfloat16),
        ],
        scratch_shapes=[pltpu.VMEM((rows, D), jnp.float32)],
        compiler_params=params(),
        cost_estimate=pl.CostEstimate(
            flops=8 * rows * D * FF,
            bytes_accessed=8 * D * FF + 4 * rows * (FF + 2 * D),
            transcendentals=rows * FF,
        ),
    )(arrived, d_arrived, pre, weights, weights)


def mirror(left, right, store):
    tile = 2 * LANES
    for a in range(0, D, tile):
        block = dot_nt(left[a : a + tile, :], right[: a + tile, :])
        store(slice(a, a + tile), slice(0, a + tile), block)
        if a:
            store(slice(0, a), slice(a, a + tile), block[:, :a].T)


def newton_gram(source, gram_ref):
    def keep(rows, columns, block):
        gram_ref[rows, columns] = block

    mirror(source, source, keep)


def newton_poly(product, poly_ref):
    def keep(rows, columns, block):
        poly_ref[rows, columns] = (
            coef_b * product[rows, columns].astype(jnp.float32) + coef_c * block
        ).astype(jnp.bfloat16)

    mirror(product, product, keep)


def newton_apply(source, poly_ref, j, outer):
    part = source[:, D * j : D * j + D]
    fresh = coef_a * part.astype(jnp.float32) + dot_nn(poly_ref[...], part)
    if outer is not None:
        fresh = fresh * outer
    source[:, D * j : D * j + D] = fresh.astype(jnp.bfloat16)


def newton_rounds(source, gram_ref, poly_ref, between, finish):
    blocks = source.shape[1] // D
    newton_gram(source, gram_ref)
    row = lax.broadcasted_iota(jnp.int32, (D, D), 0)
    column = lax.broadcasted_iota(jnp.int32, (D, D), 1)
    whole = gram_ref[...].astype(jnp.bfloat16).astype(jnp.float32)
    scale = jnp.sum(jnp.where(row == column, whole, 0.0), keepdims=True) + eps_gram
    newton_poly((whole * (1.0 / scale)).astype(jnp.bfloat16), poly_ref)
    for j in range(blocks):
        newton_apply(source, poly_ref, j, lax.rsqrt(scale))

    def turn(index, carry):
        newton_gram(source, gram_ref)
        newton_poly(gram_ref[...].astype(jnp.bfloat16), poly_ref)
        for j in range(blocks):
            newton_apply(source, poly_ref, j, None)
        return carry

    lax.fori_loop(1, NS_ITERS - 1, turn, 0)
    between()
    newton_gram(source, gram_ref)
    newton_poly(gram_ref[...].astype(jnp.bfloat16), poly_ref)
    for j in range(blocks):
        newton_apply(source, poly_ref, j, None)
        finish(j)


def newton_kernel(
    groups,
    experts,
    squares_ref,
    expert_old_ref,
    expert_grad_ref,
    dense_old_ref,
    dense_grad_ref,
    squares_out,
    expert_moment_out,
    expert_out,
    dense_out,
    moment_out,
    expert_ref,
    dense_ref,
    squares_row,
    squares_sum,
    squares_col,
    held,
    held_dense,
    matrix,
    square,
    gram_ref,
    poly_ref,
    land_expert,
    land_dense,
    all_dense,
    all_moment,
    send_sem,
    in_sem,
    back_send_sem,
    back_sem,
    orth_send_sem,
    orth_sem,
    moment_send_sem,
    moment_sem,
    row_send_sem,
    row_sem,
    col_send_sem,
    col_sem,
):
    me = lax.axis_index("mp")
    along = lax.axis_index("dp")
    own = me // 2
    count_expert, count_dense = expert_ref.shape[0], dense_ref.shape[0]
    cols, cols_dense = expert_ref.shape[2], dense_ref.shape[1]
    is_expert = ((me % 2) == 0) & (own < count_expert)
    is_dense = ((me % 2) == 1) & (own < count_dense)
    per = D // cols
    barrier = pltpu.get_barrier_semaphore()
    for step in range(1, groups):
        other = lax.rem(me + step, groups)
        pl.semaphore_signal(
            barrier, inc=1, device_id={"mp": other}, device_id_type=pl.DeviceIdType.MESH
        )
    for step in range(1, experts):
        other = lax.rem(along + step, experts)
        pl.semaphore_signal(
            barrier, inc=1, device_id={"dp": other}, device_id_type=pl.DeviceIdType.MESH
        )
    pl.semaphore_wait(barrier, groups + experts - 2)

    def remote(source, target, sent, landed, device):
        return pltpu.make_async_remote_copy(
            src_ref=source,
            dst_ref=target,
            send_sem=sent,
            recv_sem=landed,
            device_id={"mp": device},
            device_id_type=pl.DeviceIdType.MESH,
        )

    def to_row(step, source):
        return remote(
            squares_ref,
            squares_row.at[source],
            row_send_sem.at[step],
            row_sem.at[source],
            lax.rem(me + step, groups),
        )

    def to_col(step, source):
        return pltpu.make_async_remote_copy(
            src_ref=squares_sum,
            dst_ref=squares_col.at[source],
            send_sem=col_send_sem.at[step],
            recv_sem=col_sem.at[source],
            device_id={"dp": lax.rem(along + step, experts)},
            device_id_type=pl.DeviceIdType.MESH,
        )

    for step in range(1, groups):
        to_row(step, me).start()
    squares_row[me] = squares_ref[...]
    for step in range(1, groups):
        to_row(step, lax.rem(me + step, groups)).wait_recv()
    squares = squares_row[0]
    for source in range(1, groups):
        squares = squares + squares_row[source]
    squares_sum[...] = squares
    squares_col[along] = squares
    for step in range(1, experts):
        to_col(step, along).start()
    for step in range(1, experts):
        to_col(step, lax.rem(along + step, experts)).wait_recv()
    squares = squares_col[0]
    for source in range(1, experts):
        squares = squares + squares_col[source]
    squares_out[...] = squares
    norm = jnp.sqrt(jnp.sum(squares, keepdims=True))
    clip = 1.0 / jnp.maximum(norm, 1.0)
    for index in range(count_dense):
        moment = 0.5 * dense_old_ref[index] + clip * dense_grad_ref[index]
        dense_ref[index] = moment.astype(jnp.bfloat16)
    for index in range(count_expert):
        moment = 0.5 * expert_old_ref[index] + clip * expert_grad_ref[index].astype(jnp.float32)
        expert_moment_out[index] = moment
        expert_ref[index] = moment.astype(jnp.bfloat16)
    for step in range(1, groups):
        to_row(step, me).wait_send()
    for step in range(1, experts):
        to_col(step, along).wait_send()

    def outward(index, source):
        dense = index >= count_expert
        place = index - count_expert if dense else index
        held_ref = held_dense if dense else held
        own_ref = dense_ref if dense else expert_ref
        return remote(
            own_ref.at[place],
            held_ref.at[source],
            send_sem.at[index],
            in_sem.at[source],
            2 * place + (1 if dense else 0),
        )

    def sideways(step, source, orth):
        return pltpu.make_async_remote_copy(
            src_ref=land_dense if orth else dense_ref,
            dst_ref=(all_dense if orth else all_moment).at[source],
            send_sem=(orth_send_sem if orth else moment_send_sem).at[step],
            recv_sem=(orth_sem if orth else moment_sem).at[source],
            device_id={"dp": lax.rem(along + step, experts)},
            device_id_type=pl.DeviceIdType.MESH,
        )

    total = count_expert + count_dense
    owners = [2 * e for e in range(count_expert)] + [2 * d + 1 for d in range(count_dense)]
    for index in range(total):

        @pl.when(me != owners[index])
        def _(index=index):
            outward(index, me).start()

    for step in range(1, experts):
        sideways(step, along, False).start()

    for step in range(1, groups):
        source = lax.rem(me + step, groups)

        @pl.when(is_expert)
        def _(source=source):
            outward(0, source).wait_recv()

        @pl.when(is_dense)
        def _(source=source):
            outward(count_expert, source).wait_recv()

    for index in range(total):

        @pl.when(me != owners[index])
        def _(index=index):
            outward(index, me).wait_send()

    def backward_expert(target):
        return remote(
            held.at[target],
            land_expert.at[own],
            back_send_sem.at[target],
            back_sem.at[own],
            target,
        )

    def backward_dense(target):
        return remote(
            held_dense.at[target],
            land_dense.at[own],
            back_send_sem.at[target],
            back_sem.at[count_expert + own],
            target,
        )

    def share_dense():
        for index in range(count_expert, total):

            @pl.when(me != owners[index])
            def _(index=index):
                landing = land_dense.at[index - count_expert]
                remote(
                    landing, landing, send_sem.at[index], back_sem.at[index], owners[index]
                ).wait_recv()

        for step in range(1, experts):
            sideways(step, along, True).start()

    def nothing():
        return None

    @pl.when(is_expert)
    def _():
        held[me] = expert_ref[own]
        for j in range(groups // per):
            matrix[:, D * j : D * j + D] = jnp.concatenate(
                [held[per * j + inner] for inner in range(per)], axis=1
            )

        def finish(j):
            for inner in range(per):
                target = per * j + inner
                held[target] = matrix[:, cols * target : cols * target + cols]

                @pl.when(me != target)
                def _(target=target):
                    backward_expert(target).start()

        newton_rounds(matrix, gram_ref, poly_ref, share_dense, finish)
        land_expert[own] = held[me]
        for target in range(groups):

            @pl.when(me != target)
            def _(target=target):
                backward_expert(target).wait_send()

    @pl.when(is_dense)
    def _():
        held_dense[me] = dense_ref[own]
        for source in range(groups):
            square[cols_dense * source : cols_dense * source + cols_dense, :] = held_dense[source]

        def finish(j):
            for target in range(groups):
                held_dense[target] = square[
                    cols_dense * target : cols_dense * target + cols_dense, :
                ]

                @pl.when(me != target)
                def _(target=target):
                    backward_dense(target).start()

        newton_rounds(square, gram_ref, poly_ref, nothing, finish)
        land_dense[own] = held_dense[me]
        share_dense()
        for target in range(groups):

            @pl.when(me != target)
            def _(target=target):
                backward_dense(target).wait_send()

    @pl.when(jnp.logical_not(is_expert | is_dense))
    def _():
        share_dense()

    for index in range(count_expert):

        @pl.when(me != owners[index])
        def _(index=index):
            landing = land_expert.at[index]
            remote(
                landing, landing, send_sem.at[index], back_sem.at[index], owners[index]
            ).wait_recv()

    all_dense[along] = land_dense[...]
    all_moment[along] = dense_ref[...]
    for step in range(1, experts):
        sideways(step, lax.rem(along + step, experts), True).wait_recv()
        sideways(step, lax.rem(along + step, experts), False).wait_recv()
        sideways(step, along, True).wait_send()
        sideways(step, along, False).wait_send()
    expert_out[...] = land_expert[...]
    dense_out[...] = all_dense[...]
    moment_out[...] = all_moment[...]


def newton(squares, expert_old, expert_grad, dense_old, dense_grad, groups, experts):
    cols, cols_dense = expert_old.shape[2], dense_old.shape[1]
    count_expert, count_dense = expert_old.shape[0], dense_old.shape[0]
    low = jnp.bfloat16
    vmem = pl.BlockSpec(memory_space=pltpu.VMEM)
    dma = pltpu.SemaphoreType.DMA
    return pl.pallas_call(
        partial(newton_kernel, groups, experts),
        in_specs=[vmem] * 5,
        out_specs=[vmem] * 5,
        out_shape=[
            jax.ShapeDtypeStruct(squares.shape, jnp.float32),
            jax.ShapeDtypeStruct(expert_old.shape, jnp.float32),
            jax.ShapeDtypeStruct(expert_old.shape, low),
            jax.ShapeDtypeStruct((experts,) + dense_old.shape, low),
            jax.ShapeDtypeStruct((experts,) + dense_old.shape, low),
        ],
        scratch_shapes=[
            pltpu.VMEM(expert_old.shape, low),
            pltpu.VMEM(dense_old.shape, low),
            pltpu.VMEM((groups,) + squares.shape, jnp.float32),
            pltpu.VMEM(squares.shape, jnp.float32),
            pltpu.VMEM((experts,) + squares.shape, jnp.float32),
            pltpu.VMEM((groups, D, cols), low),
            pltpu.VMEM((groups, cols_dense, D), low),
            pltpu.VMEM((D, groups * cols), low),
            pltpu.VMEM((D, D), low),
            pltpu.VMEM((D, D), jnp.float32),
            pltpu.VMEM((D, D), low),
            pltpu.VMEM(expert_old.shape, low),
            pltpu.VMEM(dense_old.shape, low),
            pltpu.VMEM((experts,) + dense_old.shape, low),
            pltpu.VMEM((experts,) + dense_old.shape, low),
            dma((count_expert + count_dense,)),
            dma((groups,)),
            dma((groups,)),
            dma((count_expert + count_dense,)),
            dma((experts,)),
            dma((experts,)),
            dma((experts,)),
            dma((experts,)),
            dma((groups,)),
            dma((groups,)),
            dma((experts,)),
            dma((experts,)),
        ],
        compiler_params=pltpu.CompilerParams(
            vmem_limit_bytes=VMEM_LIMIT, collective_id=1, has_side_effects=True
        ),
        cost_estimate=pl.CostEstimate(
            flops=NS_ITERS * (4 * D * D * FF + 2 * D * D * D),
            bytes_accessed=40 * D * FF,
            transcendentals=0,
        ),
    )(squares, expert_old, expert_grad, dense_old, dense_grad)


def gather_kernel(groups, x_ref, out_ref, land, send_sem, pass_sem, land_sem):
    me = lax.axis_index("mp")
    half, side = me // 2, me % 2
    halves = groups // 2
    sibling = me + 1 - 2 * side
    barrier = pltpu.get_barrier_semaphore()
    mesh_id = pl.DeviceIdType.MESH
    for step in range(1, halves):
        other = 2 * lax.rem(half + step, halves) + side
        pl.semaphore_signal(barrier, inc=1, device_id={"mp": other}, device_id_type=mesh_id)
    pl.semaphore_signal(barrier, inc=1, device_id={"mp": sibling}, device_id_type=mesh_id)
    pl.semaphore_wait(barrier, halves)

    def remote(source, index, sent, device):
        return pltpu.make_async_remote_copy(
            src_ref=source,
            dst_ref=land.at[index],
            send_sem=sent,
            recv_sem=land_sem.at[index],
            device_id={"mp": device},
            device_id_type=mesh_id,
        )

    def direct(step):
        return remote(x_ref, me, send_sem.at[step], 2 * lax.rem(half + step, halves) + side)

    def passed(step):
        index = 2 * lax.rem(half + step, halves) + side
        return remote(land.at[index], index, pass_sem.at[step], sibling)

    for step in range(1, halves):
        direct(step).start()
    to_sibling = remote(x_ref, me, send_sem.at[0], sibling)
    to_sibling.start()
    land[me] = x_ref[...]
    for step in range(1, halves):
        index = 2 * lax.rem(half + step, halves) + side
        remote(x_ref, index, send_sem.at[step], sibling).wait_recv()
        passed(step).start()
    for step in range(halves):
        index = 2 * lax.rem(half + step, halves) + 1 - side
        remote(x_ref, index, send_sem.at[step], sibling).wait_recv()
    to_sibling.wait_send()
    for step in range(1, halves):
        direct(step).wait_send()
        passed(step).wait_send()
    out_ref[...] = land[...]


def gathered_over(array, groups, collective):
    vmem = pl.BlockSpec(memory_space=pltpu.VMEM)
    dma = pltpu.SemaphoreType.DMA
    shape = (groups,) + array.shape
    return pl.pallas_call(
        partial(gather_kernel, groups),
        in_specs=[vmem],
        out_specs=vmem,
        out_shape=jax.ShapeDtypeStruct(shape, array.dtype),
        scratch_shapes=[
            pltpu.VMEM(shape, array.dtype),
            dma((groups // 2,)),
            dma((groups // 2,)),
            dma((groups,)),
        ],
        compiler_params=pltpu.CompilerParams(
            vmem_limit_bytes=(
                4 * math.prod(shape) * array.dtype.itemsize + 2 * 1024 * 1024
            ),
            collective_id=collective,
            has_side_effects=True,
        ),
        cost_estimate=pl.CostEstimate(flops=0, bytes_accessed=20000000, transcendentals=0),
    )(array)


def lookup_kernel(vocab, wanted_ref, table_ref, out_ref, acc_ref):
    block = pl.program_id(0)
    height = table_ref.shape[0]
    place = lax.broadcasted_iota(jnp.int32, (wanted_ref.shape[0], height), 1) + block * height
    pick = (wanted_ref[...] == place).astype(jnp.bfloat16)
    row = lax.broadcasted_iota(jnp.int32, table_ref.shape, 0) + block * height
    table = jnp.where(row < vocab, table_ref[...], 0.0).astype(jnp.bfloat16)
    part = dot_nn(pick, table)

    @pl.when(block == 0)
    def _():
        acc_ref[...] = part

    @pl.when(block > 0)
    def _():
        acc_ref[...] += part

    @pl.when(block == pl.num_programs(0) - 1)
    def _():
        out_ref[...] = acc_ref[...].astype(jnp.bfloat16)


def lookup(wanted, table):
    count = wanted.shape[0]
    vocab = table.shape[0]
    height = 1024
    whole = pl.BlockSpec((count, D), lambda j: (0, 0))
    return pl.pallas_call(
        partial(lookup_kernel, vocab),
        grid=(-(-vocab // height),),
        in_specs=[
            pl.BlockSpec((count, 1), lambda j: (0, 0)),
            pl.BlockSpec((height, D), lambda j: (j, 0)),
        ],
        out_specs=whole,
        out_shape=jax.ShapeDtypeStruct((count, D), jnp.bfloat16),
        scratch_shapes=[pltpu.VMEM((count, D), jnp.float32)],
        compiler_params=params(),
        cost_estimate=pl.CostEstimate(
            flops=2 * count * vocab * D, bytes_accessed=4 * vocab * D, transcendentals=0
        ),
    )(wanted[:, None], table)


def dense_kernel(
    groups,
    experts,
    enc_ref,
    dec_ref,
    small_ref,
    out_ref,
    small_out,
    land_pair,
    paired,
    land,
    summed,
    land_enc,
    land_dec,
    small_row,
    small_sum,
    small_col,
    pair_send_sem,
    pair_sem,
    send_sem,
    land_sem,
    enc_send_sem,
    enc_sem,
    dec_send_sem,
    dec_sem,
    row_send_sem,
    row_sem,
    col_send_sem,
    col_sem,
):
    across, along = lax.axis_index("mp"), lax.axis_index("dp")
    half, side = across // 2, across % 2
    halves = groups // 2
    count = enc_ref.shape[2]
    per_enc, per_dec = land_enc.shape[1], land_dec.shape[1]
    barrier = pltpu.get_barrier_semaphore()
    mesh_id = pl.DeviceIdType.MESH
    for step in range(1, groups):
        other = lax.rem(across + step, groups)
        pl.semaphore_signal(barrier, inc=1, device_id={"mp": other}, device_id_type=mesh_id)
    for step in range(1, experts):
        other = lax.rem(along + step, experts)
        pl.semaphore_signal(barrier, inc=1, device_id={"dp": other}, device_id_type=mesh_id)
    pl.semaphore_wait(barrier, groups + experts - 2)

    def remote(source, target, sent, landed, device):
        return pltpu.make_async_remote_copy(
            src_ref=source,
            dst_ref=target,
            send_sem=sent,
            recv_sem=landed,
            device_id=device,
            device_id_type=mesh_id,
        )

    def to_small_row(step, source):
        return remote(
            small_ref,
            small_row.at[source],
            row_send_sem.at[step],
            row_sem.at[source],
            {"mp": lax.rem(across + step, groups)},
        )

    def to_small_col(step, source):
        return remote(
            small_sum,
            small_col.at[source],
            col_send_sem.at[step],
            col_sem.at[source],
            {"dp": lax.rem(along + step, experts)},
        )

    def to_half(step, source):
        other = lax.rem(half + step, halves)
        return remote(
            paired.at[other],
            land.at[source],
            send_sem.at[step],
            land_sem.at[source],
            {"mp": 2 * other + side},
        )

    def to_col(step, source, dec):
        other = lax.rem(along + step, experts)
        per = per_dec if dec else per_enc
        return remote(
            (dec_ref if dec else summed).at[pl.ds(other * per, per)],
            (land_dec if dec else land_enc).at[source],
            (dec_send_sem if dec else enc_send_sem).at[step],
            (dec_sem if dec else enc_sem).at[source],
            {"dp": other},
        )

    to_pair = remote(
        enc_ref.at[1 - side],
        land_pair,
        pair_send_sem.at[0],
        pair_sem.at[0],
        {"mp": across + 1 - 2 * side},
    )
    to_pair.start()
    for step in range(1, groups):
        to_small_row(step, across).start()
    for step in range(1, experts):
        to_col(step, along, True).start()
    small_row[across] = small_ref[...]
    land_dec[along] = dec_ref[pl.ds(along * per_dec, per_dec)]
    to_pair.wait_recv()
    for step in range(1, halves + 1):
        other = lax.rem(half + step, halves)
        for index in range(count):
            paired[other, index] = (
                enc_ref[side, other, index].astype(jnp.float32)
                + land_pair[other, index].astype(jnp.float32)
            ).astype(jnp.bfloat16)
        if step < halves:
            to_half(step, half).start()
    land[half] = paired[half]
    for step in range(1, groups):
        to_small_row(step, lax.rem(across + step, groups)).wait_recv()
    total = small_row[0]
    for source in range(1, groups):
        total = total + small_row[source]
    small_sum[...] = total
    small_col[along] = total
    for step in range(1, experts):
        to_small_col(step, along).start()
    for step in range(1, halves):
        to_half(step, lax.rem(half + step, halves)).wait_recv()
    for index in range(count):
        total = land[0, index].astype(jnp.float32)
        for source in range(1, halves):
            total = total + land[source, index].astype(jnp.float32)
        summed[index] = total.astype(jnp.bfloat16)
    for index in range(count, summed.shape[0]):
        summed[index] = jnp.zeros(summed.shape[1:], jnp.bfloat16)
    for step in range(1, experts):
        to_col(step, along, False).start()
    land_enc[along] = summed[pl.ds(along * per_enc, per_enc)]
    to_pair.wait_send()
    for step in range(1, groups):
        to_small_row(step, across).wait_send()
    for step in range(1, halves):
        to_half(step, half).wait_send()
    for step in range(1, experts):
        source = lax.rem(along + step, experts)
        to_small_col(step, source).wait_recv()
        to_col(step, source, True).wait_recv()
        to_col(step, source, False).wait_recv()
        to_small_col(step, along).wait_send()
        to_col(step, along, True).wait_send()
        to_col(step, along, False).wait_send()
    total = small_col[0]
    for source in range(1, experts):
        total = total + small_col[source]
    small_out[...] = total
    for landed, per, first in ((land_enc, per_enc, 0), (land_dec, per_dec, per_enc)):
        for index in range(per):
            total = landed[0, index].astype(jnp.float32)
            for source in range(1, experts):
                total = total + landed[source, index].astype(jnp.float32)
            out_ref[first + index] = total


def dense_total(enc, dec, small, groups, experts):
    count, cols = enc.shape[2], enc.shape[3]
    per_enc, per_dec = -(-count // experts), -(-dec.shape[0] // experts)
    dec = jnp.pad(dec, ((0, per_dec * experts - dec.shape[0]), (0, 0), (0, 0)))
    vmem = pl.BlockSpec(memory_space=pltpu.VMEM)
    dma = pltpu.SemaphoreType.DMA
    low = jnp.bfloat16
    halves = groups // 2
    return pl.pallas_call(
        partial(dense_kernel, groups, experts),
        in_specs=[vmem, vmem, vmem],
        out_specs=[vmem, vmem],
        out_shape=[
            jax.ShapeDtypeStruct((per_enc + per_dec, cols, D), jnp.float32),
            jax.ShapeDtypeStruct(small.shape, jnp.float32),
        ],
        scratch_shapes=[
            pltpu.VMEM(enc.shape[1:], low),
            pltpu.VMEM(enc.shape[1:], low),
            pltpu.VMEM(enc.shape[1:], low),
            pltpu.VMEM((per_enc * experts, cols, D), low),
            pltpu.VMEM((experts, per_enc, cols, D), low),
            pltpu.VMEM((experts, per_dec, cols, D), low),
            pltpu.VMEM((groups,) + small.shape, jnp.float32),
            pltpu.VMEM(small.shape, jnp.float32),
            pltpu.VMEM((experts,) + small.shape, jnp.float32),
            dma((1,)),
            dma((1,)),
            dma((halves,)),
            dma((halves,)),
            dma((experts,)),
            dma((experts,)),
            dma((experts,)),
            dma((experts,)),
            dma((groups,)),
            dma((groups,)),
            dma((experts,)),
            dma((experts,)),
        ],
        compiler_params=pltpu.CompilerParams(
            vmem_limit_bytes=VMEM_LIMIT, collective_id=4, has_side_effects=True
        ),
        cost_estimate=pl.CostEstimate(
            flops=0, bytes_accessed=200000000, transcendentals=0
        ),
    )(enc, dec, small)


def piece_of(array, count, experts):
    along = lax.axis_index("dp")
    pieces = []
    for part in (array[:count], array[count:]):
        per = -(-part.shape[0] // experts)
        spare = per * experts - part.shape[0]
        part = jnp.pad(part, ((0, spare),) + ((0, 0),) * (part.ndim - 1))
        pieces.append(lax.dynamic_slice_in_dim(part, along * per, per, 0))
    return jnp.concatenate(pieces, axis=0)


def whole_of(pieces, count, rest):
    per = -(-count // pieces.shape[0])
    first = pieces[:, :per].reshape((-1,) + pieces.shape[2:])[:count]
    second = pieces[:, per:].reshape((-1,) + pieces.shape[2:])[:rest]
    return jnp.concatenate([first, second], axis=0)


def project(rows, stored):
    flat = stored.reshape(-1, D)
    return dot_nt(rows, flat)


def swap_owners(buffer):
    return lax.all_to_all(buffer, "dp", split_axis=0, concat_axis=0, tiled=True)


def dispatch(places, count):
    slot = lax.broadcasted_iota(jnp.int32, (count, places.shape[0]), 0)
    return (slot == places[None, :]).astype(jnp.bfloat16)


def route_places(routes, experts, cap):
    hot = (routes[:, None] == jnp.arange(experts, dtype=jnp.int32)[None, :]).astype(jnp.float32)
    rows = routes.shape[0]
    earlier = (
        lax.broadcasted_iota(jnp.int32, (rows, rows), 1)
        < lax.broadcasted_iota(jnp.int32, (rows, rows), 0)
    ).astype(jnp.bfloat16)
    ranks = dot_nn(earlier, hot.astype(jnp.bfloat16))
    slots = jnp.sum(hot * ranks, axis=1).astype(jnp.int32)
    return hot, routes * cap + slots


def moe_send(resid, gain, router, hot, places, cap):
    experts = router.shape[1]
    normed, inverse = normalize(resid, gain)
    normed_low = normed.astype(jnp.bfloat16)
    buffer = dot_nn(dispatch(places, experts * cap), normed_low).astype(jnp.bfloat16)
    arrived = swap_owners(buffer.reshape(experts, cap, D)).reshape(-1, D)
    probs = jax.nn.softmax(
        jnp.dot(normed_low.astype(jnp.float32), router, precision=highest), axis=-1
    )
    gate = jnp.sum(probs * hot, axis=1)
    return arrived, (normed_low, inverse, probs, gate)


def moe_expert(weights, cap, arrived):
    pre, result = expert_forward(arrived, weights)
    return pre, swap_owners(result.reshape(-1, cap, D)).reshape(-1, D)


def moe_receive(resid, places, arrived, pre, returned, sent):
    outputs = dot_tn(dispatch(places, returned.shape[0]), returned)
    return (resid + sent[3][:, None] * outputs, sent + (arrived, pre, outputs))


def moe_back_send(places, cap, kept, grad):
    normed_low, inverse, probs, gate, arrived, pre, outputs = kept
    experts = arrived.shape[0] // cap
    d_rows = (gate[:, None] * grad).astype(jnp.bfloat16)
    buffer = dot_nn(dispatch(places, experts * cap), d_rows).astype(jnp.bfloat16)
    return swap_owners(buffer.reshape(experts, cap, D)).reshape(-1, D)


def moe_back_expert(weights, cap, kept, d_arrived):
    normed_low, inverse, probs, gate, arrived, pre, outputs = kept
    experts = arrived.shape[0] // cap
    d_weights, d_back = expert_backward(arrived, d_arrived, pre, weights)
    return d_weights, swap_owners(d_back.reshape(experts, cap, D)).reshape(-1, D)


def moe_back_receive(resid, gain, router, hot, places, kept, grad, returned, aux_scale, frac):
    normed_low, inverse, probs, gate, arrived, pre, outputs = kept
    d_gate = jnp.sum(grad * outputs, axis=1)
    d_probs = hot * d_gate[:, None] + aux_scale * frac[None, :]
    d_logits = probs * (d_probs - jnp.sum(probs * d_probs, axis=-1, keepdims=True))
    d_router = jnp.dot(normed_low.astype(jnp.float32).T, d_logits, precision=highest)
    d_normed = dot_tn(dispatch(places, returned.shape[0]), returned) + jnp.dot(
        d_logits, router.T, precision=highest
    )
    d_resid, d_gain = normalize_back(resid, inverse, gain, d_normed)
    return (grad + d_resid, d_gain, d_router)


def ranks_of(ids, size):
    count = ids.shape[0]
    here, there = ids[:, None], ids[None, :]
    before = lax.broadcasted_iota(jnp.int32, (count, count), 1) < lax.broadcasted_iota(
        jnp.int32, (count, count), 0
    )
    again = jnp.max(((here == there) & before).astype(jnp.int32), axis=1)
    owner = ids // size
    lower = (there < here) & (there >= (owner * size)[:, None]) & (again[None, :] == 0)
    return owner, jnp.sum(lower.astype(jnp.int32), axis=1)


def slots_of(owner, rank, owners, width, turn):
    slot = owner * width + rank - turn * width
    slot = jnp.where((rank >= turn * width) & (rank < (turn + 1) * width), slot, -1)
    return lax.broadcasted_iota(jnp.int32, (owners * width, rank.shape[0]), 0) == slot[None, :]


def ids_in(hot, local, width):
    return jnp.max(jnp.where(hot, local[None, :], -1), axis=1).reshape(-1, width)


def exchange(array, axes):
    return lax.all_to_all(array, axes, split_axis=0, concat_axis=0, tiled=True)


def rows_into(landed, rows, count):
    place = landed[None, :] == lax.broadcasted_iota(jnp.int32, (count, landed.shape[0]), 0)
    return dot_nn(place.astype(jnp.bfloat16), rows)


def in_lanes(parts):
    flat = jnp.concatenate([part.reshape(-1) for part in parts])
    rows = -(-flat.shape[0] // (8 * LANES)) * 8
    return jnp.pad(flat, (0, rows * LANES - flat.shape[0])).reshape(rows, LANES)


def from_lanes(array, parts):
    flat = array.reshape(-1)
    taken, out = 0, []
    for part in parts:
        out.append(flat[taken : taken + part.size].reshape(part.shape))
        taken += part.size
    return out


def self_forward(resid, gain, weights, parts, causal):
    normed, inverse = normalize(resid, gain)
    normed = normed.astype(jnp.bfloat16)
    joined = project(normed, weights[0:3]).astype(jnp.bfloat16)
    mixed, logsum = attend((joined, 0), (joined, 1), (joined, 2), parts, causal)
    return (resid + project(mixed, weights[3]), (resid, inverse, normed, joined, mixed, logsum))


def self_backward(gain, weights, parts, causal, kept, grad):
    resid, inverse, normed, joined, mixed, logsum = kept
    grad_low = grad.astype(jnp.bfloat16)
    d_mixed = dot_nn(grad_low, weights[3]).astype(jnp.bfloat16)
    d_query, d_key, d_value, sums = attend_back(
        (joined, 0), (joined, 1), (joined, 2), parts, causal, logsum, d_mixed
    )
    d_normed = (
        dot_nn(d_query, weights[0]) + dot_nn(d_key, weights[1]) + dot_nn(d_value, weights[2])
    )
    d_weights = [
        dot_tn(d_query, normed),
        dot_tn(d_key, normed),
        dot_tn(d_value, normed),
        dot_tn(grad_low, mixed),
    ]
    d_resid, d_gain = normalize_back(resid, inverse, gain, d_normed)
    return (grad + d_resid, d_gain, d_weights, bias_sums(sums, parts[2], parts[3]))


def cross_forward(resid, gain, weights, memory):
    normed, inverse = normalize(resid, gain)
    normed = normed.astype(jnp.bfloat16)
    query = project(normed, weights[0]).astype(jnp.bfloat16)
    joined = project(memory, weights[1:3]).astype(jnp.bfloat16)
    mixed, logsum = attend((query, 0), (joined, 0), (joined, 1), None, False)
    kept = (resid, inverse, normed, query, joined, mixed, logsum)
    return (resid + project(mixed, weights[3]), kept)


def cross_backward(gain, weights, memory, kept, grad):
    resid, inverse, normed, query, joined, mixed, logsum = kept
    grad_low = grad.astype(jnp.bfloat16)
    d_mixed = dot_nn(grad_low, weights[3]).astype(jnp.bfloat16)
    d_query, d_key, d_value = attend_back(
        (query, 0), (joined, 0), (joined, 1), None, False, logsum, d_mixed
    )
    d_normed = dot_nn(d_query, weights[0])
    d_memory = dot_nn(d_key, weights[1]) + dot_nn(d_value, weights[2])
    d_weights = [
        dot_tn(d_query, normed),
        dot_tn(d_key, memory),
        dot_tn(d_value, memory),
        dot_tn(grad_low, mixed),
    ]
    d_resid, d_gain = normalize_back(resid, inverse, gain, d_normed)
    return (grad + d_resid, d_gain, d_weights, d_memory)


def route_share(routes, experts):
    flat_routes = routes.reshape(-1)
    hot = (flat_routes[None, :] == jnp.arange(experts, dtype=jnp.int32)[:, None]).astype(
        jnp.float32
    )
    return jnp.sum(hot, axis=1) / flat_routes.shape[0]


def adam(weight, first, second, grad, rate, decay):
    first = beta_one * first + (1 - beta_one) * grad
    second = beta_two * second + (1 - beta_two) * grad * grad
    update = first / (1 - beta_one**STEP) / (jnp.sqrt(second / (1 - beta_two**STEP)) + eps_adam)
    return (weight - rate * (update + decay * weight), first, second)


def share_columns(d_weights, groups):
    split = jnp.concatenate(
        [part.astype(jnp.bfloat16).reshape(groups, -1, D) for part in d_weights], axis=1
    )
    summed = lax.psum_scatter(split.reshape(-1, D), "mp", scatter_dimension=0, tiled=True)
    return summed.reshape(len(d_weights), -1, D)


def on_device(
    src_ids,
    targets,
    loss_pos,
    loss_mask,
    routes_src,
    routes_tgt,
    dense_w,
    dense_m,
    expert_w,
    expert_m,
    table_w,
    table_m,
    table_v,
    gains_w,
    gains_m,
    gains_v,
    router_w,
    router_m,
    router_v,
    bias_w,
    bias_m,
    bias_v,
):
    groups = lax.axis_size("mp")
    column = lax.axis_index("mp")
    experts = lax.axis_size("dp")
    src_len = src_ids.shape[1]
    tgt_len = targets.shape[1]
    npos = loss_pos.shape[1]
    vocab_dev = table_w.shape[0]
    own_seq = lax.axis_index("dp") * groups + column
    count_dense = dense_w.shape[0]
    low = jnp.bfloat16
    dense_local = dense_w.astype(low).reshape(count_dense, -1, D)
    enc_dense = lax.all_gather(dense_local[0:4], "mp", axis=1, tiled=True)
    expert_local = expert_w[:, :, 0].astype(low)
    devices = experts * groups
    piece_rows = table_m.shape[0]
    own_src_ids = lax.dynamic_slice_in_dim(src_ids, column, 1, 0).reshape(-1)
    own_targets = lax.dynamic_slice_in_dim(targets, column, 1, 0).reshape(-1)
    own_ids = jnp.concatenate([own_src_ids, jnp.zeros((1,), jnp.int32), own_targets[:-1]])
    shard, rank = ranks_of(own_ids, vocab_dev)
    owner, owner_rank = ranks_of(own_ids, piece_rows)
    local_ids = own_ids - shard * vocab_dev
    piece_ids = own_ids - owner * piece_rows
    owner = (owner % experts) * groups + owner // experts
    fetch_turns = jnp.max(rank) // FETCH + 1
    give_turns = jnp.max(owner_rank) // GIVE + 1
    give_hot = (jnp.arange(piece_rows // GIVE + 2, dtype=jnp.int32) == give_turns).astype(
        jnp.float32
    )

    def asked_of(turn):
        return ids_in(slots_of(shard, rank, groups, FETCH, turn), local_ids, FETCH)

    def fetched(wanted):
        rows = lookup(wanted.reshape(-1), table_w)
        return exchange(rows.reshape(groups, FETCH, D), "mp").reshape(-1, D)

    def placed(turn, rows):
        hot = slots_of(shard, rank, groups, FETCH, turn).astype(low)
        return dot_tn(hot, rows).astype(low)

    noted = jnp.full((groups, LANES), fetch_turns)
    asked = exchange(jnp.concatenate([asked_of(0), noted], axis=1), "mp")
    fetch_turns = jnp.max(asked[:, FETCH:])
    rows = fetched(asked[:, :FETCH])

    def fetch_more(state):
        turn, more = state
        return turn + 1, more + placed(turn, fetched(exchange(asked_of(turn), "mp")))

    nothing = jnp.zeros((own_ids.shape[0], D), low)
    more = lax.cond(
        fetch_turns > 1,
        lambda: lax.while_loop(
            lambda state: state[0] < fetch_turns, fetch_more, (jnp.int32(1), nothing)
        )[1],
        lambda: nothing,
    )
    rows, more, enc_dense = lax.optimization_barrier((rows, more, enc_dense))
    embedded = (placed(0, rows) + more).astype(jnp.float32)
    enc_expert = lax.all_gather(expert_local[0], "mp", axis=0, tiled=False)
    own_src = lax.dynamic_slice_in_dim(routes_src, own_seq, 1, 0).reshape(-1)
    own_tgt = lax.dynamic_slice_in_dim(routes_tgt, own_seq, 1, 0).reshape(-1)
    cap_src = (5 * src_len + 4 * experts - 1) // (4 * experts)
    cap_tgt = (5 * tgt_len + 4 * experts - 1) // (4 * experts)
    total_src = routes_src.shape[0] * routes_src.shape[1]
    total_tgt = routes_tgt.shape[0] * routes_tgt.shape[1]
    frac_src = route_share(routes_src, experts)
    frac_tgt = route_share(routes_tgt, experts)
    hot_src, places_src = route_places(own_src, experts, cap_src)
    hot_tgt, places_tgt = route_places(own_tgt, experts, cap_tgt)
    enc_parts = bias_parts(bias_w[0], False)
    dec_parts = bias_parts(bias_w[1], True)
    enc_mid, enc_kept = self_forward(embedded[:src_len], gains_w[0], enc_dense, enc_parts, False)
    dec_local, late_table, enc_mid = lax.optimization_barrier((dense_local[4:12], table_w, enc_mid))
    arrived, enc_sent = moe_send(enc_mid, gains_w[1], router_w[0], hot_src, places_src, cap_src)
    all_dense = lax.all_gather(dec_local, "mp", axis=1, tiled=True)
    dec_dense, cross_dense = all_dense[0:4], all_dense[4:8]
    padded = -(-piece_rows // 16) * 16
    table_low = jnp.pad(
        late_table.astype(low).reshape(experts, piece_rows, D),
        ((0, 0), (0, padded - piece_rows), (0, 0)),
    ).reshape(-1, D)
    arrived, enc_expert, dec_expert_local, table_low = lax.optimization_barrier(
        (arrived, enc_expert, expert_local[1], table_low)
    )
    dec_expert = lax.all_gather(dec_expert_local, "mp", axis=0, tiled=False)
    pre, returned = moe_expert(enc_expert, cap_src, arrived)
    dec_mid, dec_kept = self_forward(embedded[src_len:], gains_w[3], dec_dense, dec_parts, True)
    returned, dec_mid = lax.optimization_barrier((returned, dec_mid))
    enc_out, enc_moe = moe_receive(enc_mid, places_src, arrived, pre, returned, enc_sent)
    memory_float, memory_inv = normalize(enc_out, gains_w[2])
    memory = memory_float.astype(low)
    dec_crossed, cross_kept = cross_forward(dec_mid, gains_w[4], cross_dense, memory)
    arrived, dec_sent = moe_send(
        dec_crossed, gains_w[5], router_w[1], hot_tgt, places_tgt, cap_tgt
    )
    pre, returned = moe_expert(dec_expert, cap_tgt, arrived)
    dec_result, dec_moe = moe_receive(dec_crossed, places_tgt, arrived, pre, returned, dec_sent)
    final_float, final_inv = normalize(dec_result, gains_w[6])
    final_low = final_float.astype(low)
    head_scale = D ** (-0.5)
    own_pos = lax.dynamic_slice_in_dim(loss_pos, column, 1, 0).reshape(-1)
    pick = (
        own_pos[:, None] == lax.broadcasted_iota(jnp.int32, (npos, tgt_len), 1)
    ).astype(low)
    chosen = dot_nn(pick, final_low).astype(low)
    gathered = gathered_over(chosen, groups, 5).reshape(-1, D)
    place = jnp.arange(experts * padded, dtype=jnp.int32)
    logits = jnp.where(
        (place % padded < piece_rows)[None, :], dot_nt(gathered, table_low) * head_scale, -1e30
    )
    at_pos = loss_pos[:, :, None] == lax.broadcasted_iota(jnp.int32, (1, 1, tgt_len), 2)
    wanted = jnp.sum(jnp.where(at_pos, targets[:, None, :], 0), axis=2).reshape(-1)
    wanted = wanted - column * vocab_dev
    here = (wanted >= 0) & (wanted < vocab_dev)
    wanted = jnp.where(here, wanted + wanted // piece_rows * (padded - piece_rows), -1)
    hits = place[None, :] == wanted[:, None]
    top = jnp.max(logits, axis=1)
    stats = gathered_over(
        jnp.stack(
            [
                top,
                jnp.sum(jnp.exp(logits - top[:, None]), axis=1),
                jnp.sum(jnp.where(hits, logits, 0.0), axis=1),
            ]
            + [jnp.zeros_like(top)] * 5
        ),
        groups,
        6,
    )
    all_top = jnp.max(stats[:, 0], axis=0)
    expsum = jnp.sum(stats[:, 1] * jnp.exp(stats[:, 0] - all_top[None, :]), axis=0)
    picked = jnp.sum(stats[:, 2], axis=0)
    logsum = all_top + jnp.log(expsum)
    mask_rows = loss_mask.reshape(-1).astype(jnp.float32)
    own_loss = jnp.sum(
        lax.dynamic_slice_in_dim(mask_rows * (logsum - picked), column * npos, npos)
    )
    own_count = jnp.sum(lax.dynamic_slice_in_dim(mask_rows, column * npos, npos))
    d_logits = (
        mask_rows[:, None] * (jnp.exp(logits - logsum[:, None]) - hits.astype(jnp.float32))
    ).astype(low)
    d_gathered = (dot_nn(d_logits, table_low) * head_scale).astype(low)
    d_gathered, d_logits = lax.optimization_barrier((d_gathered, d_logits))
    d_shares = exchange(d_gathered.reshape(groups, npos, D), "mp")
    table_grad = (dot_tn(d_logits, gathered) * head_scale).astype(low)
    d_shares, table_grad = lax.optimization_barrier((d_shares, table_grad))
    table_share = lax.psum_scatter(table_grad, "dp", scatter_dimension=0, tiled=True)
    d_chosen = jnp.sum(d_shares.astype(jnp.float32), axis=0).astype(low)
    d_final = dot_tn(pick, d_chosen)
    d_dec, gain_final = normalize_back(dec_result, final_inv, gains_w[6], d_final)
    d_arrived = moe_back_send(places_tgt, cap_tgt, dec_moe, d_dec)
    dec_dw, returned = moe_back_expert(dec_expert, cap_tgt, dec_moe, d_arrived)
    dec_share = lax.psum_scatter(dec_dw, "mp", scatter_dimension=0, tiled=False)
    d_dec, gain_dec_moe, dec_router = moe_back_receive(
        dec_crossed,
        gains_w[5],
        router_w[1],
        hot_tgt,
        places_tgt,
        dec_moe,
        d_dec,
        returned,
        aux_weight * experts / total_tgt,
        frac_tgt,
    )
    d_dec, gain_cross, cross_dw, d_memory = cross_backward(
        gains_w[4], cross_dense, memory, cross_kept, d_dec
    )
    d_enc, gain_memory = normalize_back(enc_out, memory_inv, gains_w[2], d_memory)
    d_arrived = moe_back_send(places_src, cap_src, enc_moe, d_enc)
    d_dec, gain_self, self_dw, dec_bias = self_backward(
        gains_w[3], dec_dense, dec_parts, True, dec_kept, d_dec
    )
    d_arrived, d_dec, table_share = lax.optimization_barrier((d_arrived, d_dec, table_share))
    enc_dw, returned = moe_back_expert(enc_expert, cap_src, enc_moe, d_arrived)
    dec_cols = share_columns(self_dw + cross_dw, groups)
    enc_share = lax.psum_scatter(enc_dw, "mp", scatter_dimension=0, tiled=False)
    d_enc, gain_enc_moe, enc_router = moe_back_receive(
        enc_mid,
        gains_w[1],
        router_w[0],
        hot_src,
        places_src,
        enc_moe,
        d_enc,
        returned,
        aux_weight * experts / total_src,
        frac_src,
    )
    d_enc, dec_share = lax.optimization_barrier((d_enc, dec_share))
    d_enc, gain_enc, enc_self_dw, enc_bias = self_backward(
        gains_w[0], enc_dense, enc_parts, False, enc_kept, d_enc
    )
    enc_parts = jnp.stack(
        [
            jnp.swapaxes(part.astype(low).reshape(groups // 2, 2, -1, D), 0, 1)
            for part in enc_self_dw
        ],
        axis=2,
    )
    d_embedded = jnp.concatenate([d_enc, d_dec], axis=0).astype(low)

    def given_ids(turn):
        hot = slots_of(owner, owner_rank, devices, GIVE, turn)
        return exchange(ids_in(hot, piece_ids, GIVE), ("dp", "mp")).reshape(-1)

    def given_rows(turn):
        hot = slots_of(owner, owner_rank, devices, GIVE, turn).astype(low)
        rows = dot_nn(hot, d_embedded).astype(low).reshape(devices, GIVE, D)
        return exchange(rows, ("dp", "mp")).reshape(-1, D)

    landed, d_embedded = lax.optimization_barrier((given_ids(0), d_embedded))
    arrived = given_rows(0)
    gains_grad = jnp.stack(
        [gain_enc, gain_enc_moe, gain_memory, gain_self, gain_cross, gain_dec_moe, gain_final]
    )
    router_grad = jnp.stack([enc_router, dec_router])
    bias_grad = jnp.stack([enc_bias, dec_bias])
    load_src = jnp.sum(enc_moe[2], axis=0)
    load_tgt = jnp.sum(dec_moe[2], axis=0)
    small = [
        gains_grad,
        router_grad,
        bias_grad,
        load_src,
        load_tgt,
        own_loss,
        own_count,
        give_hot,
    ]
    dense_piece, summed = dense_total(enc_parts, dec_cols, in_lanes(small), groups, experts)
    arrived, summed, dense_piece = lax.optimization_barrier((arrived, summed, dense_piece))
    table_piece = rows_into(landed, arrived, piece_rows)
    gains_grad, router_grad, bias_grad, load_src, load_tgt, loss_sum, count, give_hot = from_lanes(
        summed, small
    )
    give_turns = jnp.max(
        jnp.where(give_hot > 0.0, jnp.arange(give_hot.shape[0], dtype=jnp.int32), 0)
    )

    def give_more(state):
        turn, total = state
        return turn + 1, total + rows_into(given_ids(turn), given_rows(turn), piece_rows)

    turns, table_piece = lax.while_loop(
        lambda state: state[0] < give_turns, give_more, (jnp.int32(1), table_piece)
    )

    table_piece = table_piece + table_share[:piece_rows].astype(jnp.float32)
    expert_share = jnp.stack([enc_share, dec_share])
    own_squares = sum((jnp.sum(part * part) for part in (gains_grad, router_grad, bias_grad)))
    squares = jnp.full((8, LANES), own_squares / (8 * LANES * devices))
    for part in (dense_piece, expert_share, table_piece):
        lanes = jnp.sum(jnp.square(part.astype(jnp.float32)).reshape(-1, part.shape[-1]), axis=0)
        width = math.gcd(lanes.shape[0], LANES)
        lanes = jnp.pad(jnp.sum(lanes.reshape(-1, width), axis=0), (0, LANES - width))
        squares = squares + lanes[None, :] * 0.125
    cols = expert_w.shape[4]
    old_piece = piece_of(dense_m, 4, experts).reshape(dense_piece.shape)
    squares, expert_moment, expert_orth, dense_orth, dense_moment = newton(
        squares,
        expert_m.reshape(-1, D, cols),
        expert_share.reshape(-1, D, cols),
        old_piece,
        dense_piece,
        groups,
        experts,
    )
    expert_moment = expert_moment.reshape(expert_w.shape)
    squares = jnp.sum(squares)
    grad_norm = jnp.sqrt(squares)
    clip = 1.0 / jnp.maximum(grad_norm, 1.0)
    aux = (
        aux_weight
        * experts
        * (jnp.sum(frac_src * load_src) / total_src + jnp.sum(frac_tgt * load_tgt) / total_tgt)
    )
    loss = jnp.stack([loss_sum + aux, count])

    def as_stored(pieces):
        return whole_of(pieces, 4, count_dense - 4).reshape(count_dense, -1).astype(jnp.float32)

    dense_moment, dense_orth = as_stored(dense_moment), as_stored(dense_orth)
    keep_rate = 1 - rate_matrix * decay_matrix
    dense_new = dense_w * keep_rate - rate_matrix * 0.2 * math.sqrt(D) * dense_orth
    expert_new = expert_w * keep_rate - rate_matrix * 0.2 * math.sqrt(
        max(D, FF)
    ) * expert_orth.astype(jnp.float32).reshape(expert_w.shape)
    table_clipped = clip * table_piece
    table_new, table_first, table_second = adam(
        lax.dynamic_slice_in_dim(table_w, lax.axis_index("dp") * piece_rows, piece_rows, 0),
        table_m,
        table_v,
        table_clipped,
        1.5,
        0.01,
    )

    def part_of(array, like):
        size = like.shape[1]
        return lax.dynamic_slice_in_dim(array, column * size, size, 1)

    gains_new, gains_first, gains_second = adam(
        part_of(gains_w, gains_m), gains_m, gains_v, clip * part_of(gains_grad, gains_m), 0.5, 0.0
    )
    router_new, router_first, router_second = adam(
        part_of(router_w, router_m),
        router_m,
        router_v,
        clip * part_of(router_grad, router_m),
        0.02,
        0.01,
    )
    bias_new, bias_first, bias_second = adam(
        part_of(bias_w, bias_m), bias_m, bias_v, clip * part_of(bias_grad, bias_m), 0.5, 0.0
    )
    return (
        loss,
        grad_norm,
        dense_new,
        dense_moment,
        dense_new.astype(low),
        expert_new,
        expert_moment,
        expert_new.astype(low),
        table_new,
        table_clipped,
        table_second,
        gains_new,
        gains_first,
        gains_second,
        router_new,
        router_first,
        router_second,
        bias_new,
        bias_first,
        bias_second,
    )


def solution(mesh):
    in_specs = (
        P("dp", None),
        P("dp", None),
        P("dp", None),
        P("dp", None),
        P(),
        P(),
        P(None, "mp"),
        P(None, "mp"),
        P(None, None, "dp", None, "mp"),
        P(None, None, "dp", None, "mp"),
        P("mp", None),
        P(("mp", "dp"), None),
        P(("mp", "dp"), None),
        P(),
        P(None, "mp"),
        P(None, "mp"),
        P(),
        P(None, "mp", None),
        P(None, "mp", None),
        P(),
        P(None, "mp", None),
        P(None, "mp", None),
    )
    out_specs = (
        P(),
        P(),
        P(None, "mp"),
        P(None, "mp"),
        P(None, "mp"),
        P(None, None, "dp", None, "mp"),
        P(None, None, "dp", None, "mp"),
        P(None, None, "dp", None, "mp"),
        P(("mp", "dp"), None),
        P(("mp", "dp"), None),
        P(("mp", "dp"), None),
        P(None, "mp"),
        P(None, "mp"),
        P(None, "mp"),
        P(None, "mp", None),
        P(None, "mp", None),
        P(None, "mp", None),
        P(None, "mp", None),
        P(None, "mp", None),
        P(None, "mp", None),
    )
    return jax.shard_map(
        on_device, mesh=mesh, in_specs=in_specs, out_specs=out_specs, check_vma=False
    )
```
